32 devices in a mesh: expert: 4 (over y, x), wide: 8 (over z, core).
Axes of the slice: x: 2, y: 2, z: 4, core: 2. Of those that a mesh axis runs over, the one named last changes fastest.
Arguments:
- tokens: bfloat16 [4096, 2048], P(('expert', 'wide')), may hold values from -6 to 6
- out_grad: bfloat16 [4096, 2048], P(('expert', 'wide')), may hold values from -6 to 6
- routes: int32 [4096, 2], P(('expert', 'wide')), may hold values from 0 to 3, all different within a row; in each aligned block of 128 rows (0 to 127, 128 to 255, ...) at most 128 rows name the same one
- gate_prob: float32 [4096, 2], P(('expert', 'wide')), may hold values from 0.1 to 1
- w_gate: bfloat16 [4, 2048, 768], P('expert', 'wide'), may hold values from -0.125 to 0.125
- w_up: bfloat16 [4, 2048, 768], P('expert', 'wide'), may hold values from -0.125 to 0.125
- w_down: bfloat16 [4, 2048, 768], P('expert', 'wide'), may hold values from -0.21875 to 0.21875
Outputs:
- grad_input: bfloat16 [4096, 2048], P(('expert', 'wide'))
- grad_gate: float32 [4, 2048, 768], P('expert', 'wide')
- grad_up: float32 [4, 2048, 768], P('expert', 'wide')
- grad_down: float32 [4, 2048, 768], P('expert', 'wide')
The draws below stay inside these ranges and needn't reach their ends.
Inputs may be any that keep to these rules, and one draw needn't show every extreme that they name: `routes`: each row names 2 different experts; the 128 rows of one device name one expert at most 128 times, and in every draw some device names some expert exactly 128 times.
All inputs are finite; a program needn't handle non-finite values.
Results may differ from the reference program's by a relative error of at most 0.017.
Values may be sent and summed in bfloat16 or wider, within the bound.
No kernel may reach another device: no remote copies, remote signals or barrier semaphores. Data moves between devices by JAX's collectives and lax.ppermute only.
A program may use at most 128 MiB of HBM per device.

```python
import math
import jax
import jax.numpy as jnp
import numpy as np
from jax import lax

D = 2048
F = 768
TOK_DEV = 128
TOP = 2
EXPERTS = 4
CAP = 128
TOKENS = 4096
N_EXPERT = 4
N_WIDE = 8


def shard_levels(rng, shape, shards, least, high):
    def one(dim, blocks):
        draws = jax.random.uniform(jax.random.fold_in(jax.random.fold_in(rng, 6), dim), (blocks,), jnp.float32, least / len(shards), high / len(shards))
        return jnp.repeat(jnp.exp(draws), shape[dim] // blocks).reshape((-1,) + (1,) * (len(shape) - dim - 1))

    loudness = one(*shards[0])
    for cut in shards[1:]:
        loudness = loudness * one(*cut)
    return loudness


def deal_out(own_key, own, number, rows, number_of, top, most, lean):
    order = jax.random.permutation(own_key, number_of)
    packed, ordinary = portions_of(number_of, rows * top, most, lean, True), portions_of(number_of, rows * top, most, lean, False)
    places = jnp.arange(number_of)

    def named(lengths, rotation):
        used = int((lengths > 0).sum())
        fixed = max(1, used // 4)
        shifted = fixed + (places - fixed + rotation * (used - fixed)) % max(1, number_of - fixed)
        return jnp.zeros((number_of,), jnp.int32).at[order[jnp.where(places < fixed, places, shifted)]].set(jnp.asarray(lengths, jnp.int32))

    lengths = jnp.where(number % 4 == 0, named(packed, number // 4), named(ordinary, number - number // 4 - 1))
    mixed = jax.random.permutation(jax.random.fold_in(own, 3), number_of)
    source_of, receiver = mixed[0:number_of // 2 * 2:2], mixed[1:number_of // 2 * 2:2]
    margin = jnp.minimum(lengths[source_of] - 1, most - lengths[receiver]) // 2
    margin = jnp.where((source_of == order[0]) | (receiver == order[0]) | (lengths[receiver] == 0), 0, jnp.maximum(margin, 0))
    shifted = jax.random.randint(jax.random.fold_in(own, 4), (number_of // 2,), 0, 1 << 20) % (margin + 1)
    lengths = lengths.at[source_of].add(-shifted).at[receiver].add(shifted)
    items = jnp.searchsorted(jnp.cumsum(lengths), jnp.arange(rows * top), side="right").astype(jnp.int32)
    listing = items.reshape(top, rows).T
    listing = listing[jax.random.permutation(jax.random.fold_in(own, 1), rows)]
    rotation = jax.random.randint(jax.random.fold_in(own, 2), (rows, 1), 0, top)
    return jnp.take_along_axis(listing, (jnp.arange(top)[None, :] + rotation) % top, axis=1)


def portions_of(count, total, limit, skew, full):
    portions = [(1 << 20) // math.isqrt(standing ** skew) + 1 for standing in range(1, count + 1)]
    largest = limit if full else min(limit, max(-(-total // count), total * portions[0] // sum(portions)))
    least = 1 if total - largest >= count - 1 else 0
    counts, surplus = [largest] + [least] * (count - 1), total - largest - least * (count - 1)
    while surplus > 0:
        candidates = [i for i in range(1, count) if counts[i] < largest] or [i for i in range(1, count) if counts[i] < limit]
        mass, budget = sum([portions[i] for i in candidates]), surplus
        for i in candidates:
            more = min(limit - counts[i], max(1, budget * portions[i] // mass), surplus)
            counts[i] = counts[i] + more
            surplus = surplus - more
    return np.array(counts)


def scatter_about(rng, shape, deviation, most, shards=(), kind=jnp.bfloat16):
    level = shard_levels(rng, shape, shards, -0.22, 0.18) if shards else 1.0
    drawn = jax.random.normal(rng, shape, jnp.float32) * deviation * level
    return jnp.minimum(jnp.maximum(drawn, -most), most).astype(kind)


def setup_inputs(seed: int = 0) -> dict:
    streams_of = jax.random.split(jax.random.key(seed), 8)
    tokens = scatter_about(streams_of[0], (TOKENS, D), 1.0, 6.0, ((0, 32),))
    out_grad = scatter_about(streams_of[1], (TOKENS, D), 1.0, 6.0, ((0, 32),))
    routes_keys = jax.random.split(jax.random.fold_in(streams_of[2], 1), TOKENS // TOK_DEV)
    routes_turns = jax.random.permutation(jax.random.fold_in(streams_of[2], 3), TOKENS // TOK_DEV)
    routes = jax.vmap(lambda own, number: deal_out(jax.random.fold_in(streams_of[2], 2), own, number, TOK_DEV, EXPERTS, TOP, CAP, 2))(routes_keys, routes_turns).reshape((TOKENS, TOP))
    gate_prob = jnp.clip(0.1 + 0.9 * jax.random.uniform(streams_of[3], (TOKENS, TOP), jnp.float32) ** shard_levels(streams_of[3], (TOKENS, TOP), ((0, 32),), -0.2, 0.2), 0.1, 1.0)
    w_gate = scatter_about(streams_of[4], (EXPERTS, D, F), D ** -0.5, 0.125, ((0, 4), (1, 8)))
    w_up = scatter_about(streams_of[5], (EXPERTS, D, F), D ** -0.5, 0.125, ((0, 4), (1, 8)))
    w_down = scatter_about(streams_of[6], (EXPERTS, D, F), F ** -0.5, 0.21875, ((0, 4), (1, 8)))
    return dict(tokens=tokens, out_grad=out_grad, routes=routes, gate_prob=gate_prob, w_gate=w_gate, w_up=w_up, w_down=w_down)


def swish_backward(gate_pre, up_pre, hidden_grad):
    squash = jax.nn.sigmoid(gate_pre)
    active = gate_pre * squash
    hidden = (active * up_pre).astype(jnp.bfloat16)
    gate_act = (hidden_grad * up_pre * squash * (1.0 + gate_pre * (1.0 - squash))).astype(jnp.bfloat16)
    up_act = (hidden_grad * active).astype(jnp.bfloat16)
    return hidden, gate_act, up_act


def grouped_sum(left, right):
    left_f = left.astype(jnp.float32).reshape(N_EXPERT, N_WIDE, CAP, left.shape[1])
    right_f = right.astype(jnp.float32).reshape(N_EXPERT, N_WIDE, CAP, right.shape[1])
    partial_sums = jnp.einsum("ewcd,ewcf->wdf", left_f, right_f, precision=lax.Precision.HIGHEST)
    rounded = lax.optimization_barrier(partial_sums.astype(jnp.bfloat16))
    return jnp.sum(rounded.astype(jnp.float32), axis=0)


def reference(tokens, out_grad, routes, gate_prob, w_gate, w_up, w_down):
    device_count = TOKENS // TOK_DEV
    route_count = TOK_DEV * TOP
    block_routes = routes.reshape(device_count, route_count)
    one_hot = (block_routes[:, :, None] == jnp.arange(EXPERTS, dtype=jnp.int32)[None, None, :]).astype(jnp.int32)
    before = jnp.cumsum(one_hot, axis=1) - one_hot
    slot_index = jnp.sum(before * one_hot, axis=2)
    device_ids = jnp.arange(device_count, dtype=jnp.int32)[:, None]
    row_index = (device_ids * CAP + slot_index).reshape(-1)
    token_ids = (device_ids * TOK_DEV + jnp.arange(route_count, dtype=jnp.int32)[None, :] // TOP).reshape(-1)
    expert_ids = block_routes.reshape(-1)
    gate_flat = gate_prob.reshape(-1)
    row_total = device_count * CAP

    def one_expert(carry, expert):
        target = jnp.where(expert_ids == expert, row_index, row_total).astype(jnp.int32)
        slot_token = jnp.zeros((row_total,), jnp.int32).at[target].set(token_ids, mode="drop")
        slot_gate = jnp.zeros((row_total,), jnp.float32).at[target].set(gate_flat, mode="drop")
        live_rows = jnp.zeros((row_total,), jnp.float32).at[target].set(1.0, mode="drop")
        xin = jnp.where(live_rows[:, None] > 0, tokens[slot_token], jnp.zeros((), jnp.bfloat16))
        scaled = (out_grad[slot_token].astype(jnp.float32) * slot_gate[:, None]).astype(jnp.bfloat16)
        gate_w = w_gate[expert]
        up_w = w_up[expert]
        down_w = w_down[expert]
        gate_pre = jnp.dot(xin, gate_w, preferred_element_type=jnp.float32)
        up_pre = jnp.dot(xin, up_w, preferred_element_type=jnp.float32)
        hidden_grad = jnp.dot(scaled, down_w, preferred_element_type=jnp.float32)
        hidden, gate_act, up_act = swish_backward(gate_pre, up_pre, hidden_grad)
        route_grad = (jnp.dot(gate_act, gate_w.T, preferred_element_type=jnp.float32)
                      + jnp.dot(up_act, up_w.T, preferred_element_type=jnp.float32)).astype(jnp.bfloat16)
        added = jnp.where(live_rows[:, None] > 0, route_grad.astype(jnp.float32), 0.0)
        carry = carry.at[slot_token].add(added)
        grads = (grouped_sum(xin, gate_act), grouped_sum(xin, up_act), grouped_sum(scaled, hidden))
        return carry, grads

    start = jnp.zeros((TOKENS, D), jnp.float32)
    total, grads = lax.scan(one_expert, start, jnp.arange(EXPERTS, dtype=jnp.int32))
    return total.astype(jnp.bfloat16), grads[0], grads[1], grads[2]
```

```python
import jax
import jax.numpy as jnp
from jax import lax
from jax.sharding import PartitionSpec as P

LANES = 128
F32 = jnp.float32
BF16 = jnp.bfloat16


def swish_backward(gate_pre, up_pre, hidden_grad):
    squash = jax.nn.sigmoid(gate_pre)
    active = gate_pre * squash
    hidden = (active * up_pre).astype(BF16)
    gate_act = (hidden_grad * up_pre * squash * (1.0 + gate_pre * (1.0 - squash))).astype(BF16)
    up_act = (hidden_grad * active).astype(BF16)
    return (hidden, gate_act, up_act)


def dot(a, b):
    return jnp.dot(a, b, preferred_element_type=F32)


def dot_tn(a, b):
    return lax.dot_general(a, b, (((0,), (0,)), ((), ())), preferred_element_type=F32)


def dot_nt(a, b):
    return lax.dot_general(a, b, (((1,), (1,)), ((), ())), preferred_element_type=F32)


def add(a, b):
    return (a.astype(F32) + b.astype(F32)).astype(BF16)


def slot_plan(tokens, out_grad, routes, gate_prob, w_gate, w_up, w_down):
    experts = lax.axis_size("expert")
    tok_count, top_count = routes.shape
    capacity = min(tok_count, 2 * tok_count * top_count // experts)
    slot_count = experts * capacity
    model_width = tokens.shape[1]
    hidden_units = w_gate.shape[2]
    flat_routes = routes.reshape(-1)
    order = jnp.arange(tok_count * top_count, dtype=jnp.int32)
    same = flat_routes[:, None] == flat_routes[None, :]
    before = jnp.sum((same & (order[None, :] < order[:, None])).astype(jnp.int32), axis=1)
    positions = flat_routes * capacity + before
    chosen = (positions[None, :] == jnp.arange(slot_count, dtype=jnp.int32)[:, None]).reshape(
        slot_count, tok_count, top_count
    )
    picker = jnp.sum(chosen.astype(F32), axis=2)
    slot_gate = jnp.sum(jnp.where(chosen, gate_prob[None, :, :], 0.0), axis=(1, 2))
    picker_half = picker.astype(BF16)
    sent_rows = dot(picker_half, tokens).astype(BF16)
    sent_grad = (dot(picker_half, out_grad) * slot_gate[:, None]).astype(BF16)

    def exchange(rows):
        return lax.all_to_all(
            rows.reshape(experts, capacity, model_width),
            "expert",
            split_axis=0,
            concat_axis=0,
            tiled=True,
        ).reshape(slot_count, model_width)

    rows_in = exchange(sent_rows)
    grad_in = exchange(sent_grad)
    full_gate, full_up, full_down = (
        lax.all_gather(w, "wide", axis=1, tiled=True)[0] for w in (w_gate, w_up, w_down)
    )
    hidden, gate_act, up_act = swish_backward(
        dot(rows_in, full_gate), dot(rows_in, full_up), dot(grad_in, full_down)
    )
    merged = jnp.concatenate((gate_act, up_act), axis=1)
    input_grad = dot_nt(merged, jnp.concatenate((full_gate, full_up), axis=1)).astype(BF16)
    parts = jnp.concatenate((dot_tn(rows_in, merged), dot_tn(grad_in, hidden)), axis=1)
    summed = lax.psum_scatter(
        parts.astype(BF16), "wide", scatter_dimension=0, tiled=True
    ).astype(F32)
    grads = tuple(
        summed[:, i * hidden_units : (i + 1) * hidden_units][None] for i in range(3)
    )
    grad_input = dot_tn(picker_half, exchange(input_grad)).astype(BF16)
    return (grad_input,) + grads


def dense_plan(tokens, out_grad, routes, gate_prob, w_gate, w_up, w_down):
    experts = lax.axis_size("expert")
    wide = lax.axis_size("wide")
    line = wide // 2
    rows, width = tokens.shape
    feats = w_gate.shape[1]
    half = w_gate.shape[2] // 2
    step = LANES if half % LANES == 0 else half
    chunks = half // step
    mine = lax.axis_index("expert")
    place = lax.axis_index("wide")
    z, c = place // 2, place % 2

    def twin(a):
        return lax.ppermute(a, "wide", [(i, i ^ 1) for i in range(wide)])

    def along(a, hops):
        return lax.ppermute(
            a, "wide", [(2 * s + i, 2 * t + i) for s, t in hops for i in range(2)]
        )

    def flip(a, bit):
        return lax.ppermute(a, "expert", [(e, e ^ bit) for e in range(experts)])

    def by_core(a, b, axis):
        return jnp.where(
            c == 0, jnp.concatenate((a, b), axis), jnp.concatenate((b, a), axis)
        )

    def packed(side):
        cut = [
            lax.dynamic_slice_in_dim(w[0], side * half, half, 1).reshape(feats, chunks, step)
            for w in (w_gate, w_up, w_down)
        ]
        return [jnp.concatenate([p[:, i] for p in cut], axis=1) for i in range(chunks)]

    kept, given = packed(c), twin(jnp.stack(packed(1 - c)))
    shards = [by_core(kept[i], given[i], 0) for i in range(chunks)]

    named = jnp.arange(experts, dtype=jnp.int32)[None, :]
    gates = sum(
        jnp.where(routes[:, k : k + 1] == named, gate_prob[:, k : k + 1], 0.0)
        for k in range(routes.shape[1])
    )
    high = lax.reduce_precision(gates, 8, 7)
    middle = lax.reduce_precision(gates - high, 8, 7)
    terms = jnp.concatenate((high, middle, gates - high - middle), axis=1).astype(BF16)
    terms = jnp.pad(terms, ((0, 0), (0, LANES - terms.shape[1])))
    graded = jnp.concatenate((out_grad, terms), axis=1)

    t_two = jnp.concatenate((tokens, flip(tokens, 1)))
    g_one = flip(graded, 2)
    t_four = jnp.concatenate((t_two, flip(t_two, 2)))
    g_far = flip(jnp.concatenate((graded, g_one)), 1)
    g_four = jnp.concatenate((graded, g_far[:rows], g_one, g_far[rows:]))
    xin = jnp.concatenate((t_four, twin(t_four)))
    g_all = jnp.concatenate((g_four, twin(g_four)))
    lane = jnp.arange(LANES, dtype=jnp.int32)[None, :]
    ours = (lane % experts == mine) & (lane < 3 * experts)
    gate = jnp.sum(jnp.where(ours, g_all[:, width:].astype(F32), 0.0), axis=1, keepdims=True)
    scaled = (gate * g_all[:, :width].astype(F32)).astype(BF16)

    def gather(own):
        ups, downs = [own], [own]
        for s in range(1, line):
            ups.append(along(ups[-1], [(i, i + 1) for i in range(s - 1, line - 1)]))
            downs.append(along(downs[-1], [(i, i - 1) for i in range(1, line - s + 1)]))
        full = jnp.zeros((line,) + own.shape, own.dtype)
        full = lax.dynamic_update_index_in_dim(full, own, z, 0)
        for k in range(1, line):
            part = jnp.where(z >= k, ups[k], downs[line - k])
            full = lax.dynamic_update_index_in_dim(full, part, (z - k) % line, 0)
        return full.reshape(line * own.shape[0], own.shape[1])

    def scatter(parts):
        def block(k):
            return lax.dynamic_index_in_dim(parts, (z - k) % line, 0, keepdims=False)

        up = down = None
        for s in range(1, line):
            a, b = block(s), block(line - s)
            if up is not None:
                a, b = add(a, up), add(b, down)
            up = along(a, [(i, i + 1) for i in range(s)])
            down = along(b, [(i, i - 1) for i in range(line - s, line)])
        return block(0).astype(F32) + up.astype(F32) + down.astype(F32)

    total = None
    sums = []
    for i in range(chunks):
        full = gather(shards[i])
        pre = dot(xin, full[:, : 2 * step])
        back = dot(scaled, full[:, 2 * step :])
        hidden, gate_act, up_act = swish_backward(pre[:, :step], pre[:, step:], back)
        merged = jnp.concatenate((gate_act, up_act), axis=1)
        parts = jnp.concatenate(
            (dot_tn(xin, merged).astype(BF16), dot_tn(scaled, hidden).astype(BF16)), axis=1
        )
        sums.append(scatter(parts.reshape(line, 2 * feats, 3 * step)))
        partial = dot_nt(merged, full[:, : 2 * step])
        total = partial if total is None else total + partial

    own = [lax.dynamic_slice_in_dim(s, c * feats, feats, 0) for s in sums]
    other = [twin(lax.dynamic_slice_in_dim(s, (1 - c) * feats, feats, 0)) for s in sums]

    def grad_of(j):
        cols = slice(j * step, (j + 1) * step)
        a = jnp.concatenate([s[:, cols] for s in own], axis=1)
        b = jnp.concatenate([s[:, cols] for s in other], axis=1)
        return by_core(a, b, 1)[None]

    block = experts * rows
    ret = total[:block] + twin(total[block:].astype(BF16)).astype(F32)
    ret = ret.reshape(experts, rows, width)
    left, right = ret[:, :, : width // 2], ret[:, :, width // 2 :]
    left = left[:2] + flip(left[2:].astype(BF16), 2).astype(F32)
    odd = flip(jnp.stack((right[1], right[3])).astype(BF16), 1).astype(F32)
    left = left[0] + flip(left[1].astype(BF16), 1).astype(F32)
    right = right[0] + odd[0] + flip((right[2] + odd[1]).astype(BF16), 2).astype(F32)
    grad_input = jnp.concatenate((left, right), axis=1).astype(BF16)
    return (grad_input, grad_of(0), grad_of(1), grad_of(2))


def solution(mesh):
    experts, wide = mesh.shape["expert"], mesh.shape["wide"]
    split = P(("expert", "wide"), None)
    weight = P("expert", "wide", None)

    def on_device(tokens, out_grad, routes, *rest):
        dense = experts == 4 and wide % 2 == 0 and 2 * routes.shape[1] >= experts
        return (dense_plan if dense else slot_plan)(tokens, out_grad, routes, *rest)

    return jax.shard_map(
        on_device,
        mesh=mesh,
        in_specs=(split,) * 4 + (weight,) * 3,
        out_specs=(split, weight, weight, weight),
        check_vma=False,
    )
```

```python
import jax
import jax.numpy as jnp
from jax import lax
from jax.experimental import pallas as pl
from jax.experimental.pallas import tpu as pltpu
from jax.sharding import PartitionSpec as P

LANES = 128
F32 = jnp.float32
BF16 = jnp.bfloat16


def swish_backward(gate_pre, up_pre, hidden_grad):
    squash = jax.nn.sigmoid(gate_pre)
    active = gate_pre * squash
    hidden = (active * up_pre).astype(BF16)
    gate_act = (hidden_grad * up_pre * squash * (1.0 + gate_pre * (1.0 - squash))).astype(BF16)
    up_act = (hidden_grad * active).astype(BF16)
    return (hidden, gate_act, up_act)


def dot(a, b):
    return jnp.dot(a, b, preferred_element_type=F32)


def dot_tn(a, b):
    return lax.dot_general(a, b, (((0,), (0,)), ((), ())), preferred_element_type=F32)


def dot_nt(a, b):
    return lax.dot_general(a, b, (((1,), (1,)), ((), ())), preferred_element_type=F32)


def add(a, b):
    return (a.astype(F32) + b.astype(F32)).astype(BF16)


def slot_plan(tokens, out_grad, routes, gate_prob, w_gate, w_up, w_down):
    experts = lax.axis_size("expert")
    tok_count, top_count = routes.shape
    capacity = min(tok_count, 2 * tok_count * top_count // experts)
    slot_count = experts * capacity
    model_width = tokens.shape[1]
    hidden_units = w_gate.shape[2]
    flat_routes = routes.reshape(-1)
    order = jnp.arange(tok_count * top_count, dtype=jnp.int32)
    same = flat_routes[:, None] == flat_routes[None, :]
    before = jnp.sum((same & (order[None, :] < order[:, None])).astype(jnp.int32), axis=1)
    positions = flat_routes * capacity + before
    chosen = (positions[None, :] == jnp.arange(slot_count, dtype=jnp.int32)[:, None]).reshape(
        slot_count, tok_count, top_count
    )
    picker = jnp.sum(chosen.astype(F32), axis=2)
    slot_gate = jnp.sum(jnp.where(chosen, gate_prob[None, :, :], 0.0), axis=(1, 2))
    picker_half = picker.astype(BF16)
    sent_rows = dot(picker_half, tokens).astype(BF16)
    sent_grad = (dot(picker_half, out_grad) * slot_gate[:, None]).astype(BF16)

    def exchange(rows):
        return lax.all_to_all(
            rows.reshape(experts, capacity, model_width),
            "expert",
            split_axis=0,
            concat_axis=0,
            tiled=True,
        ).reshape(slot_count, model_width)

    rows_in = exchange(sent_rows)
    grad_in = exchange(sent_grad)
    full_gate, full_up, full_down = (
        lax.all_gather(w, "wide", axis=1, tiled=True)[0] for w in (w_gate, w_up, w_down)
    )
    hidden, gate_act, up_act = swish_backward(
        dot(rows_in, full_gate), dot(rows_in, full_up), dot(grad_in, full_down)
    )
    merged = jnp.concatenate((gate_act, up_act), axis=1)
    input_grad = dot_nt(merged, jnp.concatenate((full_gate, full_up), axis=1)).astype(BF16)
    parts = jnp.concatenate((dot_tn(rows_in, merged), dot_tn(grad_in, hidden)), axis=1)
    summed = lax.psum_scatter(
        parts.astype(BF16), "wide", scatter_dimension=0, tiled=True
    ).astype(F32)
    grads = tuple(
        summed[:, i * hidden_units : (i + 1) * hidden_units][None] for i in range(3)
    )
    grad_input = dot_tn(picker_half, exchange(input_grad)).astype(BF16)
    return (grad_input,) + grads


VMEM = pl.BlockSpec(memory_space=pltpu.VMEM)
SMEM = pl.BlockSpec(memory_space=pltpu.SMEM)
ANY = pl.BlockSpec(memory_space=pl.ANY)
LIMIT = 40 << 20


def call(body, ins, outs, operands, scratch=(), flops=0, limit=LIMIT):
    moved = sum(a.size * a.dtype.itemsize for a in operands)
    moved += sum(o.size * o.dtype.itemsize for o in outs)
    return pl.pallas_call(
        body,
        out_shape=outs,
        in_specs=ins,
        out_specs=[VMEM] * len(outs),
        scratch_shapes=list(scratch),
        cost_estimate=pl.CostEstimate(flops=flops, bytes_accessed=moved, transcendentals=0),
        compiler_params=pltpu.CompilerParams(vmem_limit_bytes=limit),
    )(*operands)


def half_of(ref, side, half, i, step):
    return ref[:, pl.ds(pl.multiple_of(side * half + i * step, step), step)]


def pack_kernel(chunks, step, at, gate, up, down, *outs):
    half = chunks * step
    c = at[1]
    for side, group in ((c, outs[:chunks]), (1 - c, outs[chunks:])):
        for i, out in enumerate(group):
            for m, ref in enumerate((gate, up, down)):
                out[:, m * step : (m + 1) * step] = half_of(ref, side, half, i, step)


def combine_kernel(chunks, at, *refs):
    kept, given, outs = refs[:chunks], refs[chunks : 2 * chunks], refs[2 * chunks :]
    feats = kept[0].shape[0]
    c = at[1]
    for a, b, out in zip(kept, given, outs):
        out[pl.ds(pl.multiple_of(c * feats, feats), feats), :] = a[...]
        out[pl.ds(pl.multiple_of((1 - c) * feats, feats), feats), :] = b[...]


def scale_kernel(experts, at, *refs):
    pieces, out = refs[:-1], refs[-1]
    rows, width = pieces[0].shape[0], out.shape[1]
    lane = lax.broadcasted_iota(jnp.int32, (rows, LANES), 1)
    ours = (lax.rem(lane, experts) == at[2]) & (lane < 3 * experts)
    for p, ref in enumerate(pieces):
        terms = jnp.where(ours, ref[:, width:].astype(F32), 0.0)
        gate = jnp.sum(terms, axis=1, keepdims=True)
        out[p * rows : (p + 1) * rows, :] = (gate * ref[:, :width].astype(F32)).astype(BF16)


def chunk_kernel(line, n_pieces, at, *refs):
    pieces, refs = refs[:n_pieces], refs[n_pieces:]
    scaled, own = refs[0], refs[1]
    ups, downs = refs[2 : 1 + line], refs[1 + line : 2 * line]
    outs = refs[2 * line : 2 * line + line + 2]
    parts, merged, both = outs[:line], outs[line], outs[line + 1]
    x, g, w, hid, xsem, gsem, wsem = refs[2 * line + line + 2 :]
    z = at[0]
    depth, step = own.shape[0], own.shape[1] // 3
    rows = x.shape[0] // n_pieces
    block = x.shape[0] // 4

    def shard(k):
        f = lax.rem(z - k + line, line)
        return w.at[pl.ds(pl.multiple_of(f * depth, depth), depth), :]

    pltpu.make_async_copy(own, shard(0), wsem.at[0]).start()
    for k in range(1, line):

        @pl.when(z >= k)
        def _(k=k):
            pltpu.make_async_copy(ups[k - 1], shard(k), wsem.at[k]).start()

        @pl.when(z < k)
        def _(k=k):
            pltpu.make_async_copy(downs[line - k - 1], shard(k), wsem.at[k]).start()

    x_copies = [
        pltpu.make_async_copy(ref, x.at[pl.ds(p * rows, rows), :], xsem.at[p])
        for p, ref in enumerate(pieces)
    ]
    g_copies = [
        pltpu.make_async_copy(
            scaled.at[pl.ds(r * block, block), :], g.at[pl.ds(r * block, block), :], gsem.at[r]
        )
        for r in range(4)
    ]
    for r in range(4):
        for p in range(r * n_pieces // 4, (r + 1) * n_pieces // 4):
            x_copies[p].start()
        g_copies[r].start()
    for k in range(line):
        pltpu.make_async_copy(own, shard(k), wsem.at[k]).wait()

    for r in range(4):
        for p in range(r * n_pieces // 4, (r + 1) * n_pieces // 4):
            x_copies[p].wait()
        g_copies[r].wait()
        here = slice(r * block, (r + 1) * block)
        pre = dot(x[here, :], w[:, : 2 * step])
        back = dot(g[here, :], w[:, 2 * step :])
        h, a, b = swish_backward(pre[:, :step], pre[:, step:], back)
        hid[here, :] = h
        merged[here, :step] = a
        merged[here, step:] = b

    for k in range(line):
        f = lax.rem(z - k + line, line)
        cols = pl.ds(pl.multiple_of(f * depth, depth), depth)
        parts[k][:, : 2 * step] = dot_tn(x[:, cols], merged[...]).astype(BF16)
        parts[k][:, 2 * step :] = dot_tn(g[:, cols], hid[...]).astype(BF16)
    both[...] = w[:, : 2 * step]


def route_kernel(chunks, *refs):
    merged, both = refs[:chunks], refs[chunks : 2 * chunks]
    keep, give = refs[2 * chunks :]
    rows, width = keep.shape
    tile = width // 8

    for out, first in ((give, rows), (keep, 0)):

        @pl.loop(0, 8)
        def _(t, out=out, first=first):
            cols = pl.ds(pl.multiple_of(t * tile, tile), tile)
            total = None
            for m, b in zip(merged, both):
                part = dot_nt(m[first : first + rows, :], b[cols, :])
                total = part if total is None else total + part
            out[:, cols] = total.astype(BF16)


def dense_plan(tokens, out_grad, routes, gate_prob, w_gate, w_up, w_down):
    experts = lax.axis_size("expert")
    wide = lax.axis_size("wide")
    line = wide // 2
    rows, width = tokens.shape
    feats = w_gate.shape[1]
    half = w_gate.shape[2] // 2
    step = LANES
    chunks = half // step
    mine = lax.axis_index("expert")
    place = lax.axis_index("wide")
    z, c = place // 2, place % 2
    at = jnp.stack((z, c, mine)).astype(jnp.int32)
    shape = jax.ShapeDtypeStruct

    def twin(a):
        return lax.ppermute(a, "wide", [(i, i ^ 1) for i in range(wide)])

    def along(a, hops):
        return lax.ppermute(
            a, "wide", [(2 * s + i, 2 * t + i) for s, t in hops for i in range(2)]
        )

    def flip(a, bit):
        return lax.ppermute(a, "expert", [(e, e ^ bit) for e in range(experts)])

    cut = [shape((feats, 3 * step), BF16)] * (2 * chunks)
    packed = call(
        lambda *r: pack_kernel(chunks, step, *r),
        [SMEM] + [VMEM] * 3,
        cut,
        (at, w_gate[0], w_up[0], w_down[0]),
    )
    given = [twin(a) for a in packed[chunks:]]
    shards = call(
        lambda *r: combine_kernel(chunks, *r),
        [SMEM] + [VMEM] * (2 * chunks),
        [shape((2 * feats, 3 * step), BF16)] * chunks,
        (at, *packed[:chunks], *given),
    )

    named = jnp.arange(experts, dtype=jnp.int32)[None, :]
    gates = sum(
        jnp.where(routes[:, k : k + 1] == named, gate_prob[:, k : k + 1], 0.0)
        for k in range(routes.shape[1])
    )
    high = lax.reduce_precision(gates, 8, 7)
    middle = lax.reduce_precision(gates - high, 8, 7)
    terms = jnp.concatenate((high, middle, gates - high - middle), axis=1).astype(BF16)
    terms = jnp.pad(terms, ((0, 0), (0, LANES - terms.shape[1])))
    graded = jnp.concatenate((out_grad, terms), axis=1)

    t = [tokens, flip(tokens, 1), flip(tokens, 2)]
    t.append(flip(t[1], 2))
    g = [graded, flip(graded, 1), flip(graded, 2)]
    g.append(flip(g[2], 1))
    t += [twin(a) for a in t]
    g += [twin(a) for a in g]
    count = len(t) * rows
    [scaled] = call(
        lambda *r: scale_kernel(experts, *r),
        [SMEM] + [VMEM] * len(g),
        [shape((count, width), BF16)],
        (at, *g),
    )

    def gather(own):
        ups, downs = [own], [own]
        for s in range(1, line):
            ups.append(along(ups[-1], [(i, i + 1) for i in range(s - 1, line - 1)]))
            downs.append(along(downs[-1], [(i, i - 1) for i in range(1, line - s + 1)]))
        return (own, *ups[1:], *downs[1:])

    def scatter(parts):
        up = down = None
        for s in range(1, line):
            a, b = parts[s], parts[line - s]
            if up is not None:
                a, b = add(a, up), add(b, down)
            up = along(a, [(i, i + 1) for i in range(s)])
            down = along(b, [(i, i - 1) for i in range(line - s, line)])
        return parts[0].astype(F32) + up.astype(F32) + down.astype(F32)

    merged, both, sums = [], [], []
    for i in range(chunks):
        got = call(
            lambda *r: chunk_kernel(line, len(t), *r),
            [SMEM] + [ANY] * (len(t) + 2 * line),
            [shape((2 * feats, 3 * step), BF16)] * line
            + [shape((count, 2 * step), BF16), shape((width, 2 * step), BF16)],
            (at, *t, scaled, *gather(shards[i])),
            (
                pltpu.VMEM((count, width), BF16),
                pltpu.VMEM((count, width), BF16),
                pltpu.VMEM((width, 3 * step), BF16),
                pltpu.VMEM((count, step), BF16),
                pltpu.SemaphoreType.DMA((len(t),)),
                pltpu.SemaphoreType.DMA((4,)),
                pltpu.SemaphoreType.DMA((line,)),
            ),
            flops=12 * count * width * step,
        )
        merged.append(got[line])
        both.append(got[line + 1])
        sums.append(scatter(got[:line]))

    block = experts * rows
    keep, give = call(
        lambda *r: route_kernel(chunks, *r),
        [VMEM] * (2 * chunks),
        [shape((block, width), BF16)] * 2,
        (*merged, *both),
        flops=4 * count * width * step * chunks,
    )
    ret = keep.astype(F32) + twin(give).astype(F32)
    ret = ret.reshape(experts, rows, width)
    left, right = ret[:, :, : width // 2], ret[:, :, width // 2 :]
    left = left[:2] + flip(left[2:].astype(BF16), 2).astype(F32)
    odd = flip(jnp.stack((right[1], right[3])).astype(BF16), 1).astype(F32)
    left = left[0] + flip(left[1].astype(BF16), 1).astype(F32)
    right = right[0] + odd[0] + flip((right[2] + odd[1]).astype(BF16), 2).astype(F32)
    grad_input = jnp.concatenate((left, right), axis=1).astype(BF16)

    own = [lax.dynamic_slice_in_dim(s, c * feats, feats, 0) for s in sums]
    other = [twin(lax.dynamic_slice_in_dim(s, (1 - c) * feats, feats, 0)) for s in sums]

    def grad_of(j):
        cols = slice(j * step, (j + 1) * step)
        a = jnp.concatenate([s[:, cols] for s in own], axis=1)
        b = jnp.concatenate([s[:, cols] for s in other], axis=1)
        first = jnp.concatenate((a, b), axis=1)
        return jnp.where(c == 0, first, jnp.concatenate((b, a), axis=1))[None]

    return (grad_input, grad_of(0), grad_of(1), grad_of(2))


def solution(mesh):
    experts, wide = mesh.shape["expert"], mesh.shape["wide"]
    split = P(("expert", "wide"), None)
    weight = P("expert", "wide", None)

    def on_device(tokens, out_grad, routes, *rest):
        dense = experts == 4 and wide % 2 == 0 and 2 * routes.shape[1] >= experts
        dense = dense and rest[1].shape[2] % (2 * LANES) == 0
        return (dense_plan if dense else slot_plan)(tokens, out_grad, routes, *rest)

    return jax.shard_map(
        on_device,
        mesh=mesh,
        in_specs=(split,) * 4 + (weight,) * 3,
        out_specs=(split, weight, weight, weight),
        check_vma=False,
    )
```

```python
import jax
import jax.numpy as jnp
from jax import lax
from jax.experimental import pallas as pl
from jax.experimental.pallas import tpu as pltpu
from jax.experimental import pallas as pl
from jax.experimental.pallas import tpu as pltpu
from jax.sharding import PartitionSpec as P

LANES = 128
F32 = jnp.float32
BF16 = jnp.bfloat16


def swish_backward(gate_pre, up_pre, hidden_grad):
    squash = jax.nn.sigmoid(gate_pre)
    active = gate_pre * squash
    hidden = (active * up_pre).astype(BF16)
    gate_act = (hidden_grad * up_pre * squash * (1.0 + gate_pre * (1.0 - squash))).astype(BF16)
    up_act = (hidden_grad * active).astype(BF16)
    return (hidden, gate_act, up_act)


def dot(a, b):
    return jnp.dot(a, b, preferred_element_type=F32)


def dot_tn(a, b):
    return lax.dot_general(a, b, (((0,), (0,)), ((), ())), preferred_element_type=F32)


def dot_nt(a, b):
    return lax.dot_general(a, b, (((1,), (1,)), ((), ())), preferred_element_type=F32)


def add(a, b):
    return (a.astype(F32) + b.astype(F32)).astype(BF16)


def slot_plan(tokens, out_grad, routes, gate_prob, w_gate, w_up, w_down):
    experts = lax.axis_size("expert")
    tok_count, top_count = routes.shape
    capacity = min(tok_count, 2 * tok_count * top_count // experts)
    slot_count = experts * capacity
    model_width = tokens.shape[1]
    hidden_units = w_gate.shape[2]
    flat_routes = routes.reshape(-1)
    order = jnp.arange(tok_count * top_count, dtype=jnp.int32)
    same = flat_routes[:, None] == flat_routes[None, :]
    before = jnp.sum((same & (order[None, :] < order[:, None])).astype(jnp.int32), axis=1)
    positions = flat_routes * capacity + before
    chosen = (positions[None, :] == jnp.arange(slot_count, dtype=jnp.int32)[:, None]).reshape(
        slot_count, tok_count, top_count
    )
    picker = jnp.sum(chosen.astype(F32), axis=2)
    slot_gate = jnp.sum(jnp.where(chosen, gate_prob[None, :, :], 0.0), axis=(1, 2))
    picker_half = picker.astype(BF16)
    sent_rows = dot(picker_half, tokens).astype(BF16)
    sent_grad = (dot(picker_half, out_grad) * slot_gate[:, None]).astype(BF16)

    def exchange(rows):
        return lax.all_to_all(
            rows.reshape(experts, capacity, model_width),
            "expert",
            split_axis=0,
            concat_axis=0,
            tiled=True,
        ).reshape(slot_count, model_width)

    rows_in = exchange(sent_rows)
    grad_in = exchange(sent_grad)
    full_gate, full_up, full_down = (
        lax.all_gather(w, "wide", axis=1, tiled=True)[0] for w in (w_gate, w_up, w_down)
    )
    hidden, gate_act, up_act = swish_backward(
        dot(rows_in, full_gate), dot(rows_in, full_up), dot(grad_in, full_down)
    )
    merged = jnp.concatenate((gate_act, up_act), axis=1)
    input_grad = dot_nt(merged, jnp.concatenate((full_gate, full_up), axis=1)).astype(BF16)
    parts = jnp.concatenate((dot_tn(rows_in, merged), dot_tn(grad_in, hidden)), axis=1)
    summed = lax.psum_scatter(
        parts.astype(BF16), "wide", scatter_dimension=0, tiled=True
    ).astype(F32)
    grads = tuple(
        summed[:, i * hidden_units : (i + 1) * hidden_units][None] for i in range(3)
    )
    grad_input = dot_tn(picker_half, exchange(input_grad)).astype(BF16)
    return (grad_input,) + grads


VMEM = pl.BlockSpec(memory_space=pltpu.VMEM)
SMEM = pl.BlockSpec(memory_space=pltpu.SMEM)
ANY = pl.BlockSpec(memory_space=pl.ANY)
LIMIT = 40 << 20


def call(body, ins, outs, operands, scratch=(), flops=0, limit=LIMIT):
    moved = sum(a.size * a.dtype.itemsize for a in operands)
    moved += sum(o.size * o.dtype.itemsize for o in outs)
    return pl.pallas_call(
        body,
        out_shape=outs,
        in_specs=ins,
        out_specs=[VMEM] * len(outs),
        scratch_shapes=list(scratch),
        cost_estimate=pl.CostEstimate(flops=flops, bytes_accessed=moved, transcendentals=0),
        compiler_params=pltpu.CompilerParams(vmem_limit_bytes=limit),
    )(*operands)


def half_of(ref, side, half, i, step):
    return ref[:, pl.ds(pl.multiple_of(side * half + i * step, step), step)]


def pack_kernel(chunks, step, at, gate, up, down, *outs):
    half = chunks * step
    c = at[1]
    for side, group in ((c, outs[:chunks]), (1 - c, outs[chunks:])):
        for i, out in enumerate(group):
            for m, ref in enumerate((gate, up, down)):
                out[:, m * step : (m + 1) * step] = half_of(ref, side, half, i, step)


def combine_kernel(chunks, at, *refs):
    kept, given, outs = refs[:chunks], refs[chunks : 2 * chunks], refs[2 * chunks :]
    feats = kept[0].shape[0]
    c = at[1]
    for a, b, out in zip(kept, given, outs):
        out[pl.ds(pl.multiple_of(c * feats, feats), feats), :] = a[...]
        out[pl.ds(pl.multiple_of((1 - c) * feats, feats), feats), :] = b[...]


def scale_kernel(experts, at, *refs):
    pieces, out = refs[:-1], refs[-1]
    rows, width = pieces[0].shape[0], out.shape[1]
    lane = lax.broadcasted_iota(jnp.int32, (rows, LANES), 1)
    ours = (lax.rem(lane, experts) == at[2]) & (lane < 3 * experts)
    for p, ref in enumerate(pieces):
        terms = jnp.where(ours, ref[:, width:].astype(F32), 0.0)
        gate = jnp.sum(terms, axis=1, keepdims=True)
        out[p * rows : (p + 1) * rows, :] = (gate * ref[:, :width].astype(F32)).astype(BF16)


def chunk_kernel(line, n_pieces, at, *refs):
    pieces, refs = refs[:n_pieces], refs[n_pieces:]
    scaled, own = refs[0], refs[1]
    ups, downs = refs[2 : 1 + line], refs[1 + line : 2 * line]
    outs = refs[2 * line : 2 * line + line + 2]
    parts, merged, both = outs[:line], outs[line], outs[line + 1]
    x, g, w, hid, xsem, gsem, wsem = refs[2 * line + line + 2 :]
    z = at[0]
    depth, step = own.shape[0], own.shape[1] // 3
    rows = x.shape[0] // n_pieces
    block = x.shape[0] // 4

    def shard(k):
        f = lax.rem(z - k + line, line)
        return w.at[pl.ds(pl.multiple_of(f * depth, depth), depth), :]

    pltpu.make_async_copy(own, shard(0), wsem.at[0]).start()
    for k in range(1, line):

        @pl.when(z >= k)
        def _(k=k):
            pltpu.make_async_copy(ups[k - 1], shard(k), wsem.at[k]).start()

        @pl.when(z < k)
        def _(k=k):
            pltpu.make_async_copy(downs[line - k - 1], shard(k), wsem.at[k]).start()

    x_copies = [
        pltpu.make_async_copy(ref, x.at[pl.ds(p * rows, rows), :], xsem.at[p])
        for p, ref in enumerate(pieces)
    ]
    g_copies = [
        pltpu.make_async_copy(
            scaled.at[pl.ds(r * block, block), :], g.at[pl.ds(r * block, block), :], gsem.at[r]
        )
        for r in range(4)
    ]
    for r in range(4):
        for p in range(r * n_pieces // 4, (r + 1) * n_pieces // 4):
            x_copies[p].start()
        g_copies[r].start()
    for k in range(line):
        pltpu.make_async_copy(own, shard(k), wsem.at[k]).wait()

    for r in range(4):
        for p in range(r * n_pieces // 4, (r + 1) * n_pieces // 4):
            x_copies[p].wait()
        g_copies[r].wait()
        here = slice(r * block, (r + 1) * block)
        pre = dot(x[here, :], w[:, : 2 * step])
        back = dot(g[here, :], w[:, 2 * step :])
        h, a, b = swish_backward(pre[:, :step], pre[:, step:], back)
        hid[here, :] = h
        merged[here, :step] = a
        merged[here, step:] = b

    for k in range(line):
        f = lax.rem(z - k + line, line)
        cols = pl.ds(pl.multiple_of(f * depth, depth), depth)
        parts[k][:, : 2 * step] = dot_tn(x[:, cols], merged[...]).astype(BF16)
        parts[k][:, 2 * step :] = dot_tn(g[:, cols], hid[...]).astype(BF16)
    both[...] = w[:, : 2 * step]


def route_kernel(chunks, *refs):
    merged, both = refs[:chunks], refs[chunks : 2 * chunks]
    keep, give = refs[2 * chunks :]
    rows, width = keep.shape
    tile = width // 8

    for out, first in ((give, rows), (keep, 0)):

        @pl.loop(0, 8)
        def _(t, out=out, first=first):
            cols = pl.ds(pl.multiple_of(t * tile, tile), tile)
            total = None
            for m, b in zip(merged, both):
                part = dot_nt(m[first : first + rows, :], b[cols, :])
                total = part if total is None else total + part
            out[:, cols] = total.astype(BF16)


def dense_plan(tokens, out_grad, routes, gate_prob, w_gate, w_up, w_down):
    experts = lax.axis_size("expert")
    wide = lax.axis_size("wide")
    line = wide // 2
    rows, width = tokens.shape
    feats = w_gate.shape[1]
    half = w_gate.shape[2] // 2
    step = LANES
    chunks = half // step
    mine = lax.axis_index("expert")
    place = lax.axis_index("wide")
    z, c = place // 2, place % 2
    at = jnp.stack((z, c, mine)).astype(jnp.int32)
    shape = jax.ShapeDtypeStruct

    def after(a, *b):
        return lax.optimization_barrier((a, *b))[0]

    def twin(a):
        return lax.ppermute(a, "wide", [(i, i ^ 1) for i in range(wide)])

    def along(a, hops):
        return lax.ppermute(
            a, "wide", [(2 * s + i, 2 * t + i) for s, t in hops for i in range(2)]
        )

    def flip(a, bit):
        return lax.ppermute(a, "expert", [(e, e ^ bit) for e in range(experts)])

    cut = [shape((feats, 3 * step), BF16)] * (2 * chunks)
    packed = call(
        lambda *r: pack_kernel(chunks, step, *r),
        [SMEM] + [VMEM] * 3,
        cut,
        (at, w_gate[0], w_up[0], w_down[0]),
    )
    given = [twin(a) for a in packed[chunks:]]
    shards = call(
        lambda *r: combine_kernel(chunks, *r),
        [SMEM] + [VMEM] * (2 * chunks),
        [shape((2 * feats, 3 * step), BF16)] * chunks,
        (at, *packed[:chunks], *given),
    )

    named = jnp.arange(experts, dtype=jnp.int32)[None, :]
    gates = sum(
        jnp.where(routes[:, k : k + 1] == named, gate_prob[:, k : k + 1], 0.0)
        for k in range(routes.shape[1])
    )
    high = lax.reduce_precision(gates, 8, 7)
    middle = lax.reduce_precision(gates - high, 8, 7)
    terms = jnp.concatenate((high, middle, gates - high - middle), axis=1).astype(BF16)
    terms = jnp.pad(terms, ((0, 0), (0, LANES - terms.shape[1])))
    graded = jnp.concatenate((out_grad, terms), axis=1)

    with jax.named_scope("rows"):
        t = [tokens, *(after(flip(tokens, bit), *shards) for bit in (1, 2))]
        g = [graded, *(after(flip(graded, bit), *shards) for bit in (1, 2))]
        t.append(flip(t[1], 2))
        g.append(flip(g[2], 1))
        t += [twin(a) for a in t]
        g += [twin(a) for a in g]
    count = len(t) * rows
    [scaled] = call(
        lambda *r: scale_kernel(experts, *r),
        [SMEM] + [VMEM] * len(g),
        [shape((count, width), BF16)],
        (at, *g),
    )

    def gather(own, before):
        own = after(own, *before)
        ups, downs = [own], [own]
        for s in range(1, line):
            with jax.named_scope(f"gather_step_{s}"):
                ups.append(along(ups[-1], [(i, i + 1) for i in range(s - 1, line - 1)]))
                downs.append(along(downs[-1], [(i, i - 1) for i in range(1, line - s + 1)]))
        return (own, *ups[1:], *downs[1:]), (ups[line - 2], downs[line - 2])

    def scatter(parts, waits):
        up = down = None
        for s in range(1, line):
            a, b = parts[s], parts[line - s]
            if up is not None:
                a, b = add(a, up), add(b, down)
            if waits:
                a, b = after(a, waits[s - 1]), after(b, waits[s - 1])
            with jax.named_scope(f"scatter_step_{s}"):
                up = along(a, [(i, i + 1) for i in range(s)])
                down = along(b, [(i, i - 1) for i in range(line - s, line)])
        return parts[0].astype(F32) + up.astype(F32) + down.astype(F32)

    merged, both, sums, before = [], [], [], ()
    for i in range(chunks):
        loaded, before = gather(shards[i], before)
        got = call(
            lambda *r: chunk_kernel(line, len(t), *r),
            [SMEM] + [ANY] * (len(t) + 2 * line),
            [shape((2 * feats, 3 * step), BF16)] * line
            + [shape((count, 2 * step), BF16), shape((width, 2 * step), BF16)],
            (at, *t, scaled, *loaded),
            (
                pltpu.VMEM((count, width), BF16),
                pltpu.VMEM((count, width), BF16),
                pltpu.VMEM((width, 3 * step), BF16),
                pltpu.VMEM((count, step), BF16),
                pltpu.SemaphoreType.DMA((len(t),)),
                pltpu.SemaphoreType.DMA((4,)),
                pltpu.SemaphoreType.DMA((line,)),
            ),
            flops=12 * count * width * step,
        )
        merged.append(got[line])
        both.append(got[line + 1])
        if i < chunks - 1:
            sums.append(scatter(got[:line], ()))

    block = experts * rows
    keep, give = call(
        lambda *r: route_kernel(chunks, *r),
        [VMEM] * (2 * chunks),
        [shape((block, width), BF16)] * 2,
        (*merged, *both),
        flops=4 * count * width * step * chunks,
    )
    with jax.named_scope("back"):
        other = twin(give)
        ret = keep.astype(F32) + other.astype(F32)
        ret = ret.reshape(experts, rows, width)
        left, right = ret[:, :, : width // 2], ret[:, :, width // 2 :]
        far = flip(left[2:].astype(BF16), 2)
        odd = flip(jnp.stack((right[1], right[3])).astype(BF16), 1)
        left = left[:2] + far.astype(F32)
        near = flip(left[1].astype(BF16), 1)
        last = flip((right[2] + odd[1].astype(F32)).astype(BF16), 2)
        left = left[0] + near.astype(F32)
        right = right[0] + odd[0].astype(F32) + last.astype(F32)
        grad_input = jnp.concatenate((left, right), axis=1).astype(BF16)
    sums.append(scatter(got[:line], (got[0], other, odd)))

    own = [lax.dynamic_slice_in_dim(s, c * feats, feats, 0) for s in sums]
    other = [twin(lax.dynamic_slice_in_dim(s, (1 - c) * feats, feats, 0)) for s in sums]

    def grad_of(j):
        cols = slice(j * step, (j + 1) * step)
        a = jnp.concatenate([s[:, cols] for s in own], axis=1)
        b = jnp.concatenate([s[:, cols] for s in other], axis=1)
        first = jnp.concatenate((a, b), axis=1)
        return jnp.where(c == 0, first, jnp.concatenate((b, a), axis=1))[None]

    return (grad_input, grad_of(0), grad_of(1), grad_of(2))


def solution(mesh):
    experts, wide = mesh.shape["expert"], mesh.shape["wide"]
    split = P(("expert", "wide"), None)
    weight = P("expert", "wide", None)

    def on_device(tokens, out_grad, routes, *rest):
        dense = experts == 4 and wide % 2 == 0 and 2 * routes.shape[1] >= experts
        dense = dense and rest[1].shape[2] % (2 * LANES) == 0
        return (dense_plan if dense else slot_plan)(tokens, out_grad, routes, *rest)

    return jax.shard_map(
        on_device,
        mesh=mesh,
        in_specs=(split,) * 4 + (weight,) * 3,
        out_specs=(split, weight, weight, weight),
        check_vma=False,
    )
```

```python
import jax
import jax.numpy as jnp
from jax import lax
from jax.experimental import pallas as pl
from jax.experimental.pallas import tpu as pltpu
from jax.experimental import pallas as pl
from jax.experimental.pallas import tpu as pltpu
from jax.experimental import pallas as pl
from jax.experimental.pallas import tpu as pltpu
from jax.experimental import pallas as pl
from jax.experimental.pallas import tpu as pltpu
from jax.sharding import PartitionSpec as P

LANES = 128
F32 = jnp.float32
BF16 = jnp.bfloat16


def swish_backward(gate_pre, up_pre, hidden_grad):
    squash = jax.nn.sigmoid(gate_pre)
    active = gate_pre * squash
    hidden = (active * up_pre).astype(BF16)
    gate_act = (hidden_grad * up_pre * squash * (1.0 + gate_pre * (1.0 - squash))).astype(BF16)
    up_act = (hidden_grad * active).astype(BF16)
    return (hidden, gate_act, up_act)


def dot(a, b):
    return jnp.dot(a, b, preferred_element_type=F32)


def dot_tn(a, b):
    return lax.dot_general(a, b, (((0,), (0,)), ((), ())), preferred_element_type=F32)


def dot_nt(a, b):
    return lax.dot_general(a, b, (((1,), (1,)), ((), ())), preferred_element_type=F32)


def add(a, b):
    return (a.astype(F32) + b.astype(F32)).astype(BF16)


def slot_plan(tokens, out_grad, routes, gate_prob, w_gate, w_up, w_down):
    experts = lax.axis_size("expert")
    tok_count, top_count = routes.shape
    capacity = min(tok_count, 2 * tok_count * top_count // experts)
    slot_count = experts * capacity
    model_width = tokens.shape[1]
    hidden_units = w_gate.shape[2]
    flat_routes = routes.reshape(-1)
    order = jnp.arange(tok_count * top_count, dtype=jnp.int32)
    same = flat_routes[:, None] == flat_routes[None, :]
    before = jnp.sum((same & (order[None, :] < order[:, None])).astype(jnp.int32), axis=1)
    positions = flat_routes * capacity + before
    chosen = (positions[None, :] == jnp.arange(slot_count, dtype=jnp.int32)[:, None]).reshape(
        slot_count, tok_count, top_count
    )
    picker = jnp.sum(chosen.astype(F32), axis=2)
    slot_gate = jnp.sum(jnp.where(chosen, gate_prob[None, :, :], 0.0), axis=(1, 2))
    picker_half = picker.astype(BF16)
    sent_rows = dot(picker_half, tokens).astype(BF16)
    sent_grad = (dot(picker_half, out_grad) * slot_gate[:, None]).astype(BF16)

    def exchange(rows):
        return lax.all_to_all(
            rows.reshape(experts, capacity, model_width),
            "expert",
            split_axis=0,
            concat_axis=0,
            tiled=True,
        ).reshape(slot_count, model_width)

    rows_in = exchange(sent_rows)
    grad_in = exchange(sent_grad)
    full_gate, full_up, full_down = (
        lax.all_gather(w, "wide", axis=1, tiled=True)[0] for w in (w_gate, w_up, w_down)
    )
    hidden, gate_act, up_act = swish_backward(
        dot(rows_in, full_gate), dot(rows_in, full_up), dot(grad_in, full_down)
    )
    merged = jnp.concatenate((gate_act, up_act), axis=1)
    input_grad = dot_nt(merged, jnp.concatenate((full_gate, full_up), axis=1)).astype(BF16)
    parts = jnp.concatenate((dot_tn(rows_in, merged), dot_tn(grad_in, hidden)), axis=1)
    summed = lax.psum_scatter(
        parts.astype(BF16), "wide", scatter_dimension=0, tiled=True
    ).astype(F32)
    grads = tuple(
        summed[:, i * hidden_units : (i + 1) * hidden_units][None] for i in range(3)
    )
    grad_input = dot_tn(picker_half, exchange(input_grad)).astype(BF16)
    return (grad_input,) + grads


VMEM = pl.BlockSpec(memory_space=pltpu.VMEM)
SMEM = pl.BlockSpec(memory_space=pltpu.SMEM)
ANY = pl.BlockSpec(memory_space=pl.ANY)
LIMIT = 28 << 20


def call(body, ins, outs, operands, scratch=(), flops=0, limit=LIMIT):
    moved = sum(a.size * a.dtype.itemsize for a in (*operands, *outs))
    return pl.pallas_call(
        body,
        out_shape=outs,
        in_specs=ins,
        out_specs=[VMEM] * len(outs),
        scratch_shapes=list(scratch),
        cost_estimate=pl.CostEstimate(flops=flops, bytes_accessed=moved, transcendentals=0),
        compiler_params=pltpu.CompilerParams(vmem_limit_bytes=limit),
    )(*operands)


def pack_kernel(step, gate, up, down, *outs):
    for i, out in enumerate(outs):
        for m, ref in enumerate((gate, up, down)):
            out[:, m * step : (m + 1) * step] = ref[:, i * step : (i + 1) * step]


def scale_kernel(experts, at, *refs):
    pieces, out = refs[:-1], refs[-1]
    rows, width = pieces[0].shape[0], out.shape[1]
    lane = lax.broadcasted_iota(jnp.int32, (rows, LANES), 1)
    ours = (lax.rem(lane, experts) == at[2]) & (lane < 3 * experts)
    for p, ref in enumerate(pieces):
        terms = jnp.where(ours, ref[:, width:].astype(F32), 0.0)
        gate = jnp.sum(terms, axis=1, keepdims=True)
        out[p * rows : (p + 1) * rows, :] = (gate * ref[:, :width].astype(F32)).astype(BF16)


def chunk_kernel(line, n_pieces, whole, at, *refs):
    pieces, scaled, refs = refs[:n_pieces], refs[n_pieces], refs[n_pieces + 1 :]
    n_weights = 1 if whole else 2 * (2 * line - 1)
    weights, refs = refs[:n_weights], refs[n_weights:]
    mine, theirs, merged, both = refs[:line], refs[line], refs[line + 1], refs[line + 2]
    x, g, w, hid, xsem, gsem, wsem = refs[line + 3 :]
    z, c = at[0], at[1]
    feats = w.shape[0] // (2 * line)
    step = w.shape[1] // 3
    rows = x.shape[0] // n_pieces
    parts = 2 * line
    blocks = 2
    block = x.shape[0] // blocks

    def rows_of(f):
        return pl.ds(pl.multiple_of(f * feats, feats), feats)

    def owner(k, side):
        return lax.rem(z - k + line, line) * 2 + (c if side == 0 else 1 - c)

    if whole:
        for f in range(parts):
            here = pl.ds(f * feats, feats)
            pltpu.make_async_copy(weights[0].at[here, :], w.at[here, :], wsem.at[f]).start()
    else:
        for side in range(2):
            own, *rest = weights[side * (2 * line - 1) : (side + 1) * (2 * line - 1)]
            ups, downs = rest[: line - 1], rest[line - 1 :]
            sem = wsem.at[side * line]
            pltpu.make_async_copy(own, w.at[rows_of(owner(0, side)), :], sem).start()
            for k in range(1, line):
                to = w.at[rows_of(owner(k, side)), :]
                sem = wsem.at[side * line + k]

                @pl.when(z >= k)
                def _(k=k, to=to, sem=sem, ups=ups):
                    pltpu.make_async_copy(ups[k - 1], to, sem).start()

                @pl.when(z < k)
                def _(k=k, to=to, sem=sem, downs=downs):
                    pltpu.make_async_copy(downs[line - k - 1], to, sem).start()

    x_copies = [
        pltpu.make_async_copy(ref, x.at[pl.ds(p * rows, rows), :], xsem.at[p])
        for p, ref in enumerate(pieces)
    ]
    g_copies = []
    for r in range(blocks):
        here = pl.ds(r * block, block)
        g_copies.append(pltpu.make_async_copy(scaled.at[here, :], g.at[here, :], gsem.at[r]))
    for r in range(blocks):
        for p in range(r * n_pieces // blocks, (r + 1) * n_pieces // blocks):
            x_copies[p].start()
        g_copies[r].start()
    for f in range(parts):
        part = w.at[pl.ds(f * feats, feats), :]
        pltpu.make_async_copy(part, part, wsem.at[f]).wait()

    for r in range(blocks):
        for p in range(r * n_pieces // blocks, (r + 1) * n_pieces // blocks):
            x_copies[p].wait()
        g_copies[r].wait()
        here = slice(r * block, (r + 1) * block)
        pre = dot(x[here, :], w[:, : 2 * step])
        back = dot(g[here, :], w[:, 2 * step :])
        h, a, b = swish_backward(pre[:, :step], pre[:, step:], back)
        hid[here, :] = h
        merged[here, :step] = a
        merged[here, step:] = b

    for side in (1, 0):
        for k in range(line):
            cols = rows_of(owner(k, side))
            out = theirs.at[k] if side else mine[k]
            out[:, : 2 * step] = dot_tn(x[:, cols], merged[...]).astype(BF16)
            out[:, 2 * step :] = dot_tn(g[:, cols], hid[...]).astype(BF16)
    both[...] = w[:, : 2 * step]


def route_kernel(chunks, rows, *refs):
    merged, both = refs[:chunks], refs[chunks : 2 * chunks]
    far, odd, left, right = refs[2 * chunks :]
    width = far.shape[1]
    tile = width // 4

    def emit(out, blocks, first):
        @pl.loop(0, 4)
        def _(t):
            cols = pl.ds(pl.multiple_of(t * tile, tile), tile)
            for n, b in enumerate(blocks):
                here = slice(b * rows, (b + 1) * rows)
                total = None
                for m, w in zip(merged, both):
                    wide_cols = pl.ds(pl.multiple_of(first + t * tile, tile), tile)
                    part = dot_nt(m[here, :], w[wide_cols, :])
                    total = part if total is None else total + part
                out[n * rows : (n + 1) * rows, cols] = total.astype(out.dtype)

    emit(far, (2, 3), 0)
    emit(odd, (1, 3), width)
    emit(left, (0, 1), 0)
    emit(right, (0, 2), width)


def dense_plan(tokens, out_grad, routes, gate_prob, w_gate, w_up, w_down):
    experts = lax.axis_size("expert")
    wide = lax.axis_size("wide")
    line = wide // 2
    rows, width = tokens.shape
    feats = w_gate.shape[1]
    step = 2 * LANES
    chunks = w_gate.shape[2] // step
    count = experts * rows
    mine = lax.axis_index("expert")
    place = lax.axis_index("wide")
    z, c = place // 2, place % 2
    at = jnp.stack((z, c, mine)).astype(jnp.int32)
    shape = jax.ShapeDtypeStruct

    def after(a, *b):
        return lax.optimization_barrier((a, *b))[0]

    def twin(a):
        return lax.ppermute(a, "wide", [(i, i ^ 1) for i in range(wide)])

    def along(a, hops):
        return lax.ppermute(
            a, "wide", [(2 * s + i, 2 * t + i) for s, t in hops for i in range(2)]
        )

    def flip(a, bit):
        return lax.ppermute(a, "expert", [(e, e ^ bit) for e in range(experts)])

    own = call(
        lambda *r: pack_kernel(step, *r),
        [VMEM] * 3,
        [shape((feats, 3 * step), BF16)] * chunks,
        (w_gate[0], w_up[0], w_down[0]),
    )
    whole = [lax.all_gather(a, "wide", axis=0, tiled=True) for a in own[1:]]

    def gather(a):
        ups, downs = [a], [a]
        for s in range(1, line):
            with jax.named_scope(f"gather_step_{s}"):
                ups.append(along(ups[-1], [(i, i + 1) for i in range(s - 1, line - 1)]))
                downs.append(along(downs[-1], [(i, i - 1) for i in range(1, line - s + 1)]))
        held = (a, *ups[1:], *downs[1:])
        return held + tuple(twin(p) for p in held)

    first = gather(own[0])

    named = jnp.arange(experts, dtype=jnp.int32)[None, :]
    gates = sum(
        jnp.where(routes[:, k : k + 1] == named, gate_prob[:, k : k + 1], 0.0)
        for k in range(routes.shape[1])
    )
    high = lax.reduce_precision(gates, 8, 7)
    middle = lax.reduce_precision(gates - high, 8, 7)
    terms = jnp.concatenate((high, middle, gates - high - middle), axis=1).astype(BF16)
    terms = jnp.pad(terms, ((0, 0), (0, LANES - terms.shape[1])))
    graded = jnp.concatenate((out_grad, terms), axis=1)
    with jax.named_scope("rows"):
        t = [tokens, flip(tokens, 1), flip(tokens, 2)]
        g = [graded, flip(graded, 1), flip(graded, 2)]
        t.append(flip(t[1], 2))
        g.append(flip(g[2], 1))
    [scaled] = call(
        lambda *r: scale_kernel(experts, *r),
        [SMEM] + [VMEM] * len(g),
        [shape((count, width), BF16)],
        (at, *g),
    )

    def scatter(parts, swapped, begin, last):
        def block(k, *more):
            total = parts[k].astype(F32)
            for m in (swapped[k], *more):
                total = total + m.astype(F32)
            return total.astype(BF16)

        with jax.named_scope("scatter_step_1"):
            a = jnp.where(z == 0, block(1), block(line - 1))
            up = down = along(after(a, *begin), [(0, 1), (line - 1, line - 2)])
            marks = [up]
        for s in range(2, line):
            if s == 2 and line == 4:
                a = b = block(2, up)
            elif s == 2:
                a = block(2, jnp.where(z == 1, up, 0))
                b = block(line - 2, jnp.where(z == line - 2, down, 0))
            else:
                a, b = block(s, up), block(line - s, down)
            if s == line - 1:
                a, b = after(a, *last), after(b, *last)
            with jax.named_scope(f"scatter_step_{s}"):
                up = along(a, [(i, i + 1) for i in range(s)])
                down = along(b, [(i, i - 1) for i in range(line - s, line)])
            marks.append(up)
        total = parts[0].astype(F32) + swapped[0].astype(F32)
        return total + up.astype(F32) + down.astype(F32), marks

    merged, both, sums, marks = [], [], [], ()
    for i in range(chunks):
        weights = first if i == 0 else (whole[i - 1],)
        got = call(
            lambda *r, i=i: chunk_kernel(line, len(t), i > 0, *r),
            [SMEM] + [ANY] * (len(t) + 1 + len(weights)),
            [shape((feats, 3 * step), BF16)] * line
            + [
                shape((line, feats, 3 * step), BF16),
                shape((count, 2 * step), BF16),
                shape((width, 2 * step), BF16),
            ],
            (at, *t, after(scaled, *marks[:1]), *weights),
            (
                pltpu.VMEM((count, width), BF16),
                pltpu.VMEM((count, width), BF16),
                pltpu.VMEM((width, 3 * step), BF16),
                pltpu.VMEM((count, step), BF16),
                pltpu.SemaphoreType.DMA((len(t),)),
                pltpu.SemaphoreType.DMA((2,)),
                pltpu.SemaphoreType.DMA((2 * line,)),
            ),
            flops=12 * count * width * step,
        )
        merged.append(got[line + 1])
        both.append(got[line + 2])
        swapped = twin(got[line])
        if i < chunks - 1:
            total, marks = scatter(got[:line], swapped, marks[1:2], ())
            sums.append(total)

    far, odd, left, right = call(
        lambda *r: route_kernel(chunks, rows, *r),
        [VMEM] * (2 * chunks),
        [shape((2 * rows, width // 2), BF16)] * 2 + [shape((2 * rows, width // 2), F32)] * 2,
        (*merged, *both),
        flops=4 * count * width * step * chunks,
    )
    with jax.named_scope("back"):
        far, odd = flip(far, 2), flip(odd, 1)
        left, right = left + far.astype(F32), right + odd.astype(F32)
        halfway = (left, right)
        near = flip(left[rows:].astype(BF16), 1)
        last = flip(right[rows:].astype(BF16), 2)
        left, right = left[:rows] + near.astype(F32), right[:rows] + last.astype(F32)
        grad_input = jnp.concatenate((left, right), axis=1).astype(BF16)
    sums.append(scatter(got[:line], swapped, marks[1:2], halfway)[0])

    def grad_of(j):
        cols = slice(j * step, (j + 1) * step)
        return jnp.concatenate([s[:, cols] for s in sums], axis=1)[None]

    return (grad_input, grad_of(0), grad_of(1), grad_of(2))


def solution(mesh):
    experts, wide = mesh.shape["expert"], mesh.shape["wide"]
    split = P(("expert", "wide"), None)
    weight = P("expert", "wide", None)

    def on_device(tokens, out_grad, routes, *rest):
        dense = experts == 4 and wide % 2 == 0 and 2 * routes.shape[1] >= experts
        dense = dense and rest[1].shape[2] % (2 * LANES) == 0
        return (dense_plan if dense else slot_plan)(tokens, out_grad, routes, *rest)

    return jax.shard_map(
        on_device,
        mesh=mesh,
        in_specs=(split,) * 4 + (weight,) * 3,
        out_specs=(split, weight, weight, weight),
        check_vma=False,
    )
```

```python
import jax
import jax.numpy as jnp
from jax import lax
from jax.experimental import pallas as pl
from jax.experimental.pallas import tpu as pltpu
from jax.experimental import pallas as pl
from jax.experimental.pallas import tpu as pltpu
from jax.experimental import pallas as pl
from jax.experimental.pallas import tpu as pltpu
from jax.experimental import pallas as pl
from jax.experimental.pallas import tpu as pltpu
from jax.experimental import pallas as pl
from jax.experimental.pallas import tpu as pltpu
from jax.experimental import pallas as pl
from jax.experimental.pallas import tpu as pltpu
from jax.experimental import pallas as pl
from jax.experimental.pallas import tpu as pltpu
from jax.sharding import PartitionSpec as P

LANES = 128
F32 = jnp.float32
BF16 = jnp.bfloat16


def swish_backward(gate_pre, up_pre, hidden_grad):
    squash = jax.nn.sigmoid(gate_pre)
    active = gate_pre * squash
    hidden = (active * up_pre).astype(BF16)
    gate_act = (hidden_grad * up_pre * squash * (1.0 + gate_pre * (1.0 - squash))).astype(BF16)
    up_act = (hidden_grad * active).astype(BF16)
    return (hidden, gate_act, up_act)


def dot(a, b):
    return jnp.dot(a, b, preferred_element_type=F32)


def dot_tn(a, b):
    return lax.dot_general(a, b, (((0,), (0,)), ((), ())), preferred_element_type=F32)


def dot_nt(a, b):
    return lax.dot_general(a, b, (((1,), (1,)), ((), ())), preferred_element_type=F32)


def add(a, b):
    return (a.astype(F32) + b.astype(F32)).astype(BF16)


def slot_plan(tokens, out_grad, routes, gate_prob, w_gate, w_up, w_down):
    experts = lax.axis_size("expert")
    tok_count, top_count = routes.shape
    capacity = min(tok_count, 2 * tok_count * top_count // experts)
    slot_count = experts * capacity
    model_width = tokens.shape[1]
    hidden_units = w_gate.shape[2]
    flat_routes = routes.reshape(-1)
    order = jnp.arange(tok_count * top_count, dtype=jnp.int32)
    same = flat_routes[:, None] == flat_routes[None, :]
    before = jnp.sum((same & (order[None, :] < order[:, None])).astype(jnp.int32), axis=1)
    positions = flat_routes * capacity + before
    chosen = (positions[None, :] == jnp.arange(slot_count, dtype=jnp.int32)[:, None]).reshape(
        slot_count, tok_count, top_count
    )
    picker = jnp.sum(chosen.astype(F32), axis=2)
    slot_gate = jnp.sum(jnp.where(chosen, gate_prob[None, :, :], 0.0), axis=(1, 2))
    picker_half = picker.astype(BF16)
    sent_rows = dot(picker_half, tokens).astype(BF16)
    sent_grad = (dot(picker_half, out_grad) * slot_gate[:, None]).astype(BF16)

    def exchange(rows):
        return lax.all_to_all(
            rows.reshape(experts, capacity, model_width),
            "expert",
            split_axis=0,
            concat_axis=0,
            tiled=True,
        ).reshape(slot_count, model_width)

    rows_in = exchange(sent_rows)
    grad_in = exchange(sent_grad)
    full_gate, full_up, full_down = (
        lax.all_gather(w, "wide", axis=1, tiled=True)[0] for w in (w_gate, w_up, w_down)
    )
    hidden, gate_act, up_act = swish_backward(
        dot(rows_in, full_gate), dot(rows_in, full_up), dot(grad_in, full_down)
    )
    merged = jnp.concatenate((gate_act, up_act), axis=1)
    input_grad = dot_nt(merged, jnp.concatenate((full_gate, full_up), axis=1)).astype(BF16)
    parts = jnp.concatenate((dot_tn(rows_in, merged), dot_tn(grad_in, hidden)), axis=1)
    summed = lax.psum_scatter(
        parts.astype(BF16), "wide", scatter_dimension=0, tiled=True
    ).astype(F32)
    grads = tuple(
        summed[:, i * hidden_units : (i + 1) * hidden_units][None] for i in range(3)
    )
    grad_input = dot_tn(picker_half, exchange(input_grad)).astype(BF16)
    return (grad_input,) + grads


VMEM = pl.BlockSpec(memory_space=pltpu.VMEM)
SMEM = pl.BlockSpec(memory_space=pltpu.SMEM)
HBM = pl.BlockSpec(memory_space=pltpu.HBM)
LIMIT = 28 << 20


def call(body, ins, outs, operands, scratch=(), flops=0, limit=LIMIT):
    moved = sum(a.size * a.dtype.itemsize for a in (*operands, *outs))
    return pl.pallas_call(
        body,
        out_shape=outs,
        in_specs=ins,
        out_specs=[VMEM] * len(outs),
        scratch_shapes=list(scratch),
        cost_estimate=pl.CostEstimate(flops=flops, bytes_accessed=moved, transcendentals=0),
        compiler_params=pltpu.CompilerParams(vmem_limit_bytes=limit),
    )(*operands)


def pack_kernel(step, gate, up, down, *outs):
    for i, out in enumerate(outs):
        for m, ref in enumerate((gate, up, down)):
            out[:, m * step : (m + 1) * step] = ref[:, i * step : (i + 1) * step]


def scale_kernel(experts, at, *refs):
    pieces, out = refs[:-1], refs[-1]
    rows, width = pieces[0].shape[0], out.shape[1]
    lane = lax.broadcasted_iota(jnp.int32, (rows, LANES), 1)
    ours = (lax.rem(lane, experts) == at[2]) & (lane < 3 * experts)
    for p, ref in enumerate(pieces):
        terms = jnp.where(ours, ref[:, width:].astype(F32), 0.0)
        gate = jnp.sum(terms, axis=1, keepdims=True)
        out[p * rows : (p + 1) * rows, :] = (gate * ref[:, :width].astype(F32)).astype(BF16)


def chunk_kernel(line, n_pieces, whole, at, *refs):
    pieces, scaled, refs = refs[:n_pieces], refs[n_pieces], refs[n_pieces + 1 :]
    n_weights = 1 if whole else 2 * (2 * line - 1)
    weights, refs = refs[:n_weights], refs[n_weights:]
    mine, theirs, merged, both = refs[:line], refs[line], refs[line + 1], refs[line + 2]
    x, g, w, hid, xsem, gsem, wsem = refs[line + 3 :]
    z, c = at[0], at[1]
    feats = w.shape[0] // (2 * line)
    step = w.shape[1] // 3
    rows = x.shape[0] // n_pieces
    parts = 2 * line
    blocks = 2
    block = x.shape[0] // blocks

    def rows_of(f):
        return pl.ds(pl.multiple_of(f * feats, feats), feats)

    def owner(k, side):
        return lax.rem(z - k + line, line) * 2 + (c if side == 0 else 1 - c)

    if whole:
        for f in range(parts):
            here = pl.ds(f * feats, feats)
            pltpu.make_async_copy(weights[0].at[here, :], w.at[here, :], wsem.at[f]).start()
    else:
        for side in range(2):
            own, *rest = weights[side * (2 * line - 1) : (side + 1) * (2 * line - 1)]
            ups, downs = rest[: line - 1], rest[line - 1 :]
            sem = wsem.at[side * line]
            pltpu.make_async_copy(own, w.at[rows_of(owner(0, side)), :], sem).start()
            for k in range(1, line):
                to = w.at[rows_of(owner(k, side)), :]
                sem = wsem.at[side * line + k]

                @pl.when(z >= k)
                def _(k=k, to=to, sem=sem, ups=ups):
                    pltpu.make_async_copy(ups[k - 1], to, sem).start()

                @pl.when(z < k)
                def _(k=k, to=to, sem=sem, downs=downs):
                    pltpu.make_async_copy(downs[line - k - 1], to, sem).start()

    x_copies = [
        pltpu.make_async_copy(ref, x.at[pl.ds(p * rows, rows), :], xsem.at[p])
        for p, ref in enumerate(pieces)
    ]
    g_copies = []
    for r in range(blocks):
        here = pl.ds(r * block, block)
        g_copies.append(pltpu.make_async_copy(scaled.at[here, :], g.at[here, :], gsem.at[r]))
    for r in range(blocks):
        for p in range(r * n_pieces // blocks, (r + 1) * n_pieces // blocks):
            x_copies[p].start()
        g_copies[r].start()
    for f in range(parts):
        part = w.at[pl.ds(f * feats, feats), :]
        pltpu.make_async_copy(part, part, wsem.at[f]).wait()

    for r in range(blocks):
        for p in range(r * n_pieces // blocks, (r + 1) * n_pieces // blocks):
            x_copies[p].wait()
        g_copies[r].wait()
        here = slice(r * block, (r + 1) * block)
        pre = dot(x[here, :], w[:, : 2 * step])
        back = dot(g[here, :], w[:, 2 * step :])
        h, a, b = swish_backward(pre[:, :step], pre[:, step:], back)
        hid[here, :] = h
        merged[here, :step] = a
        merged[here, step:] = b

    for side in (1, 0):
        for k in range(line):
            cols = rows_of(owner(k, side))
            out = theirs.at[k] if side else mine[k]
            out[:, : 2 * step] = dot_tn(x[:, cols], merged[...]).astype(BF16)
            out[:, 2 * step :] = dot_tn(g[:, cols], hid[...]).astype(BF16)
    both[...] = w[:, : 2 * step]


def route_kernel(chunks, rows, *refs):
    merged, both = refs[:chunks], refs[chunks : 2 * chunks]
    far, odd, left, right = refs[2 * chunks :]
    width = far.shape[1]
    tile = width // 4

    def emit(out, blocks, first):
        @pl.loop(0, 4)
        def _(t):
            cols = pl.ds(pl.multiple_of(t * tile, tile), tile)
            for n, b in enumerate(blocks):
                here = slice(b * rows, (b + 1) * rows)
                total = None
                for m, w in zip(merged, both):
                    wide_cols = pl.ds(pl.multiple_of(first + t * tile, tile), tile)
                    part = dot_nt(m[here, :], w[wide_cols, :])
                    total = part if total is None else total + part
                out[n * rows : (n + 1) * rows, cols] = total.astype(out.dtype)

    emit(far, (2, 3), 0)
    emit(odd, (1, 3), width)
    emit(left, (0, 1), 0)
    emit(right, (0, 2), width)


def dense_plan(tokens, out_grad, routes, gate_prob, w_gate, w_up, w_down):
    experts = lax.axis_size("expert")
    wide = lax.axis_size("wide")
    line = wide // 2
    rows, width = tokens.shape
    feats = w_gate.shape[1]
    step = 2 * LANES
    chunks = w_gate.shape[2] // step
    count = experts * rows
    mine = lax.axis_index("expert")
    place = lax.axis_index("wide")
    z, c = place // 2, place % 2
    at = jnp.stack((z, c, mine)).astype(jnp.int32)
    shape = jax.ShapeDtypeStruct

    def after(a, *b):
        return lax.optimization_barrier((a, *b))[0]

    def twin(a):
        return lax.ppermute(a, "wide", [(i, i ^ 1) for i in range(wide)])

    def along(a, hops):
        return lax.ppermute(
            a, "wide", [(2 * s + i, 2 * t + i) for s, t in hops for i in range(2)]
        )

    def flip(a, bit):
        return lax.ppermute(a, "expert", [(e, e ^ bit) for e in range(experts)])

    own = call(
        lambda *r: pack_kernel(step, *r),
        [VMEM] * 3,
        [shape((feats, 3 * step), BF16)] * chunks,
        (w_gate[0], w_up[0], w_down[0]),
    )
    whole = [lax.all_gather(a, "wide", axis=0, tiled=True) for a in own[1:]]

    named = jnp.arange(experts, dtype=jnp.int32)[None, :]
    gates = sum(
        jnp.where(routes[:, k : k + 1] == named, gate_prob[:, k : k + 1], 0.0)
        for k in range(routes.shape[1])
    )
    high = lax.reduce_precision(gates, 8, 7)
    middle = lax.reduce_precision(gates - high, 8, 7)
    terms = jnp.concatenate((high, middle, gates - high - middle), axis=1).astype(BF16)
    terms = jnp.pad(terms, ((0, 0), (0, LANES - terms.shape[1])))
    graded = jnp.concatenate((out_grad, terms), axis=1)
    def hop(ups, downs, s):
        with jax.named_scope(f"gather_step_{s}"):
            ups.append(along(ups[-1], [(i, i + 1) for i in range(s - 1, line - 1)]))
            downs.append(along(downs[-1], [(i, i - 1) for i in range(1, line - s + 1)]))

    ups, downs = [own[0]], [own[0]]
    with jax.named_scope("rows"):
        t = [tokens, flip(tokens, 1), flip(tokens, 2)]
        g = [graded, flip(graded, 1), flip(graded, 2)]
    hop(ups, downs, 1)
    with jax.named_scope("rows"):
        near = (t[1], t[2], g[1], g[2], ups[1], downs[1])
        t.append(flip(after(t[1], *near), 2))
        g.append(flip(after(g[2], *near), 1))
    for s in range(2, line):
        hop(ups, downs, s)
    held = (own[0], *ups[1:], *downs[1:])
    held += tuple(twin(p) for p in held)
    g[0] = after(graded, ups[2], downs[2])
    [scaled] = call(
        lambda *r: scale_kernel(experts, *r),
        [SMEM] + [VMEM] * len(g),
        [shape((count, width), BF16)],
        (at, *g),
    )

    def scatter(parts, swapped, begin, last):
        def block(k, *more):
            total = parts[k].astype(F32)
            for m in (swapped[k], *more):
                total = total + m.astype(F32)
            return total.astype(BF16)

        with jax.named_scope("scatter_step_1"):
            a = jnp.where(z == 0, block(1), block(line - 1))
            up = down = along(after(a, *begin), [(0, 1), (line - 1, line - 2)])
            marks = [up]
        for s in range(2, line):
            if s == 2 and line == 4:
                a = b = block(2, up)
            elif s == 2:
                a = block(2, jnp.where(z == 1, up, 0))
                b = block(line - 2, jnp.where(z == line - 2, down, 0))
            else:
                a, b = block(s, up), block(line - s, down)
            if s == line - 1:
                a, b = after(a, *last), after(b, *last)
            with jax.named_scope(f"scatter_step_{s}"):
                up = along(a, [(i, i + 1) for i in range(s)])
                down = along(b, [(i, i - 1) for i in range(line - s, line)])
            marks += [a, up]
        total = parts[0].astype(F32) + swapped[0].astype(F32)
        return total + up.astype(F32) + down.astype(F32), marks

    order = [1, 0, *range(2, chunks)]
    merged, both, sums, marks = [], [], [], ()
    for i in range(chunks):
        weights = held if i == 1 else (whole[order[i] - 1],)
        got = call(
            lambda *r, i=i: chunk_kernel(line, len(t), i != 1, *r),
            [SMEM] + [HBM] * (len(t) + 1 + len(weights)),
            [shape((feats, 3 * step), BF16)] * line
            + [
                shape((line, feats, 3 * step), BF16),
                shape((count, 2 * step), BF16),
                shape((width, 2 * step), BF16),
            ],
            (at, *t, after(scaled, *marks[:2]), *weights),
            (
                pltpu.VMEM((count, width), BF16),
                pltpu.VMEM((count, width), BF16),
                pltpu.VMEM((width, 3 * step), BF16),
                pltpu.VMEM((count, step), BF16),
                pltpu.SemaphoreType.DMA((len(t),)),
                pltpu.SemaphoreType.DMA((2,)),
                pltpu.SemaphoreType.DMA((2 * line,)),
            ),
            flops=12 * count * width * step,
        )
        merged.append(got[line + 1])
        both.append(got[line + 2])
        swapped = twin(got[line])
        if i < chunks - 1:
            total, marks = scatter(got[:line], swapped, marks[2:3], ())
            sums.append(total)

    far, odd, left, right = call(
        lambda *r: route_kernel(chunks, rows, *r),
        [VMEM] * (2 * chunks),
        [shape((2 * rows, width // 2), BF16)] * 2 + [shape((2 * rows, width // 2), F32)] * 2,
        (*merged, *both),
        flops=4 * count * width * step * chunks,
    )
    with jax.named_scope("back"):
        far, odd = flip(far, 2), flip(odd, 1)
        left, right = left + far.astype(F32), right + odd.astype(F32)
        halfway = (left, right)
        near = flip(left[rows:].astype(BF16), 1)
        last = flip(right[rows:].astype(BF16), 2)
        left, right = left[:rows] + near.astype(F32), right[:rows] + last.astype(F32)
        grad_input = jnp.concatenate((left, right), axis=1).astype(BF16)
    sums.append(scatter(got[:line], swapped, marks[2:3], halfway)[0])

    def grad_of(j):
        cols = slice(j * step, (j + 1) * step)
        return jnp.concatenate([sums[order.index(i)][:, cols] for i in range(chunks)], axis=1)[None]

    return (grad_input, grad_of(0), grad_of(1), grad_of(2))


def solution(mesh):
    experts, wide = mesh.shape["expert"], mesh.shape["wide"]
    split = P(("expert", "wide"), None)
    weight = P("expert", "wide", None)

    def on_device(tokens, out_grad, routes, *rest):
        dense = experts == 4 and wide % 2 == 0 and 2 * routes.shape[1] >= experts
        dense = dense and wide > 4 and rest[1].shape[2] >= 4 * LANES and rest[1].shape[2] % (2 * LANES) == 0
        return (dense_plan if dense else slot_plan)(tokens, out_grad, routes, *rest)

    return jax.shard_map(
        on_device,
        mesh=mesh,
        in_specs=(split,) * 4 + (weight,) * 3,
        out_specs=(split, weight, weight, weight),
        check_vma=False,
    )
```

```python
import jax
import jax.numpy as jnp
from jax import lax
from jax.experimental import pallas as pl
from jax.experimental.pallas import tpu as pltpu
from jax.experimental import pallas as pl
from jax.experimental.pallas import tpu as pltpu
from jax.experimental import pallas as pl
from jax.experimental.pallas import tpu as pltpu
from jax.experimental import pallas as pl
from jax.experimental.pallas import tpu as pltpu
from jax.experimental import pallas as pl
from jax.experimental.pallas import tpu as pltpu
from jax.experimental import pallas as pl
from jax.experimental.pallas import tpu as pltpu
from jax.experimental import pallas as pl
from jax.experimental.pallas import tpu as pltpu
from jax.experimental import pallas as pl
from jax.experimental.pallas import tpu as pltpu
from jax.experimental import pallas as pl
from jax.experimental.pallas import tpu as pltpu
from jax.sharding import PartitionSpec as P

LANES = 128
F32 = jnp.float32
BF16 = jnp.bfloat16


def swish_backward(gate_pre, up_pre, hidden_grad):
    squash = jax.nn.sigmoid(gate_pre)
    active = gate_pre * squash
    hidden = (active * up_pre).astype(BF16)
    gate_act = (hidden_grad * up_pre * squash * (1.0 + gate_pre * (1.0 - squash))).astype(BF16)
    up_act = (hidden_grad * active).astype(BF16)
    return (hidden, gate_act, up_act)


def dot(a, b):
    return jnp.dot(a, b, preferred_element_type=F32)


def dot_tn(a, b):
    return lax.dot_general(a, b, (((0,), (0,)), ((), ())), preferred_element_type=F32)


def dot_nt(a, b):
    return lax.dot_general(a, b, (((1,), (1,)), ((), ())), preferred_element_type=F32)


def add(a, b):
    return (a.astype(F32) + b.astype(F32)).astype(BF16)


def slot_plan(tokens, out_grad, routes, gate_prob, w_gate, w_up, w_down):
    experts = lax.axis_size("expert")
    tok_count, top_count = routes.shape
    capacity = min(tok_count, 2 * tok_count * top_count // experts)
    slot_count = experts * capacity
    model_width = tokens.shape[1]
    hidden_units = w_gate.shape[2]
    flat_routes = routes.reshape(-1)
    order = jnp.arange(tok_count * top_count, dtype=jnp.int32)
    same = flat_routes[:, None] == flat_routes[None, :]
    before = jnp.sum((same & (order[None, :] < order[:, None])).astype(jnp.int32), axis=1)
    positions = flat_routes * capacity + before
    chosen = (positions[None, :] == jnp.arange(slot_count, dtype=jnp.int32)[:, None]).reshape(
        slot_count, tok_count, top_count
    )
    picker = jnp.sum(chosen.astype(F32), axis=2)
    slot_gate = jnp.sum(jnp.where(chosen, gate_prob[None, :, :], 0.0), axis=(1, 2))
    picker_half = picker.astype(BF16)
    sent_rows = dot(picker_half, tokens).astype(BF16)
    sent_grad = (dot(picker_half, out_grad) * slot_gate[:, None]).astype(BF16)

    def exchange(rows):
        return lax.all_to_all(
            rows.reshape(experts, capacity, model_width),
            "expert",
            split_axis=0,
            concat_axis=0,
            tiled=True,
        ).reshape(slot_count, model_width)

    rows_in = exchange(sent_rows)
    grad_in = exchange(sent_grad)
    full_gate, full_up, full_down = (
        lax.all_gather(w, "wide", axis=1, tiled=True)[0] for w in (w_gate, w_up, w_down)
    )
    hidden, gate_act, up_act = swish_backward(
        dot(rows_in, full_gate), dot(rows_in, full_up), dot(grad_in, full_down)
    )
    merged = jnp.concatenate((gate_act, up_act), axis=1)
    input_grad = dot_nt(merged, jnp.concatenate((full_gate, full_up), axis=1)).astype(BF16)
    parts = jnp.concatenate((dot_tn(rows_in, merged), dot_tn(grad_in, hidden)), axis=1)
    summed = lax.psum_scatter(
        parts.astype(BF16), "wide", scatter_dimension=0, tiled=True
    ).astype(F32)
    grads = tuple(
        summed[:, i * hidden_units : (i + 1) * hidden_units][None] for i in range(3)
    )
    grad_input = dot_tn(picker_half, exchange(input_grad)).astype(BF16)
    return (grad_input,) + grads


VMEM = pl.BlockSpec(memory_space=pltpu.VMEM)
SMEM = pl.BlockSpec(memory_space=pltpu.SMEM)
HBM = pl.BlockSpec(memory_space=pltpu.HBM)
LIMIT = 58 << 20


def call(body, ins, outs, operands, scratch=(), flops=0, limit=LIMIT):
    moved = sum(a.size * a.dtype.itemsize for a in (*operands, *outs))
    return pl.pallas_call(
        body,
        out_shape=outs,
        in_specs=ins,
        out_specs=[VMEM] * len(outs),
        scratch_shapes=list(scratch),
        cost_estimate=pl.CostEstimate(flops=flops, bytes_accessed=moved, transcendentals=0),
        compiler_params=pltpu.CompilerParams(vmem_limit_bytes=limit),
    )(*operands)


def pack_kernel(step, first, gate, up, down, *outs):
    for i, out in enumerate(outs):
        cols = slice((first + i) * step, (first + i + 1) * step)
        for m, ref in enumerate((gate, up, down)):
            out[:, m * step : (m + 1) * step] = ref[:, cols]


def scale_kernel(experts, at, *refs):
    pieces, out = refs[:-1], refs[-1]
    rows, width = pieces[0].shape[0], out.shape[1]
    lane = lax.broadcasted_iota(jnp.int32, (rows, LANES), 1)
    ours = (lax.rem(lane, experts) == at[2]) & (lane < 3 * experts)
    for p, ref in enumerate(pieces):
        terms = jnp.where(ours, ref[:, width:].astype(F32), 0.0)
        gate = jnp.sum(terms, axis=1, keepdims=True)
        out[p * rows : (p + 1) * rows, :] = (gate * ref[:, :width].astype(F32)).astype(BF16)


def chunk_kernel(line, n_pieces, at, *refs):
    pieces, refs = refs[:n_pieces], refs[n_pieces:]
    scaled, weights, refs = refs[0], refs[1], refs[2:]
    mine, theirs, merged, both = refs[:line], refs[line], refs[line + 1], refs[line + 2]
    x, g, w, hid, xsem, gsem, wsem = refs[line + 3 :]
    z, c = at[0], at[1]
    feats = w.shape[0] // (2 * line)
    step = w.shape[1] // 3
    rows = x.shape[0] // n_pieces
    parts = 2 * line
    blocks = 2
    block = x.shape[0] // blocks

    def rows_of(f):
        return pl.ds(pl.multiple_of(f * feats, feats), feats)

    def owner(k, side):
        return lax.rem(z - k + line, line) * 2 + (c if side == 0 else 1 - c)

    for f in range(parts):
        here = pl.ds(f * feats, feats)
        pltpu.make_async_copy(weights.at[here, :], w.at[here, :], wsem.at[f]).start()
    x_copies = [
        pltpu.make_async_copy(ref, x.at[pl.ds(p * rows, rows), :], xsem.at[p])
        for p, ref in enumerate(pieces)
    ]
    g_copies = []
    for r in range(blocks):
        here = pl.ds(r * block, block)
        g_copies.append(pltpu.make_async_copy(scaled.at[here, :], g.at[here, :], gsem.at[r]))
    for r in range(blocks):
        for p in range(r * n_pieces // blocks, (r + 1) * n_pieces // blocks):
            x_copies[p].start()
        g_copies[r].start()
    for f in range(parts):
        part = w.at[pl.ds(f * feats, feats), :]
        pltpu.make_async_copy(part, part, wsem.at[f]).wait()

    for r in range(blocks):
        for p in range(r * n_pieces // blocks, (r + 1) * n_pieces // blocks):
            x_copies[p].wait()
        g_copies[r].wait()
        here = slice(r * block, (r + 1) * block)
        pre = dot(x[here, :], w[:, : 2 * step])
        back = dot(g[here, :], w[:, 2 * step :])
        h, a, b = swish_backward(pre[:, :step], pre[:, step:], back)
        hid[here, :] = h
        merged[here, :step] = a
        merged[here, step:] = b

    for side in (1, 0):
        for k in range(line):
            cols = rows_of(owner(k, side))
            out = theirs.at[k] if side else mine[k]
            out[:, : 2 * step] = dot_tn(x[:, cols], merged[...]).astype(BF16)
            out[:, 2 * step :] = dot_tn(g[:, cols], hid[...]).astype(BF16)
    both[...] = w[:, : 2 * step]


def route_kernel(chunks, rows, *refs):
    merged, both = refs[:chunks], refs[chunks : 2 * chunks]
    far, odd, left, right = refs[2 * chunks :]
    width = far.shape[1]
    tile = width // 4

    @pl.loop(0, 8)
    def _(t):
        cols = pl.ds(pl.multiple_of(t * tile, tile), tile)
        total = None
        for m, w in zip(merged, both):
            part = dot_nt(m[...], w[cols, :])
            total = part if total is None else total + part
        blocks = [total[b * rows : (b + 1) * rows] for b in range(4)]

        def emit(out, at, a, b):
            here = pl.ds(pl.multiple_of(at * tile, tile), tile)
            out[:rows, here] = blocks[a].astype(out.dtype)
            out[rows:, here] = blocks[b].astype(out.dtype)

        @pl.when(t < 4)
        def _():
            emit(far, t, 2, 3)
            emit(left, t, 0, 1)

        @pl.when(t >= 4)
        def _():
            emit(odd, t - 4, 1, 3)
            emit(right, t - 4, 0, 2)


def dense_plan(tokens, out_grad, routes, gate_prob, w_gate, w_up, w_down):
    experts = lax.axis_size("expert")
    wide = lax.axis_size("wide")
    line = wide // 2
    rows, width = tokens.shape
    feats = w_gate.shape[1]
    step = 2 * LANES
    chunks = w_gate.shape[2] // step
    count = experts * rows
    mine = lax.axis_index("expert")
    place = lax.axis_index("wide")
    z, c = place // 2, place % 2
    at = jnp.stack((z, c, mine)).astype(jnp.int32)
    shape = jax.ShapeDtypeStruct

    def after(a, *b):
        return lax.optimization_barrier((a, *b))[0]

    def twin(a):
        return lax.ppermute(a, "wide", [(i, i ^ 1) for i in range(wide)])

    def along(a, hops):
        return lax.ppermute(
            a, "wide", [(2 * s + i, 2 * t + i) for s, t in hops for i in range(2)]
        )

    def flip(a, bit):
        return lax.ppermute(a, "expert", [(e, e ^ bit) for e in range(experts)])

    own = call(
        lambda *r: pack_kernel(step, 0, *r),
        [VMEM] * 3,
        [shape((feats, 3 * step), BF16)] * chunks,
        (w_gate[0], w_up[0], w_down[0]),
    )
    whole = [lax.all_gather(a, "wide", axis=0, tiled=True) for a in own]

    named = jnp.arange(experts, dtype=jnp.int32)[None, :]
    gates = sum(
        jnp.where(routes[:, k : k + 1] == named, gate_prob[:, k : k + 1], 0.0)
        for k in range(routes.shape[1])
    )
    high = lax.reduce_precision(gates, 8, 7)
    middle = lax.reduce_precision(gates - high, 8, 7)
    terms = jnp.concatenate((high, middle, gates - high - middle), axis=1).astype(BF16)
    terms = jnp.pad(terms, ((0, 0), (0, LANES - terms.shape[1])))
    graded = jnp.concatenate((out_grad, terms), axis=1)
    with jax.named_scope("rows"):
        t = [tokens, flip(tokens, 1), flip(tokens, 2)]
        g = [graded, flip(graded, 1), flip(graded, 2)]
        near = (t[1], t[2], g[1], g[2])
        t.append(flip(after(t[1], *near), 2))
        g.append(flip(after(g[2], *near), 1))
    [scaled] = call(
        lambda *r: scale_kernel(experts, *r),
        [SMEM] + [VMEM] * len(g),
        [shape((count, width), BF16)],
        (at, *g),
    )

    def scatter(parts, swapped, begin, last):
        def block(k, *more):
            total = parts[k].astype(F32)
            for m in (swapped[k], *more):
                total = total + m.astype(F32)
            return total.astype(BF16)

        with jax.named_scope("scatter_step_1"):
            a = jnp.where(z == 0, block(1), block(line - 1))
            up = down = along(after(a, *begin), [(0, 1), (line - 1, line - 2)])
            marks = [up]
        for s in range(2, line):
            if s == 2 and line == 4:
                a = b = block(2, up)
            elif s == 2:
                a = block(2, jnp.where(z == 1, up, 0))
                b = block(line - 2, jnp.where(z == line - 2, down, 0))
            else:
                a, b = block(s, up), block(line - s, down)
            if s == line - 1:
                a, b = after(a, *last), after(b, *last)
            with jax.named_scope(f"scatter_step_{s}"):
                up = along(a, [(i, i + 1) for i in range(s)])
                down = along(b, [(i, i - 1) for i in range(line - s, line)])
            marks += [a, b, up, down]
        total = parts[0].astype(F32) + swapped[0].astype(F32)
        return total + up.astype(F32) + down.astype(F32), marks

    merged, both, sums, marks, tie = [], [], [], (), ()
    for i in range(chunks):
        got = call(
            lambda *r: chunk_kernel(line, len(t), *r),
            [SMEM] + [HBM] * (len(t) + 2),
            [shape((feats, 3 * step), BF16)] * line
            + [
                shape((line, feats, 3 * step), BF16),
                shape((count, 2 * step), BF16),
                shape((width, 2 * step), BF16),
            ],
            (at, *t, after(scaled, *tie), whole[i]),
            (
                pltpu.VMEM((count, width), BF16),
                pltpu.VMEM((count, width), BF16),
                pltpu.VMEM((width, 3 * step), BF16),
                pltpu.VMEM((count, step), BF16),
                pltpu.SemaphoreType.DMA((len(t),)),
                pltpu.SemaphoreType.DMA((2,)),
                pltpu.SemaphoreType.DMA((2 * line,)),
            ),
            flops=12 * count * width * step,
        )
        merged.append(got[line + 1])
        both.append(got[line + 2])
        swapped = twin(got[line])
        if i < chunks - 1:
            total, marks = scatter(got[:line], swapped, marks[3:5], ())
            tie = marks[: 3 if i == 0 else 5]
            sums.append(total)

    far, odd, left, right = call(
        lambda *r: route_kernel(chunks, rows, *r),
        [VMEM] * (2 * chunks),
        [shape((2 * rows, width // 2), BF16)] * 2 + [shape((2 * rows, width // 2), F32)] * 2,
        (*merged, *both),
        flops=4 * count * width * step * chunks,
    )
    with jax.named_scope("back"):
        far, odd = flip(far, 2), flip(odd, 1)
        left, right = left + far.astype(F32), right + odd.astype(F32)
        halfway = (left, right)
        near = flip(left[rows:].astype(BF16), 1)
        last = flip(right[rows:].astype(BF16), 2)
        left, right = left[:rows] + near.astype(F32), right[:rows] + last.astype(F32)
        grad_input = jnp.concatenate((left, right), axis=1).astype(BF16)
    sums.append(scatter(got[:line], swapped, marks[3:5], halfway)[0])

    def grad_of(j):
        cols = slice(j * step, (j + 1) * step)
        return jnp.concatenate([a[:, cols] for a in sums], axis=1)[None]

    return (grad_input, grad_of(0), grad_of(1), grad_of(2))


def solution(mesh):
    experts, wide = mesh.shape["expert"], mesh.shape["wide"]
    split = P(("expert", "wide"), None)
    weight = P("expert", "wide", None)

    def on_device(tokens, out_grad, routes, *rest):
        dense = experts == 4 and wide % 2 == 0 and 2 * routes.shape[1] >= experts
        dense = dense and wide > 4 and rest[1].shape[2] >= 4 * LANES and rest[1].shape[2] % (2 * LANES) == 0
        return (dense_plan if dense else slot_plan)(tokens, out_grad, routes, *rest)

    return jax.shard_map(
        on_device,
        mesh=mesh,
        in_specs=(split,) * 4 + (weight,) * 3,
        out_specs=(split, weight, weight, weight),
        check_vma=False,
    )
```

```python
import jax
import jax.numpy as jnp
from jax import lax
from jax.experimental import pallas as pl
from jax.experimental.pallas import tpu as pltpu
from jax.experimental import pallas as pl
from jax.experimental.pallas import tpu as pltpu
from jax.sharding import PartitionSpec as P

LANES = 128
F32 = jnp.float32
BF16 = jnp.bfloat16


def swish_backward(gate_pre, up_pre, hidden_grad):
    squash = jax.nn.sigmoid(gate_pre)
    active = gate_pre * squash
    hidden = (active * up_pre).astype(BF16)
    gate_act = (hidden_grad * up_pre * squash * (1.0 + gate_pre * (1.0 - squash))).astype(BF16)
    up_act = (hidden_grad * active).astype(BF16)
    return (hidden, gate_act, up_act)


def dot(a, b):
    return jnp.dot(a, b, preferred_element_type=F32)


def dot_tn(a, b):
    return lax.dot_general(a, b, (((0,), (0,)), ((), ())), preferred_element_type=F32)


def dot_nt(a, b):
    return lax.dot_general(a, b, (((1,), (1,)), ((), ())), preferred_element_type=F32)


def add(a, b):
    return (a.astype(F32) + b.astype(F32)).astype(BF16)


def slot_plan(tokens, out_grad, routes, gate_prob, w_gate, w_up, w_down):
    experts = lax.axis_size("expert")
    tok_count, top_count = routes.shape
    capacity = min(tok_count, 2 * tok_count * top_count // experts)
    slot_count = experts * capacity
    model_width = tokens.shape[1]
    hidden_units = w_gate.shape[2]
    flat_routes = routes.reshape(-1)
    order = jnp.arange(tok_count * top_count, dtype=jnp.int32)
    same = flat_routes[:, None] == flat_routes[None, :]
    before = jnp.sum((same & (order[None, :] < order[:, None])).astype(jnp.int32), axis=1)
    positions = flat_routes * capacity + before
    chosen = (positions[None, :] == jnp.arange(slot_count, dtype=jnp.int32)[:, None]).reshape(
        slot_count, tok_count, top_count
    )
    picker = jnp.sum(chosen.astype(F32), axis=2)
    slot_gate = jnp.sum(jnp.where(chosen, gate_prob[None, :, :], 0.0), axis=(1, 2))
    picker_half = picker.astype(BF16)
    sent_rows = dot(picker_half, tokens).astype(BF16)
    sent_grad = (dot(picker_half, out_grad) * slot_gate[:, None]).astype(BF16)

    def exchange(rows):
        return lax.all_to_all(
            rows.reshape(experts, capacity, model_width),
            "expert",
            split_axis=0,
            concat_axis=0,
            tiled=True,
        ).reshape(slot_count, model_width)

    rows_in = exchange(sent_rows)
    grad_in = exchange(sent_grad)
    full_gate, full_up, full_down = (
        lax.all_gather(w, "wide", axis=1, tiled=True)[0] for w in (w_gate, w_up, w_down)
    )
    hidden, gate_act, up_act = swish_backward(
        dot(rows_in, full_gate), dot(rows_in, full_up), dot(grad_in, full_down)
    )
    merged = jnp.concatenate((gate_act, up_act), axis=1)
    input_grad = dot_nt(merged, jnp.concatenate((full_gate, full_up), axis=1)).astype(BF16)
    parts = jnp.concatenate((dot_tn(rows_in, merged), dot_tn(grad_in, hidden)), axis=1)
    summed = lax.psum_scatter(
        parts.astype(BF16), "wide", scatter_dimension=0, tiled=True
    ).astype(F32)
    grads = tuple(
        summed[:, i * hidden_units : (i + 1) * hidden_units][None] for i in range(3)
    )
    grad_input = dot_tn(picker_half, exchange(input_grad)).astype(BF16)
    return (grad_input,) + grads


VMEM = pl.BlockSpec(memory_space=pltpu.VMEM)
SMEM = pl.BlockSpec(memory_space=pltpu.SMEM)
ANY = pl.BlockSpec(memory_space=pl.ANY)
LIMIT = 40 << 20


def call(body, ins, outs, operands, scratch=(), flops=0, limit=LIMIT):
    moved = sum(a.size * a.dtype.itemsize for a in operands)
    moved += sum(o.size * o.dtype.itemsize for o in outs)
    return pl.pallas_call(
        body,
        out_shape=outs,
        in_specs=ins,
        out_specs=[VMEM] * len(outs),
        scratch_shapes=list(scratch),
        cost_estimate=pl.CostEstimate(flops=flops, bytes_accessed=moved, transcendentals=0),
        compiler_params=pltpu.CompilerParams(vmem_limit_bytes=limit),
    )(*operands)


def half_of(ref, side, half, i, step):
    return ref[:, pl.ds(pl.multiple_of(side * half + i * step, step), step)]


def pack_kernel(chunks, step, at, gate, up, down, *outs):
    half = chunks * step
    c = at[1]
    for side, group in ((c, outs[:chunks]), (1 - c, outs[chunks:])):
        for i, out in enumerate(group):
            for m, ref in enumerate((gate, up, down)):
                out[:, m * step : (m + 1) * step] = half_of(ref, side, half, i, step)


def combine_kernel(chunks, at, *refs):
    kept, given, outs = refs[:chunks], refs[chunks : 2 * chunks], refs[2 * chunks :]
    feats = kept[0].shape[0]
    c = at[1]
    for a, b, out in zip(kept, given, outs):
        out[pl.ds(pl.multiple_of(c * feats, feats), feats), :] = a[...]
        out[pl.ds(pl.multiple_of((1 - c) * feats, feats), feats), :] = b[...]


def scale_kernel(experts, at, *refs):
    pieces, out = refs[:-1], refs[-1]
    rows, width = pieces[0].shape[0], out.shape[1]
    lane = lax.broadcasted_iota(jnp.int32, (rows, LANES), 1)
    ours = (lax.rem(lane, experts) == at[2]) & (lane < 3 * experts)
    for p, ref in enumerate(pieces):
        terms = jnp.where(ours, ref[:, width:].astype(F32), 0.0)
        gate = jnp.sum(terms, axis=1, keepdims=True)
        out[p * rows : (p + 1) * rows, :] = (gate * ref[:, :width].astype(F32)).astype(BF16)


def chunk_kernel(line, n_pieces, at, *refs):
    pieces, refs = refs[:n_pieces], refs[n_pieces:]
    scaled, own = refs[0], refs[1]
    ups, downs = refs[2 : 1 + line], refs[1 + line : 2 * line]
    outs = refs[2 * line : 2 * line + line + 2]
    parts, merged, both = outs[:line], outs[line], outs[line + 1]
    x, g, w, hid, xsem, gsem, wsem = refs[2 * line + line + 2 :]
    z = at[0]
    depth, step = own.shape[0], own.shape[1] // 3
    rows = x.shape[0] // n_pieces
    block = x.shape[0] // 4

    def shard(k):
        f = lax.rem(z - k + line, line)
        return w.at[pl.ds(pl.multiple_of(f * depth, depth), depth), :]

    pltpu.make_async_copy(own, shard(0), wsem.at[0]).start()
    for k in range(1, line):

        @pl.when(z >= k)
        def _(k=k):
            pltpu.make_async_copy(ups[k - 1], shard(k), wsem.at[k]).start()

        @pl.when(z < k)
        def _(k=k):
            pltpu.make_async_copy(downs[line - k - 1], shard(k), wsem.at[k]).start()

    x_copies = [
        pltpu.make_async_copy(ref, x.at[pl.ds(p * rows, rows), :], xsem.at[p])
        for p, ref in enumerate(pieces)
    ]
    g_copies = [
        pltpu.make_async_copy(
            scaled.at[pl.ds(r * block, block), :], g.at[pl.ds(r * block, block), :], gsem.at[r]
        )
        for r in range(4)
    ]
    for r in range(4):
        for p in range(r * n_pieces // 4, (r + 1) * n_pieces // 4):
            x_copies[p].start()
        g_copies[r].start()
    for k in range(line):
        pltpu.make_async_copy(own, shard(k), wsem.at[k]).wait()

    for r in range(4):
        for p in range(r * n_pieces // 4, (r + 1) * n_pieces // 4):
            x_copies[p].wait()
        g_copies[r].wait()
        here = slice(r * block, (r + 1) * block)
        pre = dot(x[here, :], w[:, : 2 * step])
        back = dot(g[here, :], w[:, 2 * step :])
        h, a, b = swish_backward(pre[:, :step], pre[:, step:], back)
        hid[here, :] = h
        merged[here, :step] = a
        merged[here, step:] = b

    for k in range(line):
        f = lax.rem(z - k + line, line)
        cols = pl.ds(pl.multiple_of(f * depth, depth), depth)
        parts[k][:, : 2 * step] = dot_tn(x[:, cols], merged[...]).astype(BF16)
        parts[k][:, 2 * step :] = dot_tn(g[:, cols], hid[...]).astype(BF16)
    both[...] = w[:, : 2 * step]


def route_kernel(chunks, *refs):
    merged, both = refs[:chunks], refs[chunks : 2 * chunks]
    keep, give = refs[2 * chunks :]
    rows, width = keep.shape
    tile = width // 8

    for out, first in ((give, rows), (keep, 0)):

        @pl.loop(0, 8)
        def _(t, out=out, first=first):
            cols = pl.ds(pl.multiple_of(t * tile, tile), tile)
            total = None
            for m, b in zip(merged, both):
                part = dot_nt(m[first : first + rows, :], b[cols, :])
                total = part if total is None else total + part
            out[:, cols] = total.astype(BF16)


def dense_plan(tokens, out_grad, routes, gate_prob, w_gate, w_up, w_down):
    experts = lax.axis_size("expert")
    wide = lax.axis_size("wide")
    line = wide // 2
    rows, width = tokens.shape
    feats = w_gate.shape[1]
    half = w_gate.shape[2] // 2
    step = LANES
    chunks = half // step
    mine = lax.axis_index("expert")
    place = lax.axis_index("wide")
    z, c = place // 2, place % 2
    at = jnp.stack((z, c, mine)).astype(jnp.int32)
    shape = jax.ShapeDtypeStruct

    def after(a, *b):
        return lax.optimization_barrier((a, *b))[0]

    def twin(a):
        return lax.ppermute(a, "wide", [(i, i ^ 1) for i in range(wide)])

    def along(a, hops):
        return lax.ppermute(
            a, "wide", [(2 * s + i, 2 * t + i) for s, t in hops for i in range(2)]
        )

    def flip(a, bit):
        return lax.ppermute(a, "expert", [(e, e ^ bit) for e in range(experts)])

    cut = [shape((feats, 3 * step), BF16)] * (2 * chunks)
    packed = call(
        lambda *r: pack_kernel(chunks, step, *r),
        [SMEM] + [VMEM] * 3,
        cut,
        (at, w_gate[0], w_up[0], w_down[0]),
    )
    given = [twin(a) for a in packed[chunks:]]
    shards = call(
        lambda *r: combine_kernel(chunks, *r),
        [SMEM] + [VMEM] * (2 * chunks),
        [shape((2 * feats, 3 * step), BF16)] * chunks,
        (at, *packed[:chunks], *given),
    )

    named = jnp.arange(experts, dtype=jnp.int32)[None, :]
    gates = sum(
        jnp.where(routes[:, k : k + 1] == named, gate_prob[:, k : k + 1], 0.0)
        for k in range(routes.shape[1])
    )
    high = lax.reduce_precision(gates, 8, 7)
    middle = lax.reduce_precision(gates - high, 8, 7)
    terms = jnp.concatenate((high, middle, gates - high - middle), axis=1).astype(BF16)
    terms = jnp.pad(terms, ((0, 0), (0, LANES - terms.shape[1])))
    graded = jnp.concatenate((out_grad, terms), axis=1)

    with jax.named_scope("rows"):
        t = [tokens, *(after(flip(tokens, bit), *shards) for bit in (1, 2))]
        g = [graded, *(after(flip(graded, bit), *shards) for bit in (1, 2))]
        t.append(flip(t[1], 2))
        g.append(flip(g[2], 1))
        t += [twin(a) for a in t]
        g += [twin(a) for a in g]
    count = len(t) * rows
    [scaled] = call(
        lambda *r: scale_kernel(experts, *r),
        [SMEM] + [VMEM] * len(g),
        [shape((count, width), BF16)],
        (at, *g),
    )

    def gather(own):
        ups, downs = [own], [own]
        for s in range(1, line):
            with jax.named_scope(f"gather_step_{s}"):
                ups.append(along(ups[-1], [(i, i + 1) for i in range(s - 1, line - 1)]))
                downs.append(along(downs[-1], [(i, i - 1) for i in range(1, line - s + 1)]))
        return (own, *ups[1:], *downs[1:])

    def scatter(parts, waits):
        with jax.named_scope("scatter_step_1"):
            a = jnp.where(z == 0, parts[1], parts[line - 1])
            up = down = along(a, [(0, 1), (line - 1, line - 2)])
        for s in range(2, line):
            if s == 2 and line == 4:
                a = b = add(parts[2], up)
            elif s == 2:
                a = add(parts[2], jnp.where(z == 1, up, 0))
                b = add(parts[line - 2], jnp.where(z == line - 2, down, 0))
            else:
                a, b = add(parts[s], up), add(parts[line - s], down)
            a, b = after(a, *waits[s - 2]), after(b, *waits[s - 2])
            with jax.named_scope(f"scatter_step_{s}"):
                up = along(a, [(i, i + 1) for i in range(s)])
                down = along(b, [(i, i - 1) for i in range(line - s, line)])
        return parts[0].astype(F32) + up.astype(F32) + down.astype(F32)

    merged, both, parts = [], [], []
    for i in range(chunks):
        loaded = gather(shards[i])
        got = call(
            lambda *r: chunk_kernel(line, len(t), *r),
            [SMEM] + [ANY] * (len(t) + 2 * line),
            [shape((2 * feats, 3 * step), BF16)] * line
            + [shape((count, 2 * step), BF16), shape((width, 2 * step), BF16)],
            (at, *t, scaled, *loaded),
            (
                pltpu.VMEM((count, width), BF16),
                pltpu.VMEM((count, width), BF16),
                pltpu.VMEM((width, 3 * step), BF16),
                pltpu.VMEM((count, step), BF16),
                pltpu.SemaphoreType.DMA((len(t),)),
                pltpu.SemaphoreType.DMA((4,)),
                pltpu.SemaphoreType.DMA((line,)),
            ),
            flops=12 * count * width * step,
        )
        merged.append(got[line])
        both.append(got[line + 1])
        parts.append(got[:line])

    block = experts * rows
    keep, give = call(
        lambda *r: route_kernel(chunks, *r),
        [VMEM] * (2 * chunks),
        [shape((block, width), BF16)] * 2,
        (*merged, *both),
        flops=4 * count * width * step * chunks,
    )
    with jax.named_scope("back"):
        other = twin(give)
        ret = keep.astype(F32) + other.astype(F32)
        ret = ret.reshape(experts, rows, width)
        left, right = ret[:, :, : width // 2], ret[:, :, width // 2 :]
        far = flip(left[2:].astype(BF16), 2)
        odd = flip(jnp.stack((right[1], right[3])).astype(BF16), 1)
        left = left[:2] + far.astype(F32)
        near = flip(left[1].astype(BF16), 1)
        last = flip((right[2] + odd[1].astype(F32)).astype(BF16), 2)
        left = left[0] + near.astype(F32)
        right = right[0] + odd[0].astype(F32) + last.astype(F32)
        grad_input = jnp.concatenate((left, right), axis=1).astype(BF16)
    sums = [scatter(p, ((other,), *(((odd, far),) * (line - 3)))) for p in parts]

    own = [lax.dynamic_slice_in_dim(s, c * feats, feats, 0) for s in sums]
    other = [twin(lax.dynamic_slice_in_dim(s, (1 - c) * feats, feats, 0)) for s in sums]

    def grad_of(j):
        cols = slice(j * step, (j + 1) * step)
        a = jnp.concatenate([s[:, cols] for s in own], axis=1)
        b = jnp.concatenate([s[:, cols] for s in other], axis=1)
        first = jnp.concatenate((a, b), axis=1)
        return jnp.where(c == 0, first, jnp.concatenate((b, a), axis=1))[None]

    return (grad_input, grad_of(0), grad_of(1), grad_of(2))


def solution(mesh):
    experts, wide = mesh.shape["expert"], mesh.shape["wide"]
    split = P(("expert", "wide"), None)
    weight = P("expert", "wide", None)

    def on_device(tokens, out_grad, routes, *rest):
        dense = experts == 4 and wide % 2 == 0 and wide > 4 and 2 * routes.shape[1] >= experts
        dense = dense and rest[1].shape[2] % (2 * LANES) == 0
        return (dense_plan if dense else slot_plan)(tokens, out_grad, routes, *rest)

    return jax.shard_map(
        on_device,
        mesh=mesh,
        in_specs=(split,) * 4 + (weight,) * 3,
        out_specs=(split, weight, weight, weight),
        check_vma=False,
    )
```

```python
import jax
import jax.numpy as jnp
from jax import lax
from jax.experimental import pallas as pl
from jax.experimental.pallas import tpu as pltpu
from jax.experimental import pallas as pl
from jax.experimental.pallas import tpu as pltpu
from jax.sharding import PartitionSpec as P

LANES = 128
F32 = jnp.float32
BF16 = jnp.bfloat16


def swish_backward(gate_pre, up_pre, hidden_grad):
    squash = jax.nn.sigmoid(gate_pre)
    active = gate_pre * squash
    hidden = (active * up_pre).astype(BF16)
    gate_act = (hidden_grad * up_pre * squash * (1.0 + gate_pre * (1.0 - squash))).astype(BF16)
    up_act = (hidden_grad * active).astype(BF16)
    return (hidden, gate_act, up_act)


def dot(a, b):
    return jnp.dot(a, b, preferred_element_type=F32)


def dot_tn(a, b):
    return lax.dot_general(a, b, (((0,), (0,)), ((), ())), preferred_element_type=F32)


def dot_nt(a, b):
    return lax.dot_general(a, b, (((1,), (1,)), ((), ())), preferred_element_type=F32)


def add(a, b):
    return (a.astype(F32) + b.astype(F32)).astype(BF16)


def slot_plan(tokens, out_grad, routes, gate_prob, w_gate, w_up, w_down):
    experts = lax.axis_size("expert")
    tok_count, top_count = routes.shape
    capacity = min(tok_count, 2 * tok_count * top_count // experts)
    slot_count = experts * capacity
    model_width = tokens.shape[1]
    hidden_units = w_gate.shape[2]
    flat_routes = routes.reshape(-1)
    order = jnp.arange(tok_count * top_count, dtype=jnp.int32)
    same = flat_routes[:, None] == flat_routes[None, :]
    before = jnp.sum((same & (order[None, :] < order[:, None])).astype(jnp.int32), axis=1)
    positions = flat_routes * capacity + before
    chosen = (positions[None, :] == jnp.arange(slot_count, dtype=jnp.int32)[:, None]).reshape(
        slot_count, tok_count, top_count
    )
    picker = jnp.sum(chosen.astype(F32), axis=2)
    slot_gate = jnp.sum(jnp.where(chosen, gate_prob[None, :, :], 0.0), axis=(1, 2))
    picker_half = picker.astype(BF16)
    sent_rows = dot(picker_half, tokens).astype(BF16)
    sent_grad = (dot(picker_half, out_grad) * slot_gate[:, None]).astype(BF16)

    def exchange(rows):
        return lax.all_to_all(
            rows.reshape(experts, capacity, model_width),
            "expert",
            split_axis=0,
            concat_axis=0,
            tiled=True,
        ).reshape(slot_count, model_width)

    rows_in = exchange(sent_rows)
    grad_in = exchange(sent_grad)
    full_gate, full_up, full_down = (
        lax.all_gather(w, "wide", axis=1, tiled=True)[0] for w in (w_gate, w_up, w_down)
    )
    hidden, gate_act, up_act = swish_backward(
        dot(rows_in, full_gate), dot(rows_in, full_up), dot(grad_in, full_down)
    )
    merged = jnp.concatenate((gate_act, up_act), axis=1)
    input_grad = dot_nt(merged, jnp.concatenate((full_gate, full_up), axis=1)).astype(BF16)
    parts = jnp.concatenate((dot_tn(rows_in, merged), dot_tn(grad_in, hidden)), axis=1)
    summed = lax.psum_scatter(
        parts.astype(BF16), "wide", scatter_dimension=0, tiled=True
    ).astype(F32)
    grads = tuple(
        summed[:, i * hidden_units : (i + 1) * hidden_units][None] for i in range(3)
    )
    grad_input = dot_tn(picker_half, exchange(input_grad)).astype(BF16)
    return (grad_input,) + grads


VMEM = pl.BlockSpec(memory_space=pltpu.VMEM)
SMEM = pl.BlockSpec(memory_space=pltpu.SMEM)
ANY = pl.BlockSpec(memory_space=pl.ANY)
LIMIT = 40 << 20


def call(body, ins, outs, operands, scratch=(), flops=0, limit=LIMIT):
    moved = sum(a.size * a.dtype.itemsize for a in operands)
    moved += sum(o.size * o.dtype.itemsize for o in outs)
    return pl.pallas_call(
        body,
        out_shape=outs,
        in_specs=ins,
        out_specs=[VMEM] * len(outs),
        scratch_shapes=list(scratch),
        cost_estimate=pl.CostEstimate(flops=flops, bytes_accessed=moved, transcendentals=0),
        compiler_params=pltpu.CompilerParams(vmem_limit_bytes=limit),
    )(*operands)


def half_of(ref, side, half, i, step):
    return ref[:, pl.ds(pl.multiple_of(side * half + i * step, step), step)]


def pack_kernel(chunks, step, at, gate, up, down, *outs):
    half = chunks * step
    c = at[1]
    for side, group in ((c, outs[:chunks]), (1 - c, outs[chunks:])):
        for i, out in enumerate(group):
            for m, ref in enumerate((gate, up, down)):
                out[:, m * step : (m + 1) * step] = half_of(ref, side, half, i, step)


def combine_kernel(chunks, at, *refs):
    kept, given, outs = refs[:chunks], refs[chunks : 2 * chunks], refs[2 * chunks :]
    feats = kept[0].shape[0]
    c = at[1]
    for a, b, out in zip(kept, given, outs):
        out[pl.ds(pl.multiple_of(c * feats, feats), feats), :] = a[...]
        out[pl.ds(pl.multiple_of((1 - c) * feats, feats), feats), :] = b[...]


def scale_kernel(experts, at, *refs):
    pieces, out = refs[:-1], refs[-1]
    rows, width = pieces[0].shape[0], out.shape[1]
    lane = lax.broadcasted_iota(jnp.int32, (rows, LANES), 1)
    ours = (lax.rem(lane, experts) == at[2]) & (lane < 3 * experts)
    for p, ref in enumerate(pieces):
        terms = jnp.where(ours, ref[:, width:].astype(F32), 0.0)
        gate = jnp.sum(terms, axis=1, keepdims=True)
        out[p * rows : (p + 1) * rows, :] = (gate * ref[:, :width].astype(F32)).astype(BF16)


def chunk_kernel(line, n_pieces, at, *refs):
    pieces, refs = refs[:n_pieces], refs[n_pieces:]
    scaled, own = refs[0], refs[1]
    ups, downs = refs[2 : 1 + line], refs[1 + line : 2 * line]
    outs = refs[2 * line : 2 * line + line + 2]
    parts, merged, both = outs[:line], outs[line], outs[line + 1]
    x, g, w, hid, xsem, gsem, wsem = refs[2 * line + line + 2 :]
    z = at[0]
    depth, step = own.shape[0], own.shape[1] // 3
    rows = x.shape[0] // n_pieces
    block = x.shape[0] // 4

    def shard(k):
        f = lax.rem(z - k + line, line)
        return w.at[pl.ds(pl.multiple_of(f * depth, depth), depth), :]

    pltpu.make_async_copy(own, shard(0), wsem.at[0]).start()
    for k in range(1, line):

        @pl.when(z >= k)
        def _(k=k):
            pltpu.make_async_copy(ups[k - 1], shard(k), wsem.at[k]).start()

        @pl.when(z < k)
        def _(k=k):
            pltpu.make_async_copy(downs[line - k - 1], shard(k), wsem.at[k]).start()

    x_copies = [
        pltpu.make_async_copy(ref, x.at[pl.ds(p * rows, rows), :], xsem.at[p])
        for p, ref in enumerate(pieces)
    ]
    g_copies = [
        pltpu.make_async_copy(
            scaled.at[pl.ds(r * block, block), :], g.at[pl.ds(r * block, block), :], gsem.at[r]
        )
        for r in range(4)
    ]
    for r in range(4):
        for p in range(r * n_pieces // 4, (r + 1) * n_pieces // 4):
            x_copies[p].start()
        g_copies[r].start()
    for k in range(line):
        pltpu.make_async_copy(own, shard(k), wsem.at[k]).wait()

    for r in range(4):
        for p in range(r * n_pieces // 4, (r + 1) * n_pieces // 4):
            x_copies[p].wait()
        g_copies[r].wait()
        here = slice(r * block, (r + 1) * block)
        pre = dot(x[here, :], w[:, : 2 * step])
        back = dot(g[here, :], w[:, 2 * step :])
        h, a, b = swish_backward(pre[:, :step], pre[:, step:], back)
        hid[here, :] = h
        merged[here, :step] = a
        merged[here, step:] = b

    for k in range(line):
        f = lax.rem(z - k + line, line)
        cols = pl.ds(pl.multiple_of(f * depth, depth), depth)
        parts[k][:, : 2 * step] = dot_tn(x[:, cols], merged[...]).astype(BF16)
        parts[k][:, 2 * step :] = dot_tn(g[:, cols], hid[...]).astype(BF16)
    both[...] = w[:, : 2 * step]


def route_kernel(chunks, *refs):
    merged, both = refs[:chunks], refs[chunks : 2 * chunks]
    keep, give = refs[2 * chunks :]
    rows, width = keep.shape
    tile = width // 8

    for out, first in ((give, rows), (keep, 0)):

        @pl.loop(0, 8)
        def _(t, out=out, first=first):
            cols = pl.ds(pl.multiple_of(t * tile, tile), tile)
            total = None
            for m, b in zip(merged, both):
                part = dot_nt(m[first : first + rows, :], b[cols, :])
                total = part if total is None else total + part
            out[:, cols] = total.astype(BF16)


def dense_plan(tokens, out_grad, routes, gate_prob, w_gate, w_up, w_down):
    experts = lax.axis_size("expert")
    wide = lax.axis_size("wide")
    line = wide // 2
    rows, width = tokens.shape
    feats = w_gate.shape[1]
    half = w_gate.shape[2] // 2
    step = LANES
    chunks = half // step
    mine = lax.axis_index("expert")
    place = lax.axis_index("wide")
    z, c = place // 2, place % 2
    at = jnp.stack((z, c, mine)).astype(jnp.int32)
    shape = jax.ShapeDtypeStruct

    def after(a, *b):
        return lax.optimization_barrier((a, *b))[0]

    def twin(a):
        return lax.ppermute(a, "wide", [(i, i ^ 1) for i in range(wide)])

    def along(a, hops):
        return lax.ppermute(
            a, "wide", [(2 * s + i, 2 * t + i) for s, t in hops for i in range(2)]
        )

    def flip(a, bit):
        return lax.ppermute(a, "expert", [(e, e ^ bit) for e in range(experts)])

    cut = [shape((feats, 3 * step), BF16)] * (2 * chunks)
    packed = call(
        lambda *r: pack_kernel(chunks, step, *r),
        [SMEM] + [VMEM] * 3,
        cut,
        (at, w_gate[0], w_up[0], w_down[0]),
    )
    given = [twin(a) for a in packed[chunks:]]
    shards = call(
        lambda *r: combine_kernel(chunks, *r),
        [SMEM] + [VMEM] * (2 * chunks),
        [shape((2 * feats, 3 * step), BF16)] * chunks,
        (at, *packed[:chunks], *given),
    )

    named = jnp.arange(experts, dtype=jnp.int32)[None, :]
    gates = sum(
        jnp.where(routes[:, k : k + 1] == named, gate_prob[:, k : k + 1], 0.0)
        for k in range(routes.shape[1])
    )
    high = lax.reduce_precision(gates, 8, 7)
    middle = lax.reduce_precision(gates - high, 8, 7)
    terms = jnp.concatenate((high, middle, gates - high - middle), axis=1).astype(BF16)
    terms = jnp.pad(terms, ((0, 0), (0, LANES - terms.shape[1])))
    graded = jnp.concatenate((out_grad, terms), axis=1)

    with jax.named_scope("rows"):
        t = [tokens, *(after(flip(tokens, bit), *shards) for bit in (1, 2))]
        graded = after(graded, *shards)
        g = [graded, flip(graded, 1), flip(graded, 2)]
        t.append(flip(t[1], 2))
        g.append(flip(g[2], 1))
        t += [twin(a) for a in t]
        g += [twin(a) for a in g]
    count = len(t) * rows
    [scaled] = call(
        lambda *r: scale_kernel(experts, *r),
        [SMEM] + [VMEM] * len(g),
        [shape((count, width), BF16)],
        (at, *g),
    )

    def gather(own, before):
        ups, downs = [own], [own]
        for s in range(1, line):
            up, down = ups[-1], downs[-1]
            if s == line - 1:
                up, down = after(up, *before), after(down, *before)
            with jax.named_scope(f"gather_step_{s}"):
                ups.append(along(up, [(i, i + 1) for i in range(s - 1, line - 1)]))
                downs.append(along(down, [(i, i - 1) for i in range(1, line - s + 1)]))
        return (own, *ups[1:], *downs[1:])

    def begin(parts):
        with jax.named_scope("scatter_step_1"):
            a = jnp.where(z == 0, parts[1], parts[line - 1])
            first = along(a, [(0, 1), (line - 1, line - 2)])
        return first, first

    def hop(parts, state, s, waits):
        up, down = state
        if s == 2 and line == 4:
            a = b = add(parts[2], up)
        elif s == 2:
            a = add(parts[2], jnp.where(z == 1, up, 0))
            b = add(parts[line - 2], jnp.where(z == line - 2, down, 0))
        else:
            a, b = add(parts[s], up), add(parts[line - s], down)
        a, b = after(a, *waits), after(b, *waits)
        with jax.named_scope(f"scatter_step_{s}"):
            up = along(a, [(i, i + 1) for i in range(s)])
            down = along(b, [(i, i - 1) for i in range(line - s, line)])
        return up, down

    merged, both, parts, states, tie, before = [], [], [], [], (), (t[experts - 1], g[experts - 1])
    for i in range(chunks):
        loaded = gather(shards[i], before)
        if i == 0:
            before = (loaded[line - 1], loaded[2 * line - 2])
        got = call(
            lambda *r: chunk_kernel(line, len(t), *r),
            [SMEM] + [ANY] * (len(t) + 2 * line),
            [shape((2 * feats, 3 * step), BF16)] * line
            + [shape((count, 2 * step), BF16), shape((width, 2 * step), BF16)],
            (at, *t, after(scaled, *tie), *loaded),
            (
                pltpu.VMEM((count, width), BF16),
                pltpu.VMEM((count, width), BF16),
                pltpu.VMEM((width, 3 * step), BF16),
                pltpu.VMEM((count, step), BF16),
                pltpu.SemaphoreType.DMA((len(t),)),
                pltpu.SemaphoreType.DMA((4,)),
                pltpu.SemaphoreType.DMA((line,)),
            ),
            flops=12 * count * width * step,
        )
        merged.append(got[line])
        both.append(got[line + 1])
        parts.append(got[:line])
        states.append(begin(got[:line]))
        if i == 0:
            before += (merged[0],)
            tie = states[0]
        else:
            tie = states[i - 1]
            states[i - 1] = hop(parts[i - 1], tie, 2, ())

    block = experts * rows
    merged[-1] = after(merged[-1], *states[-2])
    keep, give = call(
        lambda *r: route_kernel(chunks, *r),
        [VMEM] * (2 * chunks),
        [shape((block, width), BF16)] * 2,
        (*merged, *both),
        flops=4 * count * width * step * chunks,
    )
    with jax.named_scope("back"):
        other = twin(after(give, *states[-1]))
        ret = keep.astype(F32) + other.astype(F32)
        ret = ret.reshape(experts, rows, width)
        left, right = ret[:, :, : width // 2], ret[:, :, width // 2 :]
        far = flip(left[2:].astype(BF16), 2)
        odd = flip(jnp.stack((right[1], right[3])).astype(BF16), 1)
        left = left[:2] + far.astype(F32)
        near = flip(left[1].astype(BF16), 1)
        last = flip((right[2] + odd[1].astype(F32)).astype(BF16), 2)
        left = left[0] + near.astype(F32)
        right = right[0] + odd[0].astype(F32) + last.astype(F32)
        grad_input = jnp.concatenate((left, right), axis=1).astype(BF16)
    states[-1] = hop(parts[-1], states[-1], 2, (other,))
    sums = []
    for own, (up, down) in zip(parts, states):
        for s in range(3, line):
            up, down = hop(own, (up, down), s, (odd, far))
        sums.append(own[0].astype(F32) + up.astype(F32) + down.astype(F32))

    own = [lax.dynamic_slice_in_dim(s, c * feats, feats, 0) for s in sums]
    other = [twin(lax.dynamic_slice_in_dim(s, (1 - c) * feats, feats, 0)) for s in sums]

    def grad_of(j):
        cols = slice(j * step, (j + 1) * step)
        a = jnp.concatenate([s[:, cols] for s in own], axis=1)
        b = jnp.concatenate([s[:, cols] for s in other], axis=1)
        first = jnp.concatenate((a, b), axis=1)
        return jnp.where(c == 0, first, jnp.concatenate((b, a), axis=1))[None]

    return (grad_input, grad_of(0), grad_of(1), grad_of(2))


def solution(mesh):
    experts, wide = mesh.shape["expert"], mesh.shape["wide"]
    split = P(("expert", "wide"), None)
    weight = P("expert", "wide", None)

    def on_device(tokens, out_grad, routes, *rest):
        dense = experts == 4 and wide % 2 == 0 and wide > 4 and 2 * routes.shape[1] >= experts
        dense = dense and rest[1].shape[2] % (2 * LANES) == 0
        return (dense_plan if dense else slot_plan)(tokens, out_grad, routes, *rest)

    return jax.shard_map(
        on_device,
        mesh=mesh,
        in_specs=(split,) * 4 + (weight,) * 3,
        out_specs=(split, weight, weight, weight),
        check_vma=False,
    )
```

```python
import jax
import jax.numpy as jnp
from jax import lax
from jax.experimental import pallas as pl
from jax.experimental.pallas import tpu as pltpu
from jax.experimental import pallas as pl
from jax.experimental.pallas import tpu as pltpu
from jax.sharding import PartitionSpec as P

LANES = 128
F32 = jnp.float32
BF16 = jnp.bfloat16


def swish_backward(gate_pre, up_pre, hidden_grad):
    squash = jax.nn.sigmoid(gate_pre)
    active = gate_pre * squash
    hidden = (active * up_pre).astype(BF16)
    gate_act = (hidden_grad * up_pre * squash * (1.0 + gate_pre * (1.0 - squash))).astype(BF16)
    up_act = (hidden_grad * active).astype(BF16)
    return (hidden, gate_act, up_act)


def dot(a, b):
    return jnp.dot(a, b, preferred_element_type=F32)


def dot_tn(a, b):
    return lax.dot_general(a, b, (((0,), (0,)), ((), ())), preferred_element_type=F32)


def dot_nt(a, b):
    return lax.dot_general(a, b, (((1,), (1,)), ((), ())), preferred_element_type=F32)


def add(a, b):
    return (a.astype(F32) + b.astype(F32)).astype(BF16)


def slot_plan(tokens, out_grad, routes, gate_prob, w_gate, w_up, w_down):
    experts = lax.axis_size("expert")
    tok_count, top_count = routes.shape
    capacity = min(tok_count, 2 * tok_count * top_count // experts)
    slot_count = experts * capacity
    model_width = tokens.shape[1]
    hidden_units = w_gate.shape[2]
    flat_routes = routes.reshape(-1)
    order = jnp.arange(tok_count * top_count, dtype=jnp.int32)
    same = flat_routes[:, None] == flat_routes[None, :]
    before = jnp.sum((same & (order[None, :] < order[:, None])).astype(jnp.int32), axis=1)
    positions = flat_routes * capacity + before
    chosen = (positions[None, :] == jnp.arange(slot_count, dtype=jnp.int32)[:, None]).reshape(
        slot_count, tok_count, top_count
    )
    picker = jnp.sum(chosen.astype(F32), axis=2)
    slot_gate = jnp.sum(jnp.where(chosen, gate_prob[None, :, :], 0.0), axis=(1, 2))
    picker_half = picker.astype(BF16)
    sent_rows = dot(picker_half, tokens).astype(BF16)
    sent_grad = (dot(picker_half, out_grad) * slot_gate[:, None]).astype(BF16)

    def exchange(rows):
        return lax.all_to_all(
            rows.reshape(experts, capacity, model_width),
            "expert",
            split_axis=0,
            concat_axis=0,
            tiled=True,
        ).reshape(slot_count, model_width)

    rows_in = exchange(sent_rows)
    grad_in = exchange(sent_grad)
    full_gate, full_up, full_down = (
        lax.all_gather(w, "wide", axis=1, tiled=True)[0] for w in (w_gate, w_up, w_down)
    )
    hidden, gate_act, up_act = swish_backward(
        dot(rows_in, full_gate), dot(rows_in, full_up), dot(grad_in, full_down)
    )
    merged = jnp.concatenate((gate_act, up_act), axis=1)
    input_grad = dot_nt(merged, jnp.concatenate((full_gate, full_up), axis=1)).astype(BF16)
    parts = jnp.concatenate((dot_tn(rows_in, merged), dot_tn(grad_in, hidden)), axis=1)
    summed = lax.psum_scatter(
        parts.astype(BF16), "wide", scatter_dimension=0, tiled=True
    ).astype(F32)
    grads = tuple(
        summed[:, i * hidden_units : (i + 1) * hidden_units][None] for i in range(3)
    )
    grad_input = dot_tn(picker_half, exchange(input_grad)).astype(BF16)
    return (grad_input,) + grads


VMEM = pl.BlockSpec(memory_space=pltpu.VMEM)
SMEM = pl.BlockSpec(memory_space=pltpu.SMEM)
ANY = pl.BlockSpec(memory_space=pl.ANY)
LIMIT = 40 << 20


def call(body, ins, outs, operands, scratch=(), flops=0, limit=LIMIT):
    moved = sum(a.size * a.dtype.itemsize for a in operands)
    moved += sum(o.size * o.dtype.itemsize for o in outs)
    return pl.pallas_call(
        body,
        out_shape=outs,
        in_specs=ins,
        out_specs=[VMEM] * len(outs),
        scratch_shapes=list(scratch),
        cost_estimate=pl.CostEstimate(flops=flops, bytes_accessed=moved, transcendentals=0),
        compiler_params=pltpu.CompilerParams(vmem_limit_bytes=limit),
    )(*operands)


def half_of(ref, side, half, i, step):
    return ref[:, pl.ds(pl.multiple_of(side * half + i * step, step), step)]


def pack_kernel(chunks, step, at, gate, up, down, *outs):
    half = chunks * step
    c = at[1]
    for side, group in ((c, outs[:chunks]), (1 - c, outs[chunks:])):
        for i, out in enumerate(group):
            for m, ref in enumerate((gate, up, down)):
                out[:, m * step : (m + 1) * step] = half_of(ref, side, half, i, step)


def combine_kernel(chunks, at, *refs):
    kept, given, outs = refs[:chunks], refs[chunks : 2 * chunks], refs[2 * chunks :]
    feats = kept[0].shape[0]
    c = at[1]
    for a, b, out in zip(kept, given, outs):
        out[pl.ds(pl.multiple_of(c * feats, feats), feats), :] = a[...]
        out[pl.ds(pl.multiple_of((1 - c) * feats, feats), feats), :] = b[...]


def scale_kernel(experts, at, *refs):
    pieces, out = refs[:-1], refs[-1]
    rows, width = pieces[0].shape[0], out.shape[1]
    lane = lax.broadcasted_iota(jnp.int32, (rows, LANES), 1)
    ours = (lax.rem(lane, experts) == at[2]) & (lane < 3 * experts)
    for p, ref in enumerate(pieces):
        terms = jnp.where(ours, ref[:, width:].astype(F32), 0.0)
        gate = jnp.sum(terms, axis=1, keepdims=True)
        out[p * rows : (p + 1) * rows, :] = (gate * ref[:, :width].astype(F32)).astype(BF16)


def chunk_kernel(line, n_pieces, at, *refs):
    pieces, refs = refs[:n_pieces], refs[n_pieces:]
    scaled, own = refs[0], refs[1]
    ups, downs = refs[2 : 1 + line], refs[1 + line : 2 * line]
    outs = refs[2 * line : 2 * line + line + 2]
    parts, merged, both = outs[:line], outs[line], outs[line + 1]
    x, g, w, hid, xsem, gsem, wsem = refs[2 * line + line + 2 :]
    z = at[0]
    depth, step = own.shape[0], own.shape[1] // 3
    rows = x.shape[0] // n_pieces
    block = x.shape[0] // 4

    def shard(k):
        f = lax.rem(z - k + line, line)
        return w.at[pl.ds(pl.multiple_of(f * depth, depth), depth), :]

    pltpu.make_async_copy(own, shard(0), wsem.at[0]).start()
    for k in range(1, line):

        @pl.when(z >= k)
        def _(k=k):
            pltpu.make_async_copy(ups[k - 1], shard(k), wsem.at[k]).start()

        @pl.when(z < k)
        def _(k=k):
            pltpu.make_async_copy(downs[line - k - 1], shard(k), wsem.at[k]).start()

    x_copies = [
        pltpu.make_async_copy(ref, x.at[pl.ds(p * rows, rows), :], xsem.at[p])
        for p, ref in enumerate(pieces)
    ]
    g_copies = [
        pltpu.make_async_copy(
            scaled.at[pl.ds(r * block, block), :], g.at[pl.ds(r * block, block), :], gsem.at[r]
        )
        for r in range(4)
    ]
    for r in range(4):
        for p in range(r * n_pieces // 4, (r + 1) * n_pieces // 4):
            x_copies[p].start()
        g_copies[r].start()
    for k in range(line):
        pltpu.make_async_copy(own, shard(k), wsem.at[k]).wait()

    for r in range(4):
        for p in range(r * n_pieces // 4, (r + 1) * n_pieces // 4):
            x_copies[p].wait()
        g_copies[r].wait()
        here = slice(r * block, (r + 1) * block)
        pre = dot(x[here, :], w[:, : 2 * step])
        back = dot(g[here, :], w[:, 2 * step :])
        h, a, b = swish_backward(pre[:, :step], pre[:, step:], back)
        hid[here, :] = h
        merged[here, :step] = a
        merged[here, step:] = b

    for k in range(line):
        f = lax.rem(z - k + line, line)
        cols = pl.ds(pl.multiple_of(f * depth, depth), depth)
        parts[k][:, : 2 * step] = dot_tn(x[:, cols], merged[...]).astype(BF16)
        parts[k][:, 2 * step :] = dot_tn(g[:, cols], hid[...]).astype(BF16)
    both[...] = w[:, : 2 * step]


def route_kernel(chunks, *refs):
    merged, both = refs[:chunks], refs[chunks : 2 * chunks]
    keep, give = refs[2 * chunks :]
    rows, width = keep.shape
    tile = width // 8

    for out, first in ((give, rows), (keep, 0)):

        @pl.loop(0, 8)
        def _(t, out=out, first=first):
            cols = pl.ds(pl.multiple_of(t * tile, tile), tile)
            total = None
            for m, b in zip(merged, both):
                part = dot_nt(m[first : first + rows, :], b[cols, :])
                total = part if total is None else total + part
            out[:, cols] = total.astype(BF16)


def dense_plan(tokens, out_grad, routes, gate_prob, w_gate, w_up, w_down):
    experts = lax.axis_size("expert")
    wide = lax.axis_size("wide")
    line = wide // 2
    rows, width = tokens.shape
    feats = w_gate.shape[1]
    half = w_gate.shape[2] // 2
    step = LANES
    chunks = half // step
    mine = lax.axis_index("expert")
    place = lax.axis_index("wide")
    z, c = place // 2, place % 2
    at = jnp.stack((z, c, mine)).astype(jnp.int32)
    shape = jax.ShapeDtypeStruct

    def after(a, *b):
        return lax.optimization_barrier((a, *b))[0]

    def twin(a):
        return lax.ppermute(a, "wide", [(i, i ^ 1) for i in range(wide)])

    def along(a, hops):
        return lax.ppermute(
            a, "wide", [(2 * s + i, 2 * t + i) for s, t in hops for i in range(2)]
        )

    def flip(a, bit):
        return lax.ppermute(a, "expert", [(e, e ^ bit) for e in range(experts)])

    cut = [shape((feats, 3 * step), BF16)] * (2 * chunks)
    packed = call(
        lambda *r: pack_kernel(chunks, step, *r),
        [SMEM] + [VMEM] * 3,
        cut,
        (at, w_gate[0], w_up[0], w_down[0]),
    )
    given = [twin(a) for a in packed[chunks:]]
    shards = call(
        lambda *r: combine_kernel(chunks, *r),
        [SMEM] + [VMEM] * (2 * chunks),
        [shape((2 * feats, 3 * step), BF16)] * chunks,
        (at, *packed[:chunks], *given),
    )

    named = jnp.arange(experts, dtype=jnp.int32)[None, :]
    gates = sum(
        jnp.where(routes[:, k : k + 1] == named, gate_prob[:, k : k + 1], 0.0)
        for k in range(routes.shape[1])
    )
    high = lax.reduce_precision(gates, 8, 7)
    middle = lax.reduce_precision(gates - high, 8, 7)
    terms = jnp.concatenate((high, middle, gates - high - middle), axis=1).astype(BF16)
    terms = jnp.pad(terms, ((0, 0), (0, LANES - terms.shape[1])))
    graded = jnp.concatenate((out_grad, terms), axis=1)

    with jax.named_scope("rows"):
        t = [tokens, *(after(flip(tokens, bit), *shards) for bit in (1, 2))]
        graded = after(graded, *shards)
        g = [graded, flip(graded, 1), flip(graded, 2)]
        t.append(flip(t[1], 2))
        g.append(flip(g[2], 1))
        t += [twin(a) for a in t]
        g += [twin(a) for a in g]
    count = len(t) * rows
    [scaled] = call(
        lambda *r: scale_kernel(experts, *r),
        [SMEM] + [VMEM] * len(g),
        [shape((count, width), BF16)],
        (at, *g),
    )

    ups = [[a] for a in shards]
    downs = [[a] for a in shards]

    def forward(i, s, waits):
        up, down = after(ups[i][-1], *waits), after(downs[i][-1], *waits)
        with jax.named_scope(f"gather_step_{s}"):
            ups[i].append(along(up, [(j, j + 1) for j in range(s - 1, line - 1)]))
            downs[i].append(along(down, [(j, j - 1) for j in range(1, line - s + 1)]))
        return ups[i][-1], downs[i][-1]

    landed = ()
    for s in range(1, line - 1):
        landed = ()
        for i in range(chunks):
            hops = forward(i, s, ())
            if s == 1 or i == chunks - 1:
                landed += hops
        if s == 1:
            firsts = landed
    last = landed
    landed = forward(0, line - 1, firsts)

    def begin(parts):
        with jax.named_scope("scatter_step_1"):
            a = jnp.where(z == 0, parts[1], parts[line - 1])
            first = along(a, [(0, 1), (line - 1, line - 2)])
        return first, first

    def hop(parts, state, s, waits):
        up, down = state
        if s == 2 and line == 4:
            a = b = add(parts[2], up)
        elif s == 2:
            a = add(parts[2], jnp.where(z == 1, up, 0))
            b = add(parts[line - 2], jnp.where(z == line - 2, down, 0))
        else:
            a, b = add(parts[s], up), add(parts[line - s], down)
        a, b = after(a, *waits), after(b, *waits)
        with jax.named_scope(f"scatter_step_{s}"):
            up = along(a, [(i, i + 1) for i in range(s)])
            down = along(b, [(i, i - 1) for i in range(line - s, line)])
        return up, down

    merged, both, parts, states, starts, tie = [], [], [], [], [], ()
    for i in range(chunks):
        if i == 1:
            landed = forward(i, line - 1, landed + last)
        elif i > 1:
            landed = forward(i, line - 1, landed + (merged[0],))
        loaded = (shards[i], *ups[i][1:], *downs[i][1:])
        got = call(
            lambda *r: chunk_kernel(line, len(t), *r),
            [SMEM] + [ANY] * (len(t) + 2 * line),
            [shape((2 * feats, 3 * step), BF16)] * line
            + [shape((count, 2 * step), BF16), shape((width, 2 * step), BF16)],
            (at, *t, after(scaled, *tie), *loaded),
            (
                pltpu.VMEM((count, width), BF16),
                pltpu.VMEM((count, width), BF16),
                pltpu.VMEM((width, 3 * step), BF16),
                pltpu.VMEM((count, step), BF16),
                pltpu.SemaphoreType.DMA((len(t),)),
                pltpu.SemaphoreType.DMA((4,)),
                pltpu.SemaphoreType.DMA((line,)),
            ),
            flops=12 * count * width * step,
        )
        merged.append(got[line])
        both.append(got[line + 1])
        parts.append(got[:line])
        states.append(begin(got[:line]))
        starts.append(states[-1])
        if i == 0:
            tie = states[0]
        else:
            states[i - 1] = hop(parts[i - 1], states[i - 1], 2, ())

    block = experts * rows
    merged[-1] = after(merged[-1], *states[0], *starts[-2])
    keep, give = call(
        lambda *r: route_kernel(chunks, *r),
        [VMEM] * (2 * chunks),
        [shape((block, width), BF16)] * 2,
        (*merged, *both),
        flops=4 * count * width * step * chunks,
    )
    with jax.named_scope("back"):
        other = twin(after(give, *states[-1]))
        ret = keep.astype(F32) + other.astype(F32)
        ret = ret.reshape(experts, rows, width)
        left, right = ret[:, :, : width // 2], ret[:, :, width // 2 :]
        far = flip(left[2:].astype(BF16), 2)
        odd = flip(jnp.stack((right[1], right[3])).astype(BF16), 1)
        left = left[:2] + far.astype(F32)
        near = flip(left[1].astype(BF16), 1)
        last = flip((right[2] + odd[1].astype(F32)).astype(BF16), 2)
        left = left[0] + near.astype(F32)
        right = right[0] + odd[0].astype(F32) + last.astype(F32)
        grad_input = jnp.concatenate((left, right), axis=1).astype(BF16)
    states[-1] = hop(parts[-1], states[-1], 2, (other,))
    sums = []
    for i, (own, (up, down)) in enumerate(zip(parts, states)):
        for s in range(3, line):
            up, down = hop(own, (up, down), s, (odd, far) if i == chunks - 1 else (other,))
        sums.append(own[0].astype(F32) + up.astype(F32) + down.astype(F32))

    own = [lax.dynamic_slice_in_dim(s, c * feats, feats, 0) for s in sums]
    other = [twin(lax.dynamic_slice_in_dim(s, (1 - c) * feats, feats, 0)) for s in sums]

    def grad_of(j):
        cols = slice(j * step, (j + 1) * step)
        a = jnp.concatenate([s[:, cols] for s in own], axis=1)
        b = jnp.concatenate([s[:, cols] for s in other], axis=1)
        first = jnp.concatenate((a, b), axis=1)
        return jnp.where(c == 0, first, jnp.concatenate((b, a), axis=1))[None]

    return (grad_input, grad_of(0), grad_of(1), grad_of(2))


def solution(mesh):
    experts, wide = mesh.shape["expert"], mesh.shape["wide"]
    split = P(("expert", "wide"), None)
    weight = P("expert", "wide", None)

    def on_device(tokens, out_grad, routes, *rest):
        dense = experts == 4 and wide % 2 == 0 and wide > 4 and 2 * routes.shape[1] >= experts
        dense = dense and rest[1].shape[2] % (2 * LANES) == 0
        return (dense_plan if dense else slot_plan)(tokens, out_grad, routes, *rest)

    return jax.shard_map(
        on_device,
        mesh=mesh,
        in_specs=(split,) * 4 + (weight,) * 3,
        out_specs=(split, weight, weight, weight),
        check_vma=False,
    )
```

```python
import jax
import jax.numpy as jnp
from jax import lax
from jax.experimental import pallas as pl
from jax.experimental.pallas import tpu as pltpu
from jax.experimental import pallas as pl
from jax.experimental.pallas import tpu as pltpu
from jax.sharding import PartitionSpec as P

LANES = 128
F32 = jnp.float32
BF16 = jnp.bfloat16


def swish_backward(gate_pre, up_pre, hidden_grad):
    squash = jax.nn.sigmoid(gate_pre)
    active = gate_pre * squash
    hidden = (active * up_pre).astype(BF16)
    gate_act = (hidden_grad * up_pre * squash * (1.0 + gate_pre * (1.0 - squash))).astype(BF16)
    up_act = (hidden_grad * active).astype(BF16)
    return (hidden, gate_act, up_act)


def dot(a, b):
    return jnp.dot(a, b, preferred_element_type=F32)


def dot_tn(a, b):
    return lax.dot_general(a, b, (((0,), (0,)), ((), ())), preferred_element_type=F32)


def dot_nt(a, b):
    return lax.dot_general(a, b, (((1,), (1,)), ((), ())), preferred_element_type=F32)


def add(a, b):
    return (a.astype(F32) + b.astype(F32)).astype(BF16)


def slot_plan(tokens, out_grad, routes, gate_prob, w_gate, w_up, w_down):
    experts = lax.axis_size("expert")
    tok_count, top_count = routes.shape
    capacity = min(tok_count, 2 * tok_count * top_count // experts)
    slot_count = experts * capacity
    model_width = tokens.shape[1]
    hidden_units = w_gate.shape[2]
    flat_routes = routes.reshape(-1)
    order = jnp.arange(tok_count * top_count, dtype=jnp.int32)
    same = flat_routes[:, None] == flat_routes[None, :]
    before = jnp.sum((same & (order[None, :] < order[:, None])).astype(jnp.int32), axis=1)
    positions = flat_routes * capacity + before
    chosen = (positions[None, :] == jnp.arange(slot_count, dtype=jnp.int32)[:, None]).reshape(
        slot_count, tok_count, top_count
    )
    picker = jnp.sum(chosen.astype(F32), axis=2)
    slot_gate = jnp.sum(jnp.where(chosen, gate_prob[None, :, :], 0.0), axis=(1, 2))
    picker_half = picker.astype(BF16)
    sent_rows = dot(picker_half, tokens).astype(BF16)
    sent_grad = (dot(picker_half, out_grad) * slot_gate[:, None]).astype(BF16)

    def exchange(rows):
        return lax.all_to_all(
            rows.reshape(experts, capacity, model_width),
            "expert",
            split_axis=0,
            concat_axis=0,
            tiled=True,
        ).reshape(slot_count, model_width)

    rows_in = exchange(sent_rows)
    grad_in = exchange(sent_grad)
    full_gate, full_up, full_down = (
        lax.all_gather(w, "wide", axis=1, tiled=True)[0] for w in (w_gate, w_up, w_down)
    )
    hidden, gate_act, up_act = swish_backward(
        dot(rows_in, full_gate), dot(rows_in, full_up), dot(grad_in, full_down)
    )
    merged = jnp.concatenate((gate_act, up_act), axis=1)
    input_grad = dot_nt(merged, jnp.concatenate((full_gate, full_up), axis=1)).astype(BF16)
    parts = jnp.concatenate((dot_tn(rows_in, merged), dot_tn(grad_in, hidden)), axis=1)
    summed = lax.psum_scatter(
        parts.astype(BF16), "wide", scatter_dimension=0, tiled=True
    ).astype(F32)
    grads = tuple(
        summed[:, i * hidden_units : (i + 1) * hidden_units][None] for i in range(3)
    )
    grad_input = dot_tn(picker_half, exchange(input_grad)).astype(BF16)
    return (grad_input,) + grads


VMEM = pl.BlockSpec(memory_space=pltpu.VMEM)
SMEM = pl.BlockSpec(memory_space=pltpu.SMEM)
ANY = pl.BlockSpec(memory_space=pl.ANY)
LIMIT = 40 << 20


def call(body, ins, outs, operands, scratch=(), flops=0, limit=LIMIT):
    moved = sum(a.size * a.dtype.itemsize for a in operands)
    moved += sum(o.size * o.dtype.itemsize for o in outs)
    return pl.pallas_call(
        body,
        out_shape=outs,
        in_specs=ins,
        out_specs=[VMEM] * len(outs),
        scratch_shapes=list(scratch),
        cost_estimate=pl.CostEstimate(flops=flops, bytes_accessed=moved, transcendentals=0),
        compiler_params=pltpu.CompilerParams(vmem_limit_bytes=limit),
    )(*operands)


def half_of(ref, side, half, i, step):
    return ref[:, pl.ds(pl.multiple_of(side * half + i * step, step), step)]


def pack_kernel(chunks, step, at, gate, up, down, *outs):
    half = chunks * step
    c = at[1]
    for side, group in ((c, outs[:chunks]), (1 - c, outs[chunks:])):
        for i, out in enumerate(group):
            for m, ref in enumerate((gate, up, down)):
                out[:, m * step : (m + 1) * step] = half_of(ref, side, half, i, step)


def combine_kernel(chunks, at, *refs):
    kept, given, outs = refs[:chunks], refs[chunks : 2 * chunks], refs[2 * chunks :]
    feats = kept[0].shape[0]
    c = at[1]
    for a, b, out in zip(kept, given, outs):
        out[pl.ds(pl.multiple_of(c * feats, feats), feats), :] = a[...]
        out[pl.ds(pl.multiple_of((1 - c) * feats, feats), feats), :] = b[...]


def scale_kernel(experts, at, *refs):
    pieces, out = refs[:-1], refs[-1]
    rows, width = pieces[0].shape[0], out.shape[1]
    lane = lax.broadcasted_iota(jnp.int32, (rows, LANES), 1)
    ours = (lax.rem(lane, experts) == at[2]) & (lane < 3 * experts)
    for p, ref in enumerate(pieces):
        terms = jnp.where(ours, ref[:, width:].astype(F32), 0.0)
        gate = jnp.sum(terms, axis=1, keepdims=True)
        out[p * rows : (p + 1) * rows, :] = (gate * ref[:, :width].astype(F32)).astype(BF16)


def chunk_kernel(line, n_pieces, at, *refs):
    pieces, refs = refs[:n_pieces], refs[n_pieces:]
    scaled, own = refs[0], refs[1]
    ups, downs = refs[2 : 1 + line], refs[1 + line : 2 * line]
    outs = refs[2 * line : 2 * line + line + 2]
    parts, merged, both = outs[:line], outs[line], outs[line + 1]
    x, g, w, hid, xsem, gsem, wsem = refs[2 * line + line + 2 :]
    z = at[0]
    depth, step = own.shape[0], own.shape[1] // 3
    rows = x.shape[0] // n_pieces
    block = x.shape[0] // 4

    def shard(k):
        f = lax.rem(z - k + line, line)
        return w.at[pl.ds(pl.multiple_of(f * depth, depth), depth), :]

    pltpu.make_async_copy(own, shard(0), wsem.at[0]).start()
    for k in range(1, line):

        @pl.when(z >= k)
        def _(k=k):
            pltpu.make_async_copy(ups[k - 1], shard(k), wsem.at[k]).start()

        @pl.when(z < k)
        def _(k=k):
            pltpu.make_async_copy(downs[line - k - 1], shard(k), wsem.at[k]).start()

    x_copies = [
        pltpu.make_async_copy(ref, x.at[pl.ds(p * rows, rows), :], xsem.at[p])
        for p, ref in enumerate(pieces)
    ]
    g_copies = [
        pltpu.make_async_copy(
            scaled.at[pl.ds(r * block, block), :], g.at[pl.ds(r * block, block), :], gsem.at[r]
        )
        for r in range(4)
    ]
    for r in range(4):
        for p in range(r * n_pieces // 4, (r + 1) * n_pieces // 4):
            x_copies[p].start()
        g_copies[r].start()
    for k in range(line):
        pltpu.make_async_copy(own, shard(k), wsem.at[k]).wait()

    for r in range(4):
        for p in range(r * n_pieces // 4, (r + 1) * n_pieces // 4):
            x_copies[p].wait()
        g_copies[r].wait()
        here = slice(r * block, (r + 1) * block)
        pre = dot(x[here, :], w[:, : 2 * step])
        back = dot(g[here, :], w[:, 2 * step :])
        h, a, b = swish_backward(pre[:, :step], pre[:, step:], back)
        hid[here, :] = h
        merged[here, :step] = a
        merged[here, step:] = b

    for k in range(line):
        f = lax.rem(z - k + line, line)
        cols = pl.ds(pl.multiple_of(f * depth, depth), depth)
        parts[k][:, : 2 * step] = dot_tn(x[:, cols], merged[...]).astype(BF16)
        parts[k][:, 2 * step :] = dot_tn(g[:, cols], hid[...]).astype(BF16)
    both[...] = w[:, : 2 * step]


def route_kernel(chunks, *refs):
    merged, both = refs[:chunks], refs[chunks : 2 * chunks]
    keep, give = refs[2 * chunks :]
    rows, width = keep.shape
    tile = width // 8

    for out, first in ((give, rows), (keep, 0)):

        @pl.loop(0, 8)
        def _(t, out=out, first=first):
            cols = pl.ds(pl.multiple_of(t * tile, tile), tile)
            total = None
            for m, b in zip(merged, both):
                part = dot_nt(m[first : first + rows, :], b[cols, :])
                total = part if total is None else total + part
            out[:, cols] = total.astype(BF16)


def dense_plan(tokens, out_grad, routes, gate_prob, w_gate, w_up, w_down):
    experts = lax.axis_size("expert")
    wide = lax.axis_size("wide")
    line = wide // 2
    rows, width = tokens.shape
    feats = w_gate.shape[1]
    half = w_gate.shape[2] // 2
    step = LANES
    chunks = half // step
    mine = lax.axis_index("expert")
    place = lax.axis_index("wide")
    z, c = place // 2, place % 2
    at = jnp.stack((z, c, mine)).astype(jnp.int32)
    shape = jax.ShapeDtypeStruct

    def after(a, *b):
        return lax.optimization_barrier((a, *b))[0]

    def twin(a):
        return lax.ppermute(a, "wide", [(i, i ^ 1) for i in range(wide)])

    def along(a, hops):
        return lax.ppermute(
            a, "wide", [(2 * s + i, 2 * t + i) for s, t in hops for i in range(2)]
        )

    def flip(a, bit):
        return lax.ppermute(a, "expert", [(e, e ^ bit) for e in range(experts)])

    cut = [shape((feats, 3 * step), BF16)] * (2 * chunks)
    packed = call(
        lambda *r: pack_kernel(chunks, step, *r),
        [SMEM] + [VMEM] * 3,
        cut,
        (at, w_gate[0], w_up[0], w_down[0]),
    )
    given = [twin(a) for a in packed[chunks:]]
    shards = call(
        lambda *r: combine_kernel(chunks, *r),
        [SMEM] + [VMEM] * (2 * chunks),
        [shape((2 * feats, 3 * step), BF16)] * chunks,
        (at, *packed[:chunks], *given),
    )

    named = jnp.arange(experts, dtype=jnp.int32)[None, :]
    gates = sum(
        jnp.where(routes[:, k : k + 1] == named, gate_prob[:, k : k + 1], 0.0)
        for k in range(routes.shape[1])
    )
    high = lax.reduce_precision(gates, 8, 7)
    middle = lax.reduce_precision(gates - high, 8, 7)
    terms = jnp.concatenate((high, middle, gates - high - middle), axis=1).astype(BF16)
    terms = jnp.pad(terms, ((0, 0), (0, LANES - terms.shape[1])))
    graded = jnp.concatenate((out_grad, terms), axis=1)

    with jax.named_scope("rows"):
        t = [tokens, *(after(flip(tokens, bit), *shards) for bit in (1, 2))]
        graded = after(graded, *shards)
        g = [graded, flip(graded, 1), flip(graded, 2)]
        t.append(flip(t[1], 2))
        g.append(flip(g[2], 1))
        t += [twin(a) for a in t]
        g += [twin(a) for a in g]
    count = len(t) * rows
    [scaled] = call(
        lambda *r: scale_kernel(experts, *r),
        [SMEM] + [VMEM] * len(g),
        [shape((count, width), BF16)],
        (at, *g),
    )

    ups = [[a] for a in shards]
    downs = [[a] for a in shards]

    def forward(i, s, waits):
        up, down = after(ups[i][-1], *waits), after(downs[i][-1], *waits)
        with jax.named_scope(f"gather_step_{s}"):
            ups[i].append(along(up, [(j, j + 1) for j in range(s - 1, line - 1)]))
            downs[i].append(along(down, [(j, j - 1) for j in range(1, line - s + 1)]))
        return ups[i][-1], downs[i][-1]

    landed = ()
    for s in range(1, line - 1):
        landed = ()
        for i in range(chunks):
            hops = forward(i, s, ())
            if s == 1 or i == chunks - 1:
                landed += hops
        if s == 1:
            firsts = landed
    last = landed
    landed = forward(0, line - 1, firsts)

    def begin(parts):
        with jax.named_scope("scatter_step_1"):
            a = jnp.where(z == 0, parts[1], parts[line - 1])
            first = along(a, [(0, 1), (line - 1, line - 2)])
        return first, first

    def hop(parts, state, s, waits):
        up, down = state
        if s == 2 and line == 4:
            a = b = add(parts[2], up)
        elif s == 2:
            a = add(parts[2], jnp.where(z == 1, up, 0))
            b = add(parts[line - 2], jnp.where(z == line - 2, down, 0))
        else:
            a, b = add(parts[s], up), add(parts[line - s], down)
        a, b = after(a, *waits), after(b, *waits)
        with jax.named_scope(f"scatter_step_{s}"):
            up = along(a, [(i, i + 1) for i in range(s)])
            down = along(b, [(i, i - 1) for i in range(line - s, line)])
        return up, down

    merged, both, parts, states, starts, tie = [], [], [], [], [], ()
    for i in range(chunks):
        if i == 1:
            landed = forward(i, line - 1, landed + last)
        elif i > 1:
            landed = forward(i, line - 1, landed + (merged[0],))
        loaded = (shards[i], *ups[i][1:], *downs[i][1:])
        got = call(
            lambda *r: chunk_kernel(line, len(t), *r),
            [SMEM] + [ANY] * (len(t) + 2 * line),
            [shape((2 * feats, 3 * step), BF16)] * line
            + [shape((count, 2 * step), BF16), shape((width, 2 * step), BF16)],
            (at, *t, after(scaled, *tie), *loaded),
            (
                pltpu.VMEM((count, width), BF16),
                pltpu.VMEM((count, width), BF16),
                pltpu.VMEM((width, 3 * step), BF16),
                pltpu.VMEM((count, step), BF16),
                pltpu.SemaphoreType.DMA((len(t),)),
                pltpu.SemaphoreType.DMA((4,)),
                pltpu.SemaphoreType.DMA((line,)),
            ),
            flops=12 * count * width * step,
        )
        merged.append(got[line])
        both.append(got[line + 1])
        parts.append(got[:line])
        states.append(begin(got[:line]))
        starts.append(states[-1])
        if i == 0:
            tie = states[0]
        else:
            states[i - 1] = hop(parts[i - 1], states[i - 1], 2, ())

    block = experts * rows
    merged[-1] = after(merged[-1], *states[0], *starts[-2])
    keep, give = call(
        lambda *r: route_kernel(chunks, *r),
        [VMEM] * (2 * chunks),
        [shape((block, width), BF16)] * 2,
        (*merged, *both),
        flops=4 * count * width * step * chunks,
    )
    with jax.named_scope("back"):
        states[0] = hop(parts[0], states[0], line - 1, ())
        other = after(twin(after(give, *states[-1], *states[0])), *states[1])
        states[-1] = hop(parts[-1], states[-1], 2, ())
        states[1] = hop(parts[1], states[1], line - 1, (other,))
        ret = keep.astype(F32) + other.astype(F32)
        ret = ret.reshape(experts, rows, width)
        left, right = ret[:, :, : width // 2], ret[:, :, width // 2 :]
        far = flip(left[2:].astype(BF16), 2)
        odd = flip(jnp.stack((right[1], right[3])).astype(BF16), 1)
        left = left[:2] + far.astype(F32)
        busy = (*states[-1], *states[1])
        near = flip(after(left[1].astype(BF16), *busy), 1)
        last = flip(after((right[2] + odd[1].astype(F32)).astype(BF16), *busy), 2)
        left = left[0] + near.astype(F32)
        right = right[0] + odd[0].astype(F32) + last.astype(F32)
        grad_input = jnp.concatenate((left, right), axis=1).astype(BF16)
    states[-1] = hop(parts[-1], states[-1], line - 1, (odd, far))
    sums = []
    for own, (up, down) in zip(parts, states):
        sums.append(own[0].astype(F32) + up.astype(F32) + down.astype(F32))

    own = [lax.dynamic_slice_in_dim(s, c * feats, feats, 0) for s in sums]
    other = [twin(lax.dynamic_slice_in_dim(s, (1 - c) * feats, feats, 0)) for s in sums]

    def grad_of(j):
        cols = slice(j * step, (j + 1) * step)
        a = jnp.concatenate([s[:, cols] for s in own], axis=1)
        b = jnp.concatenate([s[:, cols] for s in other], axis=1)
        first = jnp.concatenate((a, b), axis=1)
        return jnp.where(c == 0, first, jnp.concatenate((b, a), axis=1))[None]

    return (grad_input, grad_of(0), grad_of(1), grad_of(2))


def solution(mesh):
    experts, wide = mesh.shape["expert"], mesh.shape["wide"]
    split = P(("expert", "wide"), None)
    weight = P("expert", "wide", None)

    def on_device(tokens, out_grad, routes, *rest):
        dense = experts == 4 and wide % 2 == 0 and wide > 4 and 2 * routes.shape[1] >= experts
        dense = dense and rest[1].shape[2] % (2 * LANES) == 0
        return (dense_plan if dense else slot_plan)(tokens, out_grad, routes, *rest)

    return jax.shard_map(
        on_device,
        mesh=mesh,
        in_specs=(split,) * 4 + (weight,) * 3,
        out_specs=(split, weight, weight, weight),
        check_vma=False,
    )
```

```python
import jax
import jax.numpy as jnp
from jax import lax
from jax.experimental import pallas as pl
from jax.experimental.pallas import tpu as pltpu
from jax.experimental import pallas as pl
from jax.experimental.pallas import tpu as pltpu
from jax.sharding import PartitionSpec as P

LANES = 128
F32 = jnp.float32
BF16 = jnp.bfloat16


def swish_backward(gate_pre, up_pre, hidden_grad):
    squash = jax.nn.sigmoid(gate_pre)
    active = gate_pre * squash
    hidden = (active * up_pre).astype(BF16)
    gate_act = (hidden_grad * up_pre * squash * (1.0 + gate_pre * (1.0 - squash))).astype(BF16)
    up_act = (hidden_grad * active).astype(BF16)
    return (hidden, gate_act, up_act)


def dot(a, b):
    return jnp.dot(a, b, preferred_element_type=F32)


def dot_tn(a, b):
    return lax.dot_general(a, b, (((0,), (0,)), ((), ())), preferred_element_type=F32)


def dot_nt(a, b):
    return lax.dot_general(a, b, (((1,), (1,)), ((), ())), preferred_element_type=F32)


def add(a, b):
    return (a.astype(F32) + b.astype(F32)).astype(BF16)


def slot_plan(tokens, out_grad, routes, gate_prob, w_gate, w_up, w_down):
    experts = lax.axis_size("expert")
    tok_count, top_count = routes.shape
    capacity = min(tok_count, 2 * tok_count * top_count // experts)
    slot_count = experts * capacity
    model_width = tokens.shape[1]
    hidden_units = w_gate.shape[2]
    flat_routes = routes.reshape(-1)
    order = jnp.arange(tok_count * top_count, dtype=jnp.int32)
    same = flat_routes[:, None] == flat_routes[None, :]
    before = jnp.sum((same & (order[None, :] < order[:, None])).astype(jnp.int32), axis=1)
    positions = flat_routes * capacity + before
    chosen = (positions[None, :] == jnp.arange(slot_count, dtype=jnp.int32)[:, None]).reshape(
        slot_count, tok_count, top_count
    )
    picker = jnp.sum(chosen.astype(F32), axis=2)
    slot_gate = jnp.sum(jnp.where(chosen, gate_prob[None, :, :], 0.0), axis=(1, 2))
    picker_half = picker.astype(BF16)
    sent_rows = dot(picker_half, tokens).astype(BF16)
    sent_grad = (dot(picker_half, out_grad) * slot_gate[:, None]).astype(BF16)

    def exchange(rows):
        return lax.all_to_all(
            rows.reshape(experts, capacity, model_width),
            "expert",
            split_axis=0,
            concat_axis=0,
            tiled=True,
        ).reshape(slot_count, model_width)

    rows_in = exchange(sent_rows)
    grad_in = exchange(sent_grad)
    full_gate, full_up, full_down = (
        lax.all_gather(w, "wide", axis=1, tiled=True)[0] for w in (w_gate, w_up, w_down)
    )
    hidden, gate_act, up_act = swish_backward(
        dot(rows_in, full_gate), dot(rows_in, full_up), dot(grad_in, full_down)
    )
    merged = jnp.concatenate((gate_act, up_act), axis=1)
    input_grad = dot_nt(merged, jnp.concatenate((full_gate, full_up), axis=1)).astype(BF16)
    parts = jnp.concatenate((dot_tn(rows_in, merged), dot_tn(grad_in, hidden)), axis=1)
    summed = lax.psum_scatter(
        parts.astype(BF16), "wide", scatter_dimension=0, tiled=True
    ).astype(F32)
    grads = tuple(
        summed[:, i * hidden_units : (i + 1) * hidden_units][None] for i in range(3)
    )
    grad_input = dot_tn(picker_half, exchange(input_grad)).astype(BF16)
    return (grad_input,) + grads


VMEM = pl.BlockSpec(memory_space=pltpu.VMEM)
SMEM = pl.BlockSpec(memory_space=pltpu.SMEM)
ANY = pl.BlockSpec(memory_space=pl.ANY)
LIMIT = 40 << 20


def call(body, ins, outs, operands, scratch=(), flops=0, limit=LIMIT):
    moved = sum(a.size * a.dtype.itemsize for a in operands)
    moved += sum(o.size * o.dtype.itemsize for o in outs)
    return pl.pallas_call(
        body,
        out_shape=outs,
        in_specs=ins,
        out_specs=[VMEM] * len(outs),
        scratch_shapes=list(scratch),
        cost_estimate=pl.CostEstimate(flops=flops, bytes_accessed=moved, transcendentals=0),
        compiler_params=pltpu.CompilerParams(vmem_limit_bytes=limit),
    )(*operands)


def half_of(ref, side, half, i, step):
    return ref[:, pl.ds(pl.multiple_of(side * half + i * step, step), step)]


def pack_kernel(chunks, step, at, gate, up, down, *outs):
    half = chunks * step
    c = at[1]
    for side, group in ((c, outs[:chunks]), (1 - c, outs[chunks:])):
        for i, out in enumerate(group):
            for m, ref in enumerate((gate, up, down)):
                out[:, m * step : (m + 1) * step] = half_of(ref, side, half, i, step)


def combine_kernel(chunks, at, *refs):
    kept, given, outs = refs[:chunks], refs[chunks : 2 * chunks], refs[2 * chunks :]
    feats = kept[0].shape[0]
    c = at[1]
    for a, b, out in zip(kept, given, outs):
        out[pl.ds(pl.multiple_of(c * feats, feats), feats), :] = a[...]
        out[pl.ds(pl.multiple_of((1 - c) * feats, feats), feats), :] = b[...]


def scale_kernel(experts, at, *refs):
    pieces, out = refs[:-1], refs[-1]
    rows, width = pieces[0].shape[0], out.shape[1]
    lane = lax.broadcasted_iota(jnp.int32, (rows, LANES), 1)
    ours = (lax.rem(lane, experts) == at[2]) & (lane < 3 * experts)
    for p, ref in enumerate(pieces):
        terms = jnp.where(ours, ref[:, width:].astype(F32), 0.0)
        gate = jnp.sum(terms, axis=1, keepdims=True)
        out[p * rows : (p + 1) * rows, :] = (gate * ref[:, :width].astype(F32)).astype(BF16)


def chunk_kernel(line, n_pieces, at, *refs):
    pieces, refs = refs[:n_pieces], refs[n_pieces:]
    scaled, own = refs[0], refs[1]
    ups, downs = refs[2 : 1 + line], refs[1 + line : 2 * line]
    outs = refs[2 * line : 2 * line + line + 2]
    parts, merged, both = outs[:line], outs[line], outs[line + 1]
    x, g, w, hid, xsem, gsem, wsem = refs[2 * line + line + 2 :]
    z = at[0]
    depth, step = own.shape[0], own.shape[1] // 3
    rows = x.shape[0] // n_pieces
    block = x.shape[0] // 4

    def shard(k):
        f = lax.rem(z - k + line, line)
        return w.at[pl.ds(pl.multiple_of(f * depth, depth), depth), :]

    pltpu.make_async_copy(own, shard(0), wsem.at[0]).start()
    for k in range(1, line):

        @pl.when(z >= k)
        def _(k=k):
            pltpu.make_async_copy(ups[k - 1], shard(k), wsem.at[k]).start()

        @pl.when(z < k)
        def _(k=k):
            pltpu.make_async_copy(downs[line - k - 1], shard(k), wsem.at[k]).start()

    x_copies = [
        pltpu.make_async_copy(ref, x.at[pl.ds(p * rows, rows), :], xsem.at[p])
        for p, ref in enumerate(pieces)
    ]
    g_copies = [
        pltpu.make_async_copy(
            scaled.at[pl.ds(r * block, block), :], g.at[pl.ds(r * block, block), :], gsem.at[r]
        )
        for r in range(4)
    ]
    for r in range(4):
        for p in range(r * n_pieces // 4, (r + 1) * n_pieces // 4):
            x_copies[p].start()
        g_copies[r].start()
    for k in range(line):
        pltpu.make_async_copy(own, shard(k), wsem.at[k]).wait()

    for r in range(4):
        for p in range(r * n_pieces // 4, (r + 1) * n_pieces // 4):
            x_copies[p].wait()
        g_copies[r].wait()
        here = slice(r * block, (r + 1) * block)
        pre = dot(x[here, :], w[:, : 2 * step])
        back = dot(g[here, :], w[:, 2 * step :])
        h, a, b = swish_backward(pre[:, :step], pre[:, step:], back)
        hid[here, :] = h
        merged[here, :step] = a
        merged[here, step:] = b

    for k in range(line):
        f = lax.rem(z - k + line, line)
        cols = pl.ds(pl.multiple_of(f * depth, depth), depth)
        parts[k][:, : 2 * step] = dot_tn(x[:, cols], merged[...]).astype(BF16)
        parts[k][:, 2 * step :] = dot_tn(g[:, cols], hid[...]).astype(BF16)
    both[...] = w[:, : 2 * step]


def route_kernel(chunks, *refs):
    merged, both = refs[:chunks], refs[chunks : 2 * chunks]
    keep, give = refs[2 * chunks :]
    rows, width = keep.shape
    tile = width // 8

    for out, first in ((give, rows), (keep, 0)):

        @pl.loop(0, 8)
        def _(t, out=out, first=first):
            cols = pl.ds(pl.multiple_of(t * tile, tile), tile)
            total = None
            for m, b in zip(merged, both):
                part = dot_nt(m[first : first + rows, :], b[cols, :])
                total = part if total is None else total + part
            out[:, cols] = total.astype(BF16)


def dense_plan(tokens, out_grad, routes, gate_prob, w_gate, w_up, w_down):
    experts = lax.axis_size("expert")
    wide = lax.axis_size("wide")
    line = wide // 2
    rows, width = tokens.shape
    feats = w_gate.shape[1]
    half = w_gate.shape[2] // 2
    step = LANES
    chunks = half // step
    mine = lax.axis_index("expert")
    place = lax.axis_index("wide")
    z, c = place // 2, place % 2
    at = jnp.stack((z, c, mine)).astype(jnp.int32)
    shape = jax.ShapeDtypeStruct

    def after(a, *b):
        return lax.optimization_barrier((a, *b))[0]

    def twin(a):
        return lax.ppermute(a, "wide", [(i, i ^ 1) for i in range(wide)])

    def along(a, hops):
        return lax.ppermute(
            a, "wide", [(2 * s + i, 2 * t + i) for s, t in hops for i in range(2)]
        )

    def flip(a, bit):
        return lax.ppermute(a, "expert", [(e, e ^ bit) for e in range(experts)])

    cut = [shape((feats, 3 * step), BF16)] * (2 * chunks)
    packed = call(
        lambda *r: pack_kernel(chunks, step, *r),
        [SMEM] + [VMEM] * 3,
        cut,
        (at, w_gate[0], w_up[0], w_down[0]),
    )
    given = [twin(a) for a in packed[chunks:]]
    shards = call(
        lambda *r: combine_kernel(chunks, *r),
        [SMEM] + [VMEM] * (2 * chunks),
        [shape((2 * feats, 3 * step), BF16)] * chunks,
        (at, *packed[:chunks], *given),
    )

    named = jnp.arange(experts, dtype=jnp.int32)[None, :]
    gates = sum(
        jnp.where(routes[:, k : k + 1] == named, gate_prob[:, k : k + 1], 0.0)
        for k in range(routes.shape[1])
    )
    high = lax.reduce_precision(gates, 8, 7)
    middle = lax.reduce_precision(gates - high, 8, 7)
    terms = jnp.concatenate((high, middle, gates - high - middle), axis=1).astype(BF16)
    terms = jnp.pad(terms, ((0, 0), (0, LANES - terms.shape[1])))
    graded = jnp.concatenate((out_grad, terms), axis=1)

    with jax.named_scope("rows"):
        t = [tokens, *(after(flip(tokens, bit), *shards) for bit in (1, 2))]
        graded = after(graded, *shards)
        g = [graded, flip(graded, 1), flip(graded, 2)]
        t.append(flip(t[1], 2))
        g.append(flip(g[2], 1))
        t += [twin(a) for a in t]
        g += [twin(a) for a in g]
    count = len(t) * rows
    [scaled] = call(
        lambda *r: scale_kernel(experts, *r),
        [SMEM] + [VMEM] * len(g),
        [shape((count, width), BF16)],
        (at, *g),
    )

    def forward(up, down, s):
        with jax.named_scope(f"gather_step_{s}"):
            return (
                along(up, [(i, i + 1) for i in range(s - 1, line - 1)]),
                along(down, [(i, i - 1) for i in range(1, line - s + 1)]),
            )

    firsts = [forward(a, a, 1) for a in shards]

    def gather(i, before):
        hops = [firsts[i]]
        for s in range(2, line):
            up, down = hops[-1]
            waits = firsts[-1] if s == 2 and 0 < i < chunks - 1 else ()
            if s == line - 1:
                waits += before
            hops.append(forward(after(up, *waits), after(down, *waits), s))
        return (shards[i], *(h[0] for h in hops), *(h[1] for h in hops))

    def begin(parts):
        with jax.named_scope("scatter_step_1"):
            a = jnp.where(z == 0, parts[1], parts[line - 1])
            first = along(a, [(0, 1), (line - 1, line - 2)])
        return first, first

    def hop(parts, state, s, waits):
        up, down = state
        if s == 2 and line == 4:
            a = b = add(parts[2], up)
        elif s == 2:
            a = add(parts[2], jnp.where(z == 1, up, 0))
            b = add(parts[line - 2], jnp.where(z == line - 2, down, 0))
        else:
            a, b = add(parts[s], up), add(parts[line - s], down)
        a, b = after(a, *waits), after(b, *waits)
        with jax.named_scope(f"scatter_step_{s}"):
            up = along(a, [(i, i + 1) for i in range(s)])
            down = along(b, [(i, i - 1) for i in range(line - s, line)])
        return up, down

    merged, both, parts, states, tie, before = [], [], [], [], (), (t[experts - 1], g[experts - 1])
    for i in range(chunks):
        loaded = gather(i, before)
        if i == 0:
            before = (loaded[line - 1], loaded[2 * line - 2])
        got = call(
            lambda *r: chunk_kernel(line, len(t), *r),
            [SMEM] + [ANY] * (len(t) + 2 * line),
            [shape((2 * feats, 3 * step), BF16)] * line
            + [shape((count, 2 * step), BF16), shape((width, 2 * step), BF16)],
            (at, *t, after(scaled, *tie), *loaded),
            (
                pltpu.VMEM((count, width), BF16),
                pltpu.VMEM((count, width), BF16),
                pltpu.VMEM((width, 3 * step), BF16),
                pltpu.VMEM((count, step), BF16),
                pltpu.SemaphoreType.DMA((len(t),)),
                pltpu.SemaphoreType.DMA((4,)),
                pltpu.SemaphoreType.DMA((line,)),
            ),
            flops=12 * count * width * step,
        )
        merged.append(got[line])
        both.append(got[line + 1])
        parts.append(got[:line])
        states.append(begin(got[:line]))
        if i == 0:
            before += (merged[0],)
            tie = states[0]
        else:
            tie = states[i - 1]
            states[i - 1] = hop(parts[i - 1], tie, 2, ())

    block = experts * rows
    merged[-1] = after(merged[-1], *states[-2])
    keep, give = call(
        lambda *r: route_kernel(chunks, *r),
        [VMEM] * (2 * chunks),
        [shape((block, width), BF16)] * 2,
        (*merged, *both),
        flops=4 * count * width * step * chunks,
    )
    with jax.named_scope("back"):
        states[0] = hop(parts[0], states[0], line - 1, ())
        other = after(twin(after(give, *states[-1])), *states[0])
        states[1] = hop(parts[1], states[1], line - 1, (other,))
        ret = keep.astype(F32) + other.astype(F32)
        ret = ret.reshape(experts, rows, width)
        left, right = ret[:, :, : width // 2], ret[:, :, width // 2 :]
        far = flip(left[2:].astype(BF16), 2)
        odd = flip(jnp.stack((right[1], right[3])).astype(BF16), 1)
        left = left[:2] + far.astype(F32)
        near = flip(after(left[1].astype(BF16), *states[1]), 1)
        last = flip(after((right[2] + odd[1].astype(F32)).astype(BF16), *states[1]), 2)
        left = left[0] + near.astype(F32)
        right = right[0] + odd[0].astype(F32) + last.astype(F32)
        grad_input = jnp.concatenate((left, right), axis=1).astype(BF16)
    states[-1] = hop(parts[-1], hop(parts[-1], states[-1], 2, (other,)), line - 1, (odd, far))
    sums = []
    for own, (up, down) in zip(parts, states):
        sums.append(own[0].astype(F32) + up.astype(F32) + down.astype(F32))

    own = [lax.dynamic_slice_in_dim(s, c * feats, feats, 0) for s in sums]
    other = [twin(lax.dynamic_slice_in_dim(s, (1 - c) * feats, feats, 0)) for s in sums]

    def grad_of(j):
        cols = slice(j * step, (j + 1) * step)
        a = jnp.concatenate([s[:, cols] for s in own], axis=1)
        b = jnp.concatenate([s[:, cols] for s in other], axis=1)
        first = jnp.concatenate((a, b), axis=1)
        return jnp.where(c == 0, first, jnp.concatenate((b, a), axis=1))[None]

    return (grad_input, grad_of(0), grad_of(1), grad_of(2))


def solution(mesh):
    experts, wide = mesh.shape["expert"], mesh.shape["wide"]
    split = P(("expert", "wide"), None)
    weight = P("expert", "wide", None)

    def on_device(tokens, out_grad, routes, *rest):
        dense = experts == 4 and wide % 2 == 0 and wide > 4 and 2 * routes.shape[1] >= experts
        dense = dense and rest[1].shape[2] % (2 * LANES) == 0
        return (dense_plan if dense else slot_plan)(tokens, out_grad, routes, *rest)

    return jax.shard_map(
        on_device,
        mesh=mesh,
        in_specs=(split,) * 4 + (weight,) * 3,
        out_specs=(split, weight, weight, weight),
        check_vma=False,
    )
```

```python
import jax
import jax.numpy as jnp
from jax import lax
from jax.experimental import pallas as pl
from jax.experimental.pallas import tpu as pltpu
from jax.experimental import pallas as pl
from jax.experimental.pallas import tpu as pltpu
from jax.sharding import PartitionSpec as P

LANES = 128
F32 = jnp.float32
BF16 = jnp.bfloat16


def swish_backward(gate_pre, up_pre, hidden_grad):
    squash = jax.nn.sigmoid(gate_pre)
    active = gate_pre * squash
    hidden = (active * up_pre).astype(BF16)
    gate_act = (hidden_grad * up_pre * squash * (1.0 + gate_pre * (1.0 - squash))).astype(BF16)
    up_act = (hidden_grad * active).astype(BF16)
    return (hidden, gate_act, up_act)


def dot(a, b):
    return jnp.dot(a, b, preferred_element_type=F32)


def dot_tn(a, b):
    return lax.dot_general(a, b, (((0,), (0,)), ((), ())), preferred_element_type=F32)


def dot_nt(a, b):
    return lax.dot_general(a, b, (((1,), (1,)), ((), ())), preferred_element_type=F32)


def add(a, b):
    return (a.astype(F32) + b.astype(F32)).astype(BF16)


def slot_plan(tokens, out_grad, routes, gate_prob, w_gate, w_up, w_down):
    experts = lax.axis_size("expert")
    tok_count, top_count = routes.shape
    capacity = min(tok_count, 2 * tok_count * top_count // experts)
    slot_count = experts * capacity
    model_width = tokens.shape[1]
    hidden_units = w_gate.shape[2]
    flat_routes = routes.reshape(-1)
    order = jnp.arange(tok_count * top_count, dtype=jnp.int32)
    same = flat_routes[:, None] == flat_routes[None, :]
    before = jnp.sum((same & (order[None, :] < order[:, None])).astype(jnp.int32), axis=1)
    positions = flat_routes * capacity + before
    chosen = (positions[None, :] == jnp.arange(slot_count, dtype=jnp.int32)[:, None]).reshape(
        slot_count, tok_count, top_count
    )
    picker = jnp.sum(chosen.astype(F32), axis=2)
    slot_gate = jnp.sum(jnp.where(chosen, gate_prob[None, :, :], 0.0), axis=(1, 2))
    picker_half = picker.astype(BF16)
    sent_rows = dot(picker_half, tokens).astype(BF16)
    sent_grad = (dot(picker_half, out_grad) * slot_gate[:, None]).astype(BF16)

    def exchange(rows):
        return lax.all_to_all(
            rows.reshape(experts, capacity, model_width),
            "expert",
            split_axis=0,
            concat_axis=0,
            tiled=True,
        ).reshape(slot_count, model_width)

    rows_in = exchange(sent_rows)
    grad_in = exchange(sent_grad)
    full_gate, full_up, full_down = (
        lax.all_gather(w, "wide", axis=1, tiled=True)[0] for w in (w_gate, w_up, w_down)
    )
    hidden, gate_act, up_act = swish_backward(
        dot(rows_in, full_gate), dot(rows_in, full_up), dot(grad_in, full_down)
    )
    merged = jnp.concatenate((gate_act, up_act), axis=1)
    input_grad = dot_nt(merged, jnp.concatenate((full_gate, full_up), axis=1)).astype(BF16)
    parts = jnp.concatenate((dot_tn(rows_in, merged), dot_tn(grad_in, hidden)), axis=1)
    summed = lax.psum_scatter(
        parts.astype(BF16), "wide", scatter_dimension=0, tiled=True
    ).astype(F32)
    grads = tuple(
        summed[:, i * hidden_units : (i + 1) * hidden_units][None] for i in range(3)
    )
    grad_input = dot_tn(picker_half, exchange(input_grad)).astype(BF16)
    return (grad_input,) + grads


VMEM = pl.BlockSpec(memory_space=pltpu.VMEM)
SMEM = pl.BlockSpec(memory_space=pltpu.SMEM)
ANY = pl.BlockSpec(memory_space=pl.ANY)
LIMIT = 40 << 20


def call(body, ins, outs, operands, scratch=(), flops=0, limit=LIMIT):
    moved = sum(a.size * a.dtype.itemsize for a in operands)
    moved += sum(o.size * o.dtype.itemsize for o in outs)
    return pl.pallas_call(
        body,
        out_shape=outs,
        in_specs=ins,
        out_specs=[VMEM] * len(outs),
        scratch_shapes=list(scratch),
        cost_estimate=pl.CostEstimate(flops=flops, bytes_accessed=moved, transcendentals=0),
        compiler_params=pltpu.CompilerParams(vmem_limit_bytes=limit),
    )(*operands)


def half_of(ref, side, half, i, step):
    return ref[:, pl.ds(pl.multiple_of(side * half + i * step, step), step)]


def pack_kernel(chunks, step, at, gate, up, down, *outs):
    half = chunks * step
    c = at[1]
    for side, group in ((c, outs[:chunks]), (1 - c, outs[chunks:])):
        for i, out in enumerate(group):
            for m, ref in enumerate((gate, up, down)):
                out[:, m * step : (m + 1) * step] = half_of(ref, side, half, i, step)


def combine_kernel(chunks, at, *refs):
    kept, given, outs = refs[:chunks], refs[chunks : 2 * chunks], refs[2 * chunks :]
    feats = kept[0].shape[0]
    c = at[1]
    for a, b, out in zip(kept, given, outs):
        out[pl.ds(pl.multiple_of(c * feats, feats), feats), :] = a[...]
        out[pl.ds(pl.multiple_of((1 - c) * feats, feats), feats), :] = b[...]


def scale_kernel(experts, at, *refs):
    pieces, out = refs[:-1], refs[-1]
    rows, width = pieces[0].shape[0], out.shape[1]
    lane = lax.broadcasted_iota(jnp.int32, (rows, LANES), 1)
    ours = (lax.rem(lane, experts) == at[2]) & (lane < 3 * experts)
    for p, ref in enumerate(pieces):
        terms = jnp.where(ours, ref[:, width:].astype(F32), 0.0)
        gate = jnp.sum(terms, axis=1, keepdims=True)
        out[p * rows : (p + 1) * rows, :] = (gate * ref[:, :width].astype(F32)).astype(BF16)


def chunk_kernel(line, n_pieces, at, *refs):
    pieces, refs = refs[:n_pieces], refs[n_pieces:]
    scaled, own = refs[0], refs[1]
    ups, downs = refs[2 : 1 + line], refs[1 + line : 2 * line]
    outs = refs[2 * line : 2 * line + line + 2]
    parts, merged, both = outs[:line], outs[line], outs[line + 1]
    x, g, w, hid, xsem, gsem, wsem = refs[2 * line + line + 2 :]
    z = at[0]
    depth, step = own.shape[0], own.shape[1] // 3
    rows = x.shape[0] // n_pieces
    block = x.shape[0] // 4

    def shard(k):
        f = lax.rem(z - k + line, line)
        return w.at[pl.ds(pl.multiple_of(f * depth, depth), depth), :]

    pltpu.make_async_copy(own, shard(0), wsem.at[0]).start()
    for k in range(1, line):

        @pl.when(z >= k)
        def _(k=k):
            pltpu.make_async_copy(ups[k - 1], shard(k), wsem.at[k]).start()

        @pl.when(z < k)
        def _(k=k):
            pltpu.make_async_copy(downs[line - k - 1], shard(k), wsem.at[k]).start()

    x_copies = [
        pltpu.make_async_copy(ref, x.at[pl.ds(p * rows, rows), :], xsem.at[p])
        for p, ref in enumerate(pieces)
    ]
    g_copies = [
        pltpu.make_async_copy(
            scaled.at[pl.ds(r * block, block), :], g.at[pl.ds(r * block, block), :], gsem.at[r]
        )
        for r in range(4)
    ]
    for r in range(4):
        for p in range(r * n_pieces // 4, (r + 1) * n_pieces // 4):
            x_copies[p].start()
        g_copies[r].start()
    for k in range(line):
        pltpu.make_async_copy(own, shard(k), wsem.at[k]).wait()

    for r in range(4):
        for p in range(r * n_pieces // 4, (r + 1) * n_pieces // 4):
            x_copies[p].wait()
        g_copies[r].wait()
        here = slice(r * block, (r + 1) * block)
        pre = dot(x[here, :], w[:, : 2 * step])
        back = dot(g[here, :], w[:, 2 * step :])
        h, a, b = swish_backward(pre[:, :step], pre[:, step:], back)
        hid[here, :] = h
        merged[here, :step] = a
        merged[here, step:] = b

    for k in range(line):
        f = lax.rem(z - k + line, line)
        cols = pl.ds(pl.multiple_of(f * depth, depth), depth)
        parts[k][:, : 2 * step] = dot_tn(x[:, cols], merged[...]).astype(BF16)
        parts[k][:, 2 * step :] = dot_tn(g[:, cols], hid[...]).astype(BF16)
    both[...] = w[:, : 2 * step]


def route_kernel(chunks, *refs):
    merged, both = refs[:chunks], refs[chunks : 2 * chunks]
    keep, give = refs[2 * chunks :]
    rows, width = keep.shape
    tile = width // 8

    for out, first in ((give, rows), (keep, 0)):

        @pl.loop(0, 8)
        def _(t, out=out, first=first):
            cols = pl.ds(pl.multiple_of(t * tile, tile), tile)
            total = None
            for m, b in zip(merged, both):
                part = dot_nt(m[first : first + rows, :], b[cols, :])
                total = part if total is None else total + part
            out[:, cols] = total.astype(BF16)


def dense_plan(tokens, out_grad, routes, gate_prob, w_gate, w_up, w_down):
    experts = lax.axis_size("expert")
    wide = lax.axis_size("wide")
    line = wide // 2
    rows, width = tokens.shape
    feats = w_gate.shape[1]
    half = w_gate.shape[2] // 2
    step = LANES
    chunks = half // step
    mine = lax.axis_index("expert")
    place = lax.axis_index("wide")
    z, c = place // 2, place % 2
    at = jnp.stack((z, c, mine)).astype(jnp.int32)
    shape = jax.ShapeDtypeStruct

    def after(a, *b):
        return lax.optimization_barrier((a, *b))[0]

    def twin(a):
        return lax.ppermute(a, "wide", [(i, i ^ 1) for i in range(wide)])

    def along(a, hops):
        return lax.ppermute(
            a, "wide", [(2 * s + i, 2 * t + i) for s, t in hops for i in range(2)]
        )

    def flip(a, bit):
        return lax.ppermute(a, "expert", [(e, e ^ bit) for e in range(experts)])

    cut = [shape((feats, 3 * step), BF16)] * (2 * chunks)
    packed = call(
        lambda *r: pack_kernel(chunks, step, *r),
        [SMEM] + [VMEM] * 3,
        cut,
        (at, w_gate[0], w_up[0], w_down[0]),
    )
    given = [twin(a) for a in packed[chunks:]]
    shards = call(
        lambda *r: combine_kernel(chunks, *r),
        [SMEM] + [VMEM] * (2 * chunks),
        [shape((2 * feats, 3 * step), BF16)] * chunks,
        (at, *packed[:chunks], *given),
    )

    named = jnp.arange(experts, dtype=jnp.int32)[None, :]
    gates = sum(
        jnp.where(routes[:, k : k + 1] == named, gate_prob[:, k : k + 1], 0.0)
        for k in range(routes.shape[1])
    )
    high = lax.reduce_precision(gates, 8, 7)
    middle = lax.reduce_precision(gates - high, 8, 7)
    terms = jnp.concatenate((high, middle, gates - high - middle), axis=1).astype(BF16)
    terms = jnp.pad(terms, ((0, 0), (0, LANES - terms.shape[1])))
    graded = jnp.concatenate((out_grad, terms), axis=1)

    with jax.named_scope("rows"):
        t = [tokens, *(after(flip(tokens, bit), *shards) for bit in (1, 2))]
        graded = after(graded, *shards)
        g = [graded, flip(graded, 1), flip(graded, 2)]
        t.append(flip(t[1], 2))
        g.append(flip(g[2], 1))
        t += [twin(a) for a in t]
        g += [twin(a) for a in g]
    count = len(t) * rows
    [scaled] = call(
        lambda *r: scale_kernel(experts, *r),
        [SMEM] + [VMEM] * len(g),
        [shape((count, width), BF16)],
        (at, *g),
    )

    def gather(own, before):
        ups, downs = [own], [own]
        for s in range(1, line):
            up, down = ups[-1], downs[-1]
            if s == line - 1:
                up, down = after(up, *before), after(down, *before)
            with jax.named_scope(f"gather_step_{s}"):
                ups.append(along(up, [(i, i + 1) for i in range(s - 1, line - 1)]))
                downs.append(along(down, [(i, i - 1) for i in range(1, line - s + 1)]))
        return (own, *ups[1:], *downs[1:])

    def begin(parts):
        with jax.named_scope("scatter_step_1"):
            a = jnp.where(z == 0, parts[1], parts[line - 1])
            first = along(a, [(0, 1), (line - 1, line - 2)])
        return first, first

    def hop(parts, state, s, waits):
        up, down = state
        if s == 2 and line == 4:
            a = b = add(parts[2], up)
        elif s == 2:
            a = add(parts[2], jnp.where(z == 1, up, 0))
            b = add(parts[line - 2], jnp.where(z == line - 2, down, 0))
        else:
            a, b = add(parts[s], up), add(parts[line - s], down)
        a, b = after(a, *waits), after(b, *waits)
        with jax.named_scope(f"scatter_step_{s}"):
            up = along(a, [(i, i + 1) for i in range(s)])
            down = along(b, [(i, i - 1) for i in range(line - s, line)])
        return up, down

    merged, both, parts, states, tie, before = [], [], [], [], (), (t[experts - 1], g[experts - 1])
    for i in range(chunks):
        loaded = gather(shards[i], before)
        if i == 0:
            before = (loaded[line - 1], loaded[2 * line - 2])
        got = call(
            lambda *r: chunk_kernel(line, len(t), *r),
            [SMEM] + [ANY] * (len(t) + 2 * line),
            [shape((2 * feats, 3 * step), BF16)] * line
            + [shape((count, 2 * step), BF16), shape((width, 2 * step), BF16)],
            (at, *t, after(scaled, *tie), *loaded),
            (
                pltpu.VMEM((count, width), BF16),
                pltpu.VMEM((count, width), BF16),
                pltpu.VMEM((width, 3 * step), BF16),
                pltpu.VMEM((count, step), BF16),
                pltpu.SemaphoreType.DMA((len(t),)),
                pltpu.SemaphoreType.DMA((4,)),
                pltpu.SemaphoreType.DMA((line,)),
            ),
            flops=12 * count * width * step,
        )
        merged.append(got[line])
        both.append(got[line + 1])
        parts.append(got[:line])
        states.append(begin(got[:line]))
        if i == 0:
            before += (merged[0],)
            tie = states[0]
        else:
            tie = states[i - 1]
            states[i - 1] = hop(parts[i - 1], tie, 2, ())

    block = experts * rows
    merged[-1] = after(merged[-1], *states[-2])
    keep, give = call(
        lambda *r: route_kernel(chunks, *r),
        [VMEM] * (2 * chunks),
        [shape((block, width), BF16)] * 2,
        (*merged, *both),
        flops=4 * count * width * step * chunks,
    )
    with jax.named_scope("back"):
        other = twin(after(give, *states[-1]))
        ret = keep.astype(F32) + other.astype(F32)
        ret = ret.reshape(experts, rows, width)
        left, right = ret[:, :, : width // 2], ret[:, :, width // 2 :]
        far = flip(left[2:].astype(BF16), 2)
        odd = flip(jnp.stack((right[1], right[3])).astype(BF16), 1)
        for s in range(3, line):
            states[0] = hop(parts[0], states[0], s, ())
        left = left[:2] + far.astype(F32)
        near = flip(after(left[1].astype(BF16), *states[0]), 1)
        last = flip(after((right[2] + odd[1].astype(F32)).astype(BF16), *states[0]), 2)
        left = left[0] + near.astype(F32)
        right = right[0] + odd[0].astype(F32) + last.astype(F32)
        grad_input = jnp.concatenate((left, right), axis=1).astype(BF16)
    states[-1] = hop(parts[-1], states[-1], 2, (other,))
    sums = []
    for i, (own, (up, down)) in enumerate(zip(parts, states)):
        for s in range(3 if i else line, line):
            up, down = hop(own, (up, down), s, (odd, far))
        sums.append(own[0].astype(F32) + up.astype(F32) + down.astype(F32))

    own = [lax.dynamic_slice_in_dim(s, c * feats, feats, 0) for s in sums]
    other = [twin(lax.dynamic_slice_in_dim(s, (1 - c) * feats, feats, 0)) for s in sums]

    def grad_of(j):
        cols = slice(j * step, (j + 1) * step)
        a = jnp.concatenate([s[:, cols] for s in own], axis=1)
        b = jnp.concatenate([s[:, cols] for s in other], axis=1)
        first = jnp.concatenate((a, b), axis=1)
        return jnp.where(c == 0, first, jnp.concatenate((b, a), axis=1))[None]

    return (grad_input, grad_of(0), grad_of(1), grad_of(2))


def solution(mesh):
    experts, wide = mesh.shape["expert"], mesh.shape["wide"]
    split = P(("expert", "wide"), None)
    weight = P("expert", "wide", None)

    def on_device(tokens, out_grad, routes, *rest):
        dense = experts == 4 and wide % 2 == 0 and wide > 4 and 2 * routes.shape[1] >= experts
        dense = dense and rest[1].shape[2] % (2 * LANES) == 0
        return (dense_plan if dense else slot_plan)(tokens, out_grad, routes, *rest)

    return jax.shard_map(
        on_device,
        mesh=mesh,
        in_specs=(split,) * 4 + (weight,) * 3,
        out_specs=(split, weight, weight, weight),
        check_vma=False,
    )
```
